32 devices in a mesh: lat: 8 (over y, x, core), lon: 4 (over z).
Axes of the slice: x: 2, y: 2, z: 4, core: 2. Of those that a mesh axis runs over, the one named last changes fastest.
Arguments:
- fields: bfloat16 [384, 512, 128], P('lat', 'lon'), may hold values from -6 to 6
- wet_mask: int32 [384, 512], P('lat', 'lon'), may hold values 0 or 1
- conv_kernel: float32 [2, 49, 128], replicated, may hold values from -0.875 to 0.875
- conv_bias: float32 [2, 128], replicated, may hold values from -3 to 3
- norm_gain: float32 [2, 128], replicated, may hold values from 0.5 to 1.5
- norm_bias: float32 [2, 128], replicated, may hold values from -2 to 2
- in_weight: bfloat16 [2, 128, 512], replicated, may hold values from -0.5 to 0.5
- in_bias: float32 [2, 512], replicated, may hold values from -3 to 3
- out_weight: bfloat16 [2, 512, 128], replicated, may hold values from -0.25 to 0.25
- out_bias: float32 [2, 128], replicated, may hold values from -2 to 2
- layer_scale: float32 [2, 128], replicated, may hold values from 0.5 to 1.5
Outputs:
- result: bfloat16 [384, 512, 128], P('lat', 'lon')
The draws below stay inside these ranges and needn't reach their ends.
Inputs may be any that keep to these rules, and one draw needn't show every extreme that they name: wet_mask holds only 0 and 1.
All inputs are finite; a program needn't handle non-finite values. No bound on the sum of `wet_mask` on one device may be relied on, other than what follows from the above.
Results may differ from the reference program's by a relative error of at most 0.0057.
Values may be sent and summed in bfloat16 or wider, within the bound.
No kernel may reach another device: no remote copies, remote signals or barrier semaphores. Data moves between devices by JAX's collectives and lax.ppermute only.
A program may use at most 64 MiB of HBM per device.

```python
import jax
import jax.numpy as jnp
from jax import lax

C = 128
HID = 512
RD = 48
H = 384
W = 512


def with_ends(drawn, stream_key, smallest, high):
    longest = drawn.shape.index(max(drawn.shape))
    spots = []
    for shift in (0, 1):
        where = [jax.random.randint(jax.random.fold_in(stream_key, axis), (), 0, length) for axis, length in enumerate(drawn.shape)]
        where[longest] = (where[longest] + shift) % drawn.shape[longest]
        spots.append(tuple(where))
    return drawn.at[spots[0]].set(smallest).at[spots[1]].set(high)


def block_levels(own_key, dims, shards, smallest, top_value):
    def one(axis_at, parts):
        heights = jax.random.uniform(jax.random.fold_in(jax.random.fold_in(own_key, 6), axis_at), (parts,), jnp.float32, smallest / len(shards), top_value / len(shards))
        return jnp.repeat(jnp.exp(heights), dims[axis_at] // parts).reshape((-1,) + (1,) * (len(dims) - axis_at - 1))

    level = one(*shards[0])
    for cut in shards[1:]:
        level = level * one(*cut)
    return level


def bell_draw(rng, extent, spread, bound, split=(), held_as=jnp.bfloat16):
    loudness = block_levels(rng, extent, split, -0.22, 0.18) if split else 1.0
    array = jax.random.normal(rng, extent, jnp.float32) * spread * loudness
    return jnp.minimum(jnp.maximum(array, -bound), bound).astype(held_as)


def setup_inputs(seed: int = 0) -> dict:
    key_list = jax.random.split(jax.random.key(seed), 12)
    return {
        "fields": bell_draw(key_list[0], (H, W, C), 1.0, 6.0, ((0, 8), (1, 4))),
        "wet_mask": with_ends((jax.random.randint(key_list[1], (H, W), 0, 4) < 3).astype(jnp.int32), jax.random.fold_in(key_list[1], 1), 0, 1),
        "conv_kernel": bell_draw(key_list[2], (2, 49, C), 49 ** -0.5, 0.875, (), jnp.float32),
        "conv_bias": bell_draw(key_list[3], (2, C), 0.5, 3.0, (), jnp.float32),
        "norm_gain": jnp.clip(1.0 + 0.1 * jax.random.normal(key_list[4], (2, C), jnp.float32), 0.5, 1.5),
        "norm_bias": bell_draw(key_list[5], (2, C), 0.3, 2.0, (), jnp.float32),
        "in_weight": bell_draw(key_list[6], (2, C, HID), C ** -0.5, 0.5),
        "in_bias": bell_draw(key_list[7], (2, HID), 0.5, 3.0, (), jnp.float32),
        "out_weight": bell_draw(key_list[8], (2, HID, C), HID ** -0.5, 0.25),
        "out_bias": bell_draw(key_list[9], (2, C), 0.3, 2.0, (), jnp.float32),
        "layer_scale": jnp.clip(1.0 + 0.1 * jax.random.normal(key_list[10], (2, C), jnp.float32), 0.5, 1.5),
    }


def pad_grid(values):
    ext = jnp.concatenate([values[:, -3:], values, values[:, :3]], axis=1)
    south = jnp.zeros((3,) + ext.shape[1:], ext.dtype)
    north = ext[-3:][::-1, ::-1]
    return jnp.concatenate([south, ext, north], axis=0)

def block_rows(band, residual, index, conv_kernel, conv_bias, norm_gain, norm_bias, in_weight, in_bias, out_weight, out_bias, layer_scale):
    rows = residual.shape[0]
    cols = residual.shape[1]
    acc = jnp.zeros((rows, cols, band.shape[2]), jnp.float32)
    for row_tap in range(7):
        for col_tap in range(7):
            acc = acc + band[row_tap:row_tap + rows, col_tap:col_tap + cols].astype(jnp.float32) * conv_kernel[index, 7 * row_tap + col_tap]
    acc = acc + conv_bias[index]
    mean = lax.optimization_barrier(jnp.mean(acc, axis=-1, keepdims=True))
    var = lax.optimization_barrier(jnp.mean((acc - mean) ** 2, axis=-1, keepdims=True))
    normed = ((acc - mean) * lax.rsqrt(var + 1e-06) * norm_gain[index] + norm_bias[index]).astype(jnp.bfloat16)
    flat = normed.reshape(rows * cols, -1)
    hidden = jnp.dot(flat, in_weight[index], preferred_element_type=jnp.float32) + in_bias[index]
    hidden = jax.nn.gelu(hidden, approximate=False).astype(jnp.bfloat16)
    branch = jnp.dot(hidden, out_weight[index], preferred_element_type=jnp.float32) + out_bias[index]
    branch = branch * layer_scale[index]
    return (residual.astype(jnp.float32) + branch.reshape(rows, cols, -1)).astype(jnp.bfloat16)

def reference(fields, wet_mask, conv_kernel, conv_bias, norm_gain, norm_bias, in_weight, in_bias, out_weight, out_bias, layer_scale):
    mask_bf = wet_mask.astype(jnp.bfloat16)
    state = fields * mask_bf[:, :, None]
    bands = H // RD
    for index in range(2):
        padded = pad_grid(state)

        def one_band(band_index):
            start = (band_index * RD).astype(jnp.int32)
            band = lax.dynamic_slice_in_dim(padded, start, RD + 6, 0)
            residual = lax.dynamic_slice_in_dim(state, start, RD, 0)
            return block_rows(band, residual, index, conv_kernel, conv_bias, norm_gain, norm_bias, in_weight, in_bias, out_weight, out_bias, layer_scale)
        state = lax.map(one_band, jnp.arange(bands, dtype=jnp.int32)).reshape(H, W, -1)
    return state * mask_bf[:, :, None]
```

```python
import functools

import jax
import jax.numpy as jnp
import numpy as np
from jax import lax
from jax.experimental import pallas as pl
from jax.experimental.pallas import tpu as pltpu
from jax.sharding import PartitionSpec as P

BF = jnp.bfloat16
F32 = jnp.float32
TAPS = 7
HALO = 3
VMEM_LIMIT = 56 * 1024 * 1024


def partners(nlat, nlon, parity):
    route = []
    for lat in range(nlat):
        for lon in range(nlon):
            here = lat * nlon + lon
            if lat % 2 == parity:
                there = here + nlon if lat + 1 < nlat else lat * nlon + nlon - 1 - lon
            elif lat > 0:
                there = here - nlon
            else:
                continue
            route.append((here, there))
    return route


def exchange(state):
    nlat, nlon = lax.axis_size("lat"), lax.axis_size("lon")
    lat = lax.axis_index("lat")
    rows, cols = state.shape[0], state.shape[1]
    up = [(i, (i + 1) % nlon) for i in range(nlon)]
    down = [(j, i) for i, j in up]
    left = lax.ppermute(state[:, cols - HALO :], "lon", up)
    right = lax.ppermute(state[:, :HALO], "lon", down)
    first = jnp.concatenate([left[:HALO], state[:HALO], right[:HALO]], axis=1)
    last = jnp.concatenate([left[rows - HALO :], state[rows - HALO :], right[rows - HALO :]], axis=1)
    even = lat % 2 == 0
    got_a = lax.ppermute(jnp.where(even, last, first), ("lat", "lon"), partners(nlat, nlon, 0))
    got_b = lax.ppermute(jnp.where(even, first, last), ("lat", "lon"), partners(nlat, nlon, 1))
    north = jnp.where(even, got_a, got_b)
    south = jnp.where(even, got_b, got_a)
    north = jnp.where(lat == nlat - 1, north[::-1, ::-1], north)
    return left, right, south, north


def taps_kernel(k_ref, w_ref):
    ch = k_ref.shape[2]
    diag = lax.broadcasted_iota(jnp.int32, (ch, ch), 0) == lax.broadcasted_iota(jnp.int32, (ch, ch), 1)
    zero = jnp.zeros((ch, ch), BF)
    for s in range(TAPS):
        for a in range(TAPS + 1):
            for o in range(2):
                r = a - o
                if 0 <= r < TAPS:
                    tile = jnp.where(diag, k_ref[0, pl.ds(TAPS * r + s, 1), :], 0.0).astype(BF)
                else:
                    tile = zero
                w_ref[0, pl.ds((s * (TAPS + 1) + a) * ch, ch), o * ch : (o + 1) * ch] = tile


def tap_matrices(conv_kernel):
    blocks, _, ch = conv_kernel.shape
    depth = TAPS * (TAPS + 1) * ch
    return pl.pallas_call(
        taps_kernel,
        grid=(blocks,),
        in_specs=[pl.BlockSpec((1, TAPS * TAPS, ch), lambda b: (b, 0, 0))],
        out_specs=pl.BlockSpec((1, depth, 2 * ch), lambda b: (b, 0, 0)),
        out_shape=jax.ShapeDtypeStruct((blocks, depth, 2 * ch), BF),
        compiler_params=pltpu.CompilerParams(vmem_limit_bytes=VMEM_LIMIT),
        cost_estimate=pl.CostEstimate(flops=0, bytes_accessed=2 * blocks * depth * 2 * ch, transcendentals=0),
        name="tap_matrices",
    )(conv_kernel)


def block_kernel(
    pairs,
    last,
    x_ref,
    left_ref,
    right_ref,
    south_ref,
    north_ref,
    mask_ref,
    w_ref,
    vec_ref,
    inw_ref,
    inb_ref,
    outw_ref,
    out_ref,
    pad_ref,
    shifted_ref,
):
    rows, cols, ch = x_ref.shape
    base = 8
    lead = base - HALO
    wide = cols + 2 * HALO
    pad_ref[0:HALO, lead : lead + wide, :] = south_ref[...].astype(F32)
    pad_ref[rows + HALO : rows + 2 * HALO, lead : lead + wide, :] = north_ref[...].astype(F32)

    def fill(i, carry):
        pad_ref[i + HALO, lead:base, :] = left_ref[i].astype(F32)
        pad_ref[i + HALO, base : base + cols, :] = x_ref[i].astype(F32)
        pad_ref[i + HALO, base + cols : base + cols + HALO, :] = right_ref[i].astype(F32)
        return carry

    lax.fori_loop(0, rows, fill, 0)

    def shift(q, carry):
        for s in range(TAPS):
            for h in range(2):
                shifted_ref[s, q, :, h * ch : (h + 1) * ch] = pad_ref[2 * q + h, lead + s : lead + s + cols, :].astype(BF)
        return carry

    lax.fori_loop(0, (rows + 2 * HALO) // 2, shift, 0)

    conv_bias, gain, nbias, outb, scale = (vec_ref[i : i + 1, :] for i in range(5))
    inb = inb_ref[...]
    if last:
        diag = lax.broadcasted_iota(jnp.int32, (cols, cols), 0) == lax.broadcasted_iota(jnp.int32, (cols, cols), 1)

    def chunk(t, carry):
        p = t * pairs
        cells = pairs * cols
        parts = []
        for s in range(TAPS):
            for a in range((TAPS + 1) // 2):
                parts.append(shifted_ref[s, pl.ds(p + a, pairs)].reshape(cells, 2 * ch))
        acc = jnp.dot(jnp.concatenate(parts, axis=1), w_ref[...], preferred_element_type=F32)
        for h in range(2):
            conv = acc[:, h * ch : (h + 1) * ch] + conv_bias
            mean = jnp.mean(conv, axis=-1, keepdims=True)
            cen = conv - mean
            var = jnp.mean(cen * cen, axis=-1, keepdims=True)
            normed = (cen * lax.rsqrt(var + 1e-6) * gain + nbias).astype(BF)
            hid = jnp.dot(normed, inw_ref[...], preferred_element_type=F32) + inb
            hid = (0.5 * hid * (1.0 + lax.erf(hid * np.float32(np.sqrt(0.5))))).astype(BF)
            branch = (jnp.dot(hid, outw_ref[...], preferred_element_type=F32) + outb) * scale
            for j in range(pairs):
                row = 2 * (p + j) + h
                new = (x_ref[row].astype(F32) + branch[j * cols : (j + 1) * cols]).astype(BF)
                if last:
                    keep = jnp.where(diag, mask_ref[pl.ds(row, 1), :], 0.0).astype(BF)
                    new = jnp.dot(keep, new, preferred_element_type=F32).astype(BF)
                out_ref[row] = new
        return carry

    lax.fori_loop(0, rows // (2 * pairs), chunk, 0)


def run_block(state, halos, mask, w, vec, inw, inb, outw, last):
    rows, cols, ch = state.shape
    hid = inw.shape[1]
    half = rows // 2
    pairs = max(d for d in (1, 2, 4) if half % d == 0)
    spec = pl.BlockSpec(memory_space=pltpu.VMEM)
    cells = rows * cols
    return pl.pallas_call(
        functools.partial(block_kernel, pairs, last),
        in_specs=[spec] * 11,
        out_specs=spec,
        out_shape=jax.ShapeDtypeStruct(state.shape, BF),
        scratch_shapes=[
            pltpu.VMEM((rows + 2 * HALO, cols + 16, ch), F32),
            pltpu.VMEM((TAPS, (rows + 2 * HALO) // 2, cols, 2 * ch), BF),
        ],
        compiler_params=pltpu.CompilerParams(vmem_limit_bytes=VMEM_LIMIT),
        cost_estimate=pl.CostEstimate(
            flops=cells * (4 * ch * hid + 2 * ch * w.shape[0]), bytes_accessed=4 * cells * ch, transcendentals=cells * hid
        ),
        name="block",
    )(state, *halos, mask, w, vec, inw, inb, outw)


def shards(
    fields,
    wet_mask,
    conv_kernel,
    conv_bias,
    norm_gain,
    norm_bias,
    in_weight,
    in_bias,
    out_weight,
    out_bias,
    layer_scale,
):
    state = fields * wet_mask.astype(BF)[:, :, None]
    mask = wet_mask.astype(F32)
    w = tap_matrices(conv_kernel)
    vec = jnp.stack([conv_bias, norm_gain, norm_bias, out_bias, layer_scale], axis=1)
    blocks = conv_kernel.shape[0]
    for b in range(blocks):
        halos = exchange(state)
        state = run_block(
            state, halos, mask, w[b], vec[b], in_weight[b], in_bias[b][None], out_weight[b], b == blocks - 1
        )
    return state


def solution(mesh):
    return jax.shard_map(
        shards,
        mesh=mesh,
        in_specs=(P("lat", "lon", None), P("lat", "lon")) + (P(),) * 9,
        out_specs=P("lat", "lon", None),
        check_vma=False,
    )
```

```python
import functools

import jax
import jax.numpy as jnp
from jax import lax
from jax.experimental import pallas as pl
from jax.experimental.pallas import tpu as pltpu
from jax.sharding import PartitionSpec as P

BF = jnp.bfloat16
F32 = jnp.float32
TAPS = 7
HALO = 3
REACH = 2 * HALO
OUTS = 8
VMEM_LIMIT = 62 * 1024 * 1024
ERF_POLY = (0.7978323547267507, 0.036463673384825215, -0.0001230322006747663, -3.081922192956723e-05, 1.128904780388478e-06)


def partners(nlat, nlon, parity):
    route = []
    for lat in range(nlat):
        for lon in range(nlon):
            here = lat * nlon + lon
            if lat % 2 == parity:
                there = here + nlon if lat + 1 < nlat else lat * nlon + nlon - 1 - lon
            elif lat > 0:
                there = here - nlon
            else:
                continue
            route.append((here, there))
    return route


def exchange(fields, wet_mask):
    nlat, nlon = lax.axis_size("lat"), lax.axis_size("lon")
    lat = lax.axis_index("lat")
    rows, cols = wet_mask.shape

    def edge(r0, r1, c0, c1):
        return fields[r0:r1, c0:c1] * wet_mask[r0:r1, c0:c1].astype(BF)[:, :, None]

    up = [(i, (i + 1) % nlon) for i in range(nlon)]
    down = [(j, i) for i, j in up]
    left = lax.ppermute(edge(0, rows, cols - REACH, cols), "lon", up)
    right = lax.ppermute(edge(0, rows, 0, REACH), "lon", down)
    first = jnp.concatenate([left[:REACH], edge(0, REACH, 0, cols), right[:REACH]], axis=1)
    last = jnp.concatenate([left[rows - REACH :], edge(rows - REACH, rows, 0, cols), right[rows - REACH :]], axis=1)
    even = lat % 2 == 0
    got_a = lax.ppermute(jnp.where(even, last, first), ("lat", "lon"), partners(nlat, nlon, 0))
    got_b = lax.ppermute(jnp.where(even, first, last), ("lat", "lon"), partners(nlat, nlon, 1))
    flags = jnp.stack([even, lat == nlat - 1, lat == 0]).astype(jnp.int32)
    return left, right, got_a, got_b, flags


def tap_vectors(conv_kernel):
    blocks, _, ch = conv_kernel.shape
    width = 2 * ch // OUTS
    taps = conv_kernel.reshape(blocks, TAPS, TAPS, ch // width, width)
    taps = jnp.pad(taps, ((0, 0), (OUTS - 1, 2 * OUTS - TAPS), (0, 0), (0, 0), (0, 0)))
    by_out = [taps[:, OUTS - 1 - o : 3 * OUTS - 1 - o] for o in range(OUTS)]
    stacked = jnp.stack(by_out, axis=4)
    return stacked.transpose(0, 3, 2, 1, 4, 5).reshape(blocks, ch // width * TAPS, 2 * OUTS, OUTS * width)


def regroup(parts, width):
    parts = list(parts)
    ch = parts[0].shape[-1]
    block = lax.broadcasted_iota(jnp.int32, parts[0].shape, parts[0].ndim - 1) // width
    step = 1
    while step < len(parts):
        low = (block & step) == 0
        for i in range(len(parts)):
            if not i & step:
                x, y = parts[i], parts[i + step]
                parts[i] = jnp.where(low, x, pltpu.roll(y, step * width, x.ndim - 1))
                parts[i + step] = jnp.where(low, pltpu.roll(x, ch - step * width, x.ndim - 1), y)
        step *= 2
    return parts


def both_blocks(
    flags_ref,
    x_ref,
    mask_ref,
    left_ref,
    right_ref,
    a_ref,
    b_ref,
    k_ref,
    kv_ref,
    vec_ref,
    inw_ref,
    inb_ref,
    outw_ref,
    out_ref,
    x0_ref,
    x1_ref,
    shifted_ref,
    group_ref,
    w_ref,
    acc_ref,
    strip_ref,
    flip_ref,
):
    rows, cols, ch = x_ref.shape
    width = 2 * ch // OUTS
    groups = ch // width
    octets = rows // OUTS
    quads = 2 * octets + 2
    wide0 = x1_ref.shape[1]
    base = 8
    ext = cols + 2 * REACH
    lead = base - REACH
    total = x0_ref.shape[1]
    even, top, bottom = (flags_ref[i] == 1 for i in range(3))

    def fill(i, carry):
        x0_ref[i + REACH, 0:base, :] = jnp.zeros((base, ch), F32)
        x0_ref[i + REACH, lead:base, :] = left_ref[i].astype(F32)
        x0_ref[i + REACH, base : base + cols, :] = x_ref[i].astype(F32)
        x0_ref[i + REACH, base + cols : total, :] = jnp.zeros((total - base - cols, ch), F32)
        x0_ref[i + REACH, base + cols : base + cols + REACH, :] = right_ref[i].astype(F32)
        return carry

    lax.fori_loop(0, rows, fill, 0)
    flip_ref[...] = jnp.zeros(flip_ref.shape, F32)
    at = lax.broadcasted_iota(jnp.int32, (wide0, wide0), 0)
    to = lax.broadcasted_iota(jnp.int32, (wide0, wide0), 1)
    mirror = jnp.where(to == jnp.where(top, ext - 1 - at, at), 1.0, 0.0).astype(BF)
    for i in range(REACH):
        x0_ref[i, :, :] = jnp.zeros((total, ch), F32)
        x0_ref[i, lead : lead + ext, :] = jnp.where(even, b_ref[i].astype(F32), a_ref[i].astype(F32))
        src = jnp.where(top, REACH - 1 - i, i)
        flip_ref[0:ext, :] = jnp.where(even, a_ref[src].astype(F32), b_ref[src].astype(F32))
        turned = jnp.dot(mirror, flip_ref[0:wide0, :].astype(BF), preferred_element_type=F32)
        x0_ref[rows + REACH + i, :, :] = jnp.zeros((total, ch), F32)
        x0_ref[rows + REACH + i, lead : lead + wide0, :] = turned

    own = (lax.broadcasted_iota(jnp.int32, (width, OUTS * width), 1) & (width - 1)) == lax.broadcasted_iota(
        jnp.int32, (width, OUTS * width), 0
    )

    def build(b):
        for s in range(TAPS):
            def one(gr, carry):
                for a in range(2 * OUTS):
                    vec = kv_ref[b, gr * TAPS + s, a : a + 1, :]
                    w_ref[gr, (s * 2 * OUTS + a) * width : (s * 2 * OUTS + a + 1) * width, :] = jnp.where(
                        own, vec, 0.0
                    ).astype(BF)
                return carry

            lax.fori_loop(0, groups, one, 0)

    def shift(src_ref, row0, col0, wide):
        span = wide + 8

        def one(q, carry):
            parts = [src_ref[row0 + 4 * q + j, :, :] for j in range(groups)]
            for j, part in enumerate(regroup(parts, width)):
                group_ref[j, 0 : part.shape[0], :] = part
            for s in range(TAPS):
                for j in range(groups):
                    shifted_ref[s, j, q % 2, q // 2, 0:wide, :] = group_ref[j, col0 + s : col0 + s + wide, :].astype(BF)
            return carry

        lax.fori_loop(0, quads, one, 0)

    def conv(wide):
        def one(gr, carry):
            parts = []
            for s in range(TAPS):
                for a in range(4):
                    part = shifted_ref[s, gr, a % 2, a // 2 : a // 2 + octets, 0:wide, :]
                    parts.append(part.reshape(octets * wide, ch))
            acc_ref[gr, 0 : octets * wide, :] = jnp.dot(
                jnp.concatenate(parts, axis=1), w_ref[gr], preferred_element_type=F32
            )
            return carry

        lax.fori_loop(0, groups, one, 0)

    def mlp(b, conv_rows):
        conv_bias, gain, nbias, outb, scale = (vec_ref[b, i : i + 1, :] for i in range(5))
        val = jnp.concatenate(conv_rows, axis=0) + conv_bias
        mean = jnp.mean(val, axis=-1, keepdims=True)
        cen = val - mean
        var = jnp.mean(cen * cen, axis=-1, keepdims=True)
        normed = (cen * lax.rsqrt(var + 1e-6) * gain + nbias).astype(BF)
        h = jnp.dot(normed, inw_ref[b], preferred_element_type=F32) + inb_ref[b : b + 1, :]
        z = h * h
        p = jnp.full_like(z, ERF_POLY[-1])
        for coef in ERF_POLY[-2::-1]:
            p = p * z + coef
        t = jnp.tanh(h * p)
        twice = (h + h * t).astype(BF)
        branch = jnp.dot(twice, outw_ref[b], preferred_element_type=F32) * (0.5 * scale) + outb * scale
        n = conv_rows[0].shape[0]
        return [branch[i * n : (i + 1) * n] for i in range(len(conv_rows))]

    def inner(b, wide, emit):
        def one(t, carry):
            for half in range(2):
                parts = [
                    acc_ref[gr, pl.ds(pl.multiple_of(t * wide, 16), wide), half * ch : (half + 1) * ch]
                    for gr in range(groups)
                ]
                for j, branch in enumerate(mlp(b, regroup(parts, width))):
                    emit(OUTS * t + half * (OUTS // 2) + j, branch)
            return carry

        lax.fori_loop(0, octets, one, 0)

    build(0)
    shift(x0_ref, REACH - HALO, lead, wide0)
    conv(wide0)

    def keep0(row, branch):
        new = x0_ref[row + REACH, lead + HALO : lead + HALO + wide0, :] + branch
        x1_ref[row + HALO, :, :] = new.astype(BF).astype(F32)

    inner(0, wide0, keep0)
    piece = wide0 // 3
    for side in range(2):
        first = 0 if side == 0 else rows + HALO
        for c in range(0, wide0, piece):
            sums = [jnp.zeros((piece, ch), F32) for _ in range(HALO)]
            for s in range(TAPS):
                lines = [x0_ref[first + i, lead + s + c : lead + s + c + piece, :] for i in range(TAPS + HALO - 1)]
                for r in range(TAPS):
                    tap = TAPS * r + s
                    if side == 1:
                        tap = jnp.where(top, TAPS * TAPS - 1 - tap, tap)
                    weight = k_ref[0, pl.ds(tap, 1), :]
                    for i in range(HALO):
                        sums[i] = sums[i] + lines[i + r] * weight
            for i in range(HALO):
                strip_ref[side * HALO + i, c : c + piece, :] = sums[i]
    for side in range(2):
        branches = mlp(0, [strip_ref[side * HALO + i] for i in range(HALO)])
        for i, branch in enumerate(branches):
            row = i - HALO if side == 0 else rows + i
            new = x0_ref[row + REACH, lead + HALO : lead + HALO + wide0, :] + branch
            new = new.astype(BF).astype(F32)
            if side == 0:
                new = jnp.where(bottom, 0.0, new)
            x1_ref[row + HALO, :, :] = new
    for i in range(rows + 2 * HALO, x1_ref.shape[0]):
        x1_ref[i, :, :] = jnp.zeros((wide0, ch), F32)

    build(1)
    shift(x1_ref, 0, 0, cols)
    conv(cols)

    def keep1(row, branch):
        new = x1_ref[row + HALO, HALO : HALO + cols, :] + branch
        out_ref[row] = new.astype(BF) * mask_ref[row]

    inner(1, cols, keep1)


def shards(
    fields,
    wet_mask,
    conv_kernel,
    conv_bias,
    norm_gain,
    norm_bias,
    in_weight,
    in_bias,
    out_weight,
    out_bias,
    layer_scale,
):
    rows, cols, ch = fields.shape
    left, right, got_a, got_b, flags = exchange(fields, wet_mask)
    mask = jnp.broadcast_to(wet_mask.astype(BF)[:, :, None], fields.shape)
    state = fields * mask
    vec = jnp.stack([conv_bias, norm_gain, norm_bias, out_bias, layer_scale], axis=1)
    vectors = tap_vectors(conv_kernel)
    hid = in_weight.shape[2]
    width = 2 * ch // OUTS
    groups = ch // width
    wide0 = cols + 16
    octets = rows // OUTS
    cells = rows * cols
    vmem = pl.BlockSpec(memory_space=pltpu.VMEM)
    return pl.pallas_call(
        both_blocks,
        in_specs=[pl.BlockSpec(memory_space=pltpu.SMEM)] + [vmem] * 12,
        out_specs=vmem,
        out_shape=jax.ShapeDtypeStruct(fields.shape, BF),
        scratch_shapes=[
            pltpu.VMEM((rows + 2 * REACH, wide0 + 8, ch), F32),
            pltpu.VMEM((rows + 8, wide0, ch), F32),
            pltpu.VMEM((TAPS, groups, 2, octets + 1, wide0, ch), BF),
            pltpu.VMEM((groups, wide0 + 8, ch), F32),
            pltpu.VMEM((groups, TAPS * 2 * OUTS * width, OUTS * width), BF),
            pltpu.VMEM((groups, octets * wide0, OUTS * width), F32),
            pltpu.VMEM((2 * HALO, wide0, ch), F32),
            pltpu.VMEM((wide0 + 8, ch), F32),
        ],
        compiler_params=pltpu.CompilerParams(vmem_limit_bytes=VMEM_LIMIT),
        cost_estimate=pl.CostEstimate(
            flops=4 * cells * (4 * ch * hid + 8 * ch * 2 * ch), bytes_accessed=6 * cells * ch, transcendentals=2 * cells * hid
        ),
        name="both_blocks",
    )(flags, state, mask, left, right, got_a, got_b, conv_kernel, vectors, vec, in_weight, in_bias, out_weight)


def solution(mesh):
    return jax.shard_map(
        shards,
        mesh=mesh,
        in_specs=(P("lat", "lon", None), P("lat", "lon")) + (P(),) * 9,
        out_specs=P("lat", "lon", None),
        check_vma=False,
    )
```

```python
import jax
import jax.numpy as jnp
from jax import lax
from jax.experimental import pallas as pl
from jax.experimental.pallas import tpu as pltpu
from jax.sharding import PartitionSpec as P

BF = jnp.bfloat16
F32 = jnp.float32
TAPS = 7
HALO = 3
REACH = 2 * HALO
OUTS = 8
VMEM_LIMIT = 62 * 1024 * 1024
ERF_POLY = (0.7975078797359708, 0.03700565107996738, -0.0003515176683895368)


def partners(nlat, nlon, parity):
    route = []
    for lat in range(nlat):
        for lon in range(nlon):
            here = lat * nlon + lon
            if lat % 2 == parity:
                there = here + nlon if lat + 1 < nlat else lat * nlon + nlon - 1 - lon
            elif lat > 0:
                there = here - nlon
            else:
                continue
            route.append((here, there))
    return route


def exchange(fields, wet_mask):
    nlat, nlon = lax.axis_size("lat"), lax.axis_size("lon")
    lat = lax.axis_index("lat")
    rows, cols = wet_mask.shape

    def edge(r0, r1, c0, c1):
        return fields[r0:r1, c0:c1] * wet_mask[r0:r1, c0:c1].astype(BF)[:, :, None]

    up = [(i, (i + 1) % nlon) for i in range(nlon)]
    down = [(j, i) for i, j in up]
    left = lax.ppermute(edge(0, rows, cols - REACH, cols), "lon", up)
    right = lax.ppermute(edge(0, rows, 0, REACH), "lon", down)
    first = jnp.concatenate([left[:REACH], edge(0, REACH, 0, cols), right[:REACH]], axis=1)
    last = jnp.concatenate([left[rows - REACH :], edge(rows - REACH, rows, 0, cols), right[rows - REACH :]], axis=1)
    even = lat % 2 == 0
    got_a = lax.ppermute(jnp.where(even, last, first), ("lat", "lon"), partners(nlat, nlon, 0))
    got_b = lax.ppermute(jnp.where(even, first, last), ("lat", "lon"), partners(nlat, nlon, 1))
    return left, right, got_a, got_b


def regroup(parts, width):
    parts = list(parts)
    ch = parts[0].shape[-1]
    block = lax.broadcasted_iota(jnp.int32, parts[0].shape, parts[0].ndim - 1) // width
    step = 1
    while step < len(parts):
        low = (block & step) == 0
        for i in range(len(parts)):
            if not i & step:
                x, y = parts[i], parts[i + step]
                parts[i] = jnp.where(low, x, pltpu.roll(y, step * width, x.ndim - 1))
                parts[i + step] = jnp.where(low, pltpu.roll(x, ch - step * width, x.ndim - 1), y)
        step *= 2
    return parts


def both_blocks(
    x_ref,
    mask_ref,
    left_ref,
    right_ref,
    a_ref,
    b_ref,
    k_ref,
    cbias_ref,
    gain_ref,
    nbias_ref,
    inw_ref,
    inb_ref,
    outw_ref,
    outb_ref,
    scale_ref,
    out_ref,
    x0_ref,
    x1_ref,
    shifted_ref,
    group_ref,
    w_ref,
    acc_ref,
    strip_ref,
    flip_ref,
    kv_ref,
):
    rows, cols, ch = x_ref.shape
    width = 2 * ch // OUTS
    groups = ch // width
    octets = rows // OUTS
    quads = 2 * octets + 2
    wide0 = x1_ref.shape[1]
    base = 8
    ext = cols + 2 * REACH
    lead = base - REACH
    total = x0_ref.shape[1]
    lat = lax.axis_index("lat")
    even, top, bottom = lat % 2 == 0, lat == lax.axis_size("lat") - 1, lat == 0

    def fill(i, carry):
        x0_ref[i + REACH, 0:base, :] = jnp.zeros((base, ch), F32)
        x0_ref[i + REACH, lead:base, :] = left_ref[i].astype(F32)
        x0_ref[i + REACH, base : base + cols, :] = x_ref[i].astype(F32)
        x0_ref[i + REACH, base + cols : total, :] = jnp.zeros((total - base - cols, ch), F32)
        x0_ref[i + REACH, base + cols : base + cols + REACH, :] = right_ref[i].astype(F32)
        return carry

    lax.fori_loop(0, rows, fill, 0)
    flip_ref[...] = jnp.zeros(flip_ref.shape, F32)
    at = lax.broadcasted_iota(jnp.int32, (wide0, wide0), 0)
    to = lax.broadcasted_iota(jnp.int32, (wide0, wide0), 1)
    mirror = jnp.where(to == jnp.where(top, ext - 1 - at, at), 1.0, 0.0).astype(BF)
    for i in range(REACH):
        x0_ref[i, :, :] = jnp.zeros((total, ch), F32)
        x0_ref[i, lead : lead + ext, :] = jnp.where(even, b_ref[i].astype(F32), a_ref[i].astype(F32))
        src = jnp.where(top, REACH - 1 - i, i)
        flip_ref[0:ext, :] = jnp.where(even, a_ref[src].astype(F32), b_ref[src].astype(F32))
        turned = jnp.dot(mirror, flip_ref[0:wide0, :].astype(BF), preferred_element_type=F32)
        x0_ref[rows + REACH + i, :, :] = jnp.zeros((total, ch), F32)
        x0_ref[rows + REACH + i, lead : lead + wide0, :] = turned

    own = (lax.broadcasted_iota(jnp.int32, (width, OUTS * width), 1) & (width - 1)) == lax.broadcasted_iota(
        jnp.int32, (width, OUTS * width), 0
    )

    lanes = OUTS * width
    out_row = lax.broadcasted_iota(jnp.int32, (TAPS, lanes), 1) // width

    def build(b):
        down = [k_ref[b, TAPS * r : TAPS * (r + 1), :] for r in range(TAPS - 1, -1, -1)]
        down.append(jnp.zeros((TAPS, ch), F32))
        halves = [regroup(down[i : i + groups], width) for i in range(0, OUTS, groups)]
        for gr in range(groups):
            line = jnp.concatenate([half[gr] for half in halves], axis=1)
            for a in range(2 * OUTS):
                turned = pltpu.roll(line, (a - TAPS + 1) * width % lanes, 1)
                seen = (out_row <= a) & (out_row >= a - TAPS + 1)
                kv_ref[gr, a, 0:TAPS, :] = jnp.where(seen, turned, 0.0)

        def one(i, carry):
            gr, s = i // TAPS, i % TAPS
            for a in range(2 * OUTS):
                vec = kv_ref[gr, a, pl.ds(s, 1), :]
                at = pl.multiple_of(s * (2 * OUTS * width), 2 * OUTS * width) + a * width
                w_ref[gr, pl.ds(at, width), :] = jnp.where(own, vec, 0.0).astype(BF)
            return carry

        lax.fori_loop(0, groups * TAPS, one, 0)

    def shift(src_ref, row0, col0, wide):
        def one(q, carry):
            parts = [src_ref[row0 + 4 * q + j, :, :] for j in range(groups)]
            for j, part in enumerate(regroup(parts, width)):
                group_ref[j, 0 : part.shape[0], :] = part

            def column(s, inside):
                for j in range(groups):
                    shifted_ref[s, j, q % 2, q // 2, 0:wide, :] = group_ref[j, pl.ds(col0 + s, wide), :].astype(BF)
                return inside

            return lax.fori_loop(0, TAPS, column, carry)

        lax.fori_loop(0, quads, one, 0)

    def conv(wide):
        def one(gr, carry):
            parts = []
            for s in range(TAPS):
                for a in range(4):
                    part = shifted_ref[s, gr, a % 2, a // 2 : a // 2 + octets, 0:wide, :]
                    parts.append(part.reshape(octets * wide, ch))
            acc_ref[gr, 0 : octets * wide, :] = jnp.dot(
                jnp.concatenate(parts, axis=1), w_ref[gr], preferred_element_type=F32
            )
            return carry

        lax.fori_loop(0, groups, one, 0)

    def gelu_twice(h):
        z = h * h
        p = jnp.full_like(z, ERF_POLY[-1])
        for coef in ERF_POLY[-2::-1]:
            p = p * z + jnp.asarray(coef, z.dtype)
        return h + h * jnp.tanh(h * p)

    def norm(b, val):
        val = val + cbias_ref[b : b + 1, :]
        cen = val - jnp.mean(val, axis=-1, keepdims=True)
        var = jnp.mean(cen * cen, axis=-1, keepdims=True)
        return (cen * lax.rsqrt(var + 1e-6) * gain_ref[b : b + 1, :] + nbias_ref[b : b + 1, :]).astype(BF)

    def mlp(b, conv_rows):
        n = conv_rows[0].shape[0]
        normed = jnp.concatenate([norm(b, row) for row in conv_rows], axis=0)
        tile = n // 3 if n % 48 == 0 else n // 2
        branch = None
        half_hid = inw_ref.shape[2] // 2
        for c in range(0, 2 * half_hid, half_hid):
            hid = jnp.dot(normed, inw_ref[b, :, c : c + half_hid], preferred_element_type=F32)
            bias = inb_ref[b : b + 1, c : c + half_hid]
            act = [gelu_twice((hid[i : i + tile] + bias).astype(BF)) for i in range(0, hid.shape[0], tile)]
            part = jnp.dot(jnp.concatenate(act, axis=0), outw_ref[b, c : c + half_hid, :], preferred_element_type=F32)
            branch = part if branch is None else branch + part
        scale = scale_ref[b : b + 1, :]
        branch = branch * (0.5 * scale) + outb_ref[b : b + 1, :] * scale
        return [branch[i * n : (i + 1) * n] for i in range(len(conv_rows))]

    def inner(b, wide, emit):
        def one(t, carry):
            for half in range(2):
                parts = [
                    acc_ref[gr, pl.ds(pl.multiple_of(t * wide, 16), wide), half * ch : (half + 1) * ch]
                    for gr in range(groups)
                ]
                for j, branch in enumerate(mlp(b, regroup(parts, width))):
                    emit(OUTS * t + half * (OUTS // 2) + j, branch)
            return carry

        lax.fori_loop(0, octets, one, 0)

    build(0)
    shift(x0_ref, REACH - HALO, lead, wide0)
    conv(wide0)

    def keep0(row, branch):
        new = x0_ref[row + REACH, lead + HALO : lead + HALO + wide0, :] + branch
        x1_ref[row + HALO, :, :] = new.astype(BF).astype(F32)

    inner(0, wide0, keep0)
    piece = wide0 // 3
    for side in range(2):
        first = 0 if side == 0 else rows + HALO
        for c in range(0, wide0, piece):
            sums = [jnp.zeros((piece, ch), F32) for _ in range(HALO)]
            for s in range(TAPS):
                lines = [x0_ref[first + i, lead + s + c : lead + s + c + piece, :] for i in range(TAPS + HALO - 1)]
                for r in range(TAPS):
                    tap = TAPS * r + s
                    if side == 1:
                        tap = jnp.where(top, TAPS * TAPS - 1 - tap, tap)
                    weight = k_ref[0, pl.ds(tap, 1), :]
                    for i in range(HALO):
                        sums[i] = sums[i] + lines[i + r] * weight
            for i in range(HALO):
                strip_ref[side * HALO + i, c : c + piece, :] = sums[i]
    for side in range(2):
        branches = mlp(0, [strip_ref[side * HALO + i] for i in range(HALO)])
        for i, branch in enumerate(branches):
            row = i - HALO if side == 0 else rows + i
            new = x0_ref[row + REACH, lead + HALO : lead + HALO + wide0, :] + branch
            new = new.astype(BF).astype(F32)
            if side == 0:
                new = jnp.where(bottom, 0.0, new)
            x1_ref[row + HALO, :, :] = new
    for i in range(rows + 2 * HALO, x1_ref.shape[0]):
        x1_ref[i, :, :] = jnp.zeros((wide0, ch), F32)

    build(1)
    shift(x1_ref, 0, 0, cols)
    conv(cols)

    def keep1(row, branch):
        new = x1_ref[row + HALO, HALO : HALO + cols, :] + branch
        out_ref[row] = new.astype(BF) * mask_ref[row]

    inner(1, cols, keep1)


def shards(
    fields,
    wet_mask,
    conv_kernel,
    conv_bias,
    norm_gain,
    norm_bias,
    in_weight,
    in_bias,
    out_weight,
    out_bias,
    layer_scale,
):
    rows, cols, ch = fields.shape
    left, right, got_a, got_b = exchange(fields, wet_mask)
    mask = jnp.broadcast_to(wet_mask.astype(BF)[:, :, None], fields.shape)
    state = fields * mask
    hid = in_weight.shape[2]
    width = 2 * ch // OUTS
    groups = ch // width
    wide0 = cols + 16
    octets = rows // OUTS
    cells = rows * cols
    vmem = pl.BlockSpec(memory_space=pltpu.VMEM)
    return pl.pallas_call(
        both_blocks,
        in_specs=[vmem] * 15,
        out_specs=vmem,
        out_shape=jax.ShapeDtypeStruct(fields.shape, BF),
        scratch_shapes=[
            pltpu.VMEM((rows + 2 * REACH, wide0 + 8, ch), F32),
            pltpu.VMEM((rows + 8, wide0, ch), F32),
            pltpu.VMEM((TAPS, groups, 2, octets + 1, wide0, ch), BF),
            pltpu.VMEM((groups, wide0 + 8, ch), F32),
            pltpu.VMEM((groups, TAPS * 2 * OUTS * width, OUTS * width), BF),
            pltpu.VMEM((groups, octets * wide0, OUTS * width), F32),
            pltpu.VMEM((2 * HALO, wide0, ch), F32),
            pltpu.VMEM((wide0 + 8, ch), F32),
            pltpu.VMEM((groups, 2 * OUTS, 8, OUTS * width), F32),
        ],
        compiler_params=pltpu.CompilerParams(vmem_limit_bytes=VMEM_LIMIT),
        cost_estimate=pl.CostEstimate(
            flops=4 * cells * (4 * ch * hid + 8 * ch * 2 * ch), bytes_accessed=6 * cells * ch, transcendentals=2 * cells * hid
        ),
        name="both_blocks",
    )(
        state,
        mask,
        left,
        right,
        got_a,
        got_b,
        conv_kernel,
        conv_bias,
        norm_gain,
        norm_bias,
        in_weight,
        in_bias,
        out_weight,
        out_bias,
        layer_scale,
    )


def solution(mesh):
    return jax.shard_map(
        shards,
        mesh=mesh,
        in_specs=(P("lat", "lon", None), P("lat", "lon")) + (P(),) * 9,
        out_specs=P("lat", "lon", None),
        check_vma=False,
    )
```

```python
import jax
import jax.numpy as jnp
from jax import lax
from jax.experimental import pallas as pl
from jax.experimental.pallas import tpu as pltpu
from jax.sharding import PartitionSpec as P

BF = jnp.bfloat16
F32 = jnp.float32
TAPS = 7
HALO = 3
REACH = 2 * HALO
OUTS = 8
ROLLED = jnp.bfloat16
VMEM_LIMIT = 48 * 1024 * 1024
ERF_POLY = (0.7975078797359708, 0.03700565107996738, -0.0003515176683895368)


def partners(nlat, nlon, parity):
    route = []
    for lat in range(nlat):
        for lon in range(nlon):
            here = lat * nlon + lon
            if lat % 2 == parity:
                there = here + nlon if lat + 1 < nlat else lat * nlon + nlon - 1 - lon
            elif lat > 0:
                there = here - nlon
            else:
                continue
            route.append((here, there))
    return route


def exchange(fields, wet_mask):
    nlat, nlon = lax.axis_size("lat"), lax.axis_size("lon")
    lat = lax.axis_index("lat")
    rows, cols = wet_mask.shape

    def edge(r0, r1, c0, c1):
        return fields[r0:r1, c0:c1] * wet_mask[r0:r1, c0:c1].astype(BF)[:, :, None]

    up = [(i, (i + 1) % nlon) for i in range(nlon)]
    down = [(j, i) for i, j in up]
    left = lax.ppermute(edge(0, rows, cols - REACH, cols), "lon", up)
    right = lax.ppermute(edge(0, rows, 0, REACH), "lon", down)
    first = jnp.concatenate([left[:REACH], edge(0, REACH, 0, cols), right[:REACH]], axis=1)
    last = jnp.concatenate([left[rows - REACH :], edge(rows - REACH, rows, 0, cols), right[rows - REACH :]], axis=1)
    even = lat % 2 == 0
    got_a = lax.ppermute(jnp.where(even, last, first), ("lat", "lon"), partners(nlat, nlon, 0))
    got_b = lax.ppermute(jnp.where(even, first, last), ("lat", "lon"), partners(nlat, nlon, 1))
    return left, right, got_a, got_b


def regroup(parts, width):
    parts = list(parts)
    ch = parts[0].shape[-1]
    block = lax.broadcasted_iota(jnp.int32, parts[0].shape, parts[0].ndim - 1) // width
    step = 1
    while step < len(parts):
        low = (block & step) == 0
        for i in range(len(parts)):
            if not i & step:
                x, y = parts[i], parts[i + step]
                parts[i] = jnp.where(low, x, pltpu.roll(y, step * width, x.ndim - 1))
                parts[i + step] = jnp.where(low, pltpu.roll(x, ch - step * width, x.ndim - 1), y)
        step *= 2
    return parts


def tap_kernel(k_ref, w_ref, kv_ref):
    ch = k_ref.shape[2]
    lanes = w_ref.shape[3]
    width = lanes // OUTS
    groups = ch // width
    gr = pl.program_id(1)

    @pl.when(gr == 0)
    def _():
        down = [k_ref[0, pl.ds(s, TAPS, stride=TAPS), :] for s in range(TAPS - 1, -1, -1)]
        down.append(jnp.zeros((TAPS, ch), F32))
        halves = [regroup(down[i : i + groups], width) for i in range(0, OUTS, groups)]
        out_col = lax.broadcasted_iota(jnp.int32, (TAPS, lanes), 1) // width
        for g in range(groups):
            line = jnp.concatenate([half[g] for half in halves], axis=1)
            for p in range(2 * OUTS):
                turned = pltpu.roll(line, (p - TAPS + 1) * width % lanes, 1)
                seen = (out_col <= p) & (out_col >= p - TAPS + 1)
                kv_ref[g, p, 0:TAPS, :] = jnp.where(seen, turned, 0.0)

    lane = lax.broadcasted_iota(jnp.int32, (width, lanes), 1)
    own = (lane % width) == lax.broadcasted_iota(jnp.int32, (width, lanes), 0)
    for r in range(TAPS):
        for p in range(2 * OUTS):
            vec = kv_ref[gr, p, r : r + 1, :]
            at = (r * 2 * OUTS + p) * width
            w_ref[0, 0, at : at + width, :] = jnp.where(own, vec, 0.0).astype(BF)


def tap_matrices(conv_kernel):
    blocks, taps, ch = conv_kernel.shape
    lanes = 2 * ch
    width = lanes // OUTS
    groups = ch // width
    depth = TAPS * 2 * OUTS * width
    return pl.pallas_call(
        tap_kernel,
        grid=(blocks, groups),
        in_specs=[pl.BlockSpec((1, taps, ch), lambda b, g: (b, 0, 0))],
        out_specs=pl.BlockSpec((1, 1, depth, lanes), lambda b, g: (b, g, 0, 0)),
        out_shape=jax.ShapeDtypeStruct((blocks, groups, depth, lanes), BF),
        scratch_shapes=[pltpu.VMEM((groups, 2 * OUTS, 8, lanes), F32)],
        compiler_params=pltpu.CompilerParams(vmem_limit_bytes=24 * 1024 * 1024),
        cost_estimate=pl.CostEstimate(
            flops=0, bytes_accessed=2 * blocks * groups * depth * lanes, transcendentals=0
        ),
        name="tap_matrices",
    )(conv_kernel)


def both_blocks(
    x_ref,
    mask_ref,
    left_ref,
    right_ref,
    a_ref,
    b_ref,
    k_ref,
    w_hbm,
    cbias_ref,
    gain_ref,
    nbias_ref,
    inw_ref,
    inb_ref,
    outw_ref,
    outb_ref,
    scale_ref,
    out_ref,
    x0_ref,
    x1_ref,
    relaid_ref,
    w_ref,
    acc_ref,
    strip_ref,
    flip_ref,
    w_sem,
):
    rows, cols, ch = x_ref.shape
    width = 2 * ch // OUTS
    groups = ch // width
    octets = cols // OUTS
    base = 8
    ext = cols + 2 * REACH
    lead = base - REACH
    near = base - HALO
    pitch = cols + 24
    wide0 = cols + 16
    lat = lax.axis_index("lat")
    even, top, bottom = lat % 2 == 0, lat == lax.axis_size("lat") - 1, lat == 0

    copies = [pltpu.make_async_copy(w_hbm.at[b], w_ref.at[b], w_sem.at[b]) for b in range(2)]
    for copy in copies:
        copy.start()

    def line(row):
        return pl.multiple_of((row + REACH) * pitch, 8)

    def fill(i, carry):
        at = line(i)
        x0_ref[pl.ds(at, base), :] = jnp.zeros((base, ch), F32)
        x0_ref[pl.ds(at + lead, REACH), :] = left_ref[i].astype(F32)
        x0_ref[pl.ds(at + base, cols), :] = x_ref[i].astype(F32)
        x0_ref[pl.ds(at + base + cols, 16), :] = jnp.zeros((16, ch), F32)
        x0_ref[pl.ds(at + base + cols, REACH), :] = right_ref[i].astype(F32)
        x1_ref[pl.ds(at, base), :] = jnp.zeros((base, ch), F32)
        x1_ref[pl.ds(at + base + cols, 16), :] = jnp.zeros((16, ch), F32)
        return carry

    lax.fori_loop(0, rows, fill, 0)
    flip_ref[...] = jnp.zeros(flip_ref.shape, F32)
    at = lax.broadcasted_iota(jnp.int32, (wide0, wide0), 0)
    to = lax.broadcasted_iota(jnp.int32, (wide0, wide0), 1)
    mirror = jnp.where(to == jnp.where(top, ext - 1 - at, at), 1.0, 0.0).astype(BF)
    for i in range(REACH):
        south, north = i * pitch, (rows + REACH + i) * pitch
        x0_ref[south : south + pitch, :] = jnp.zeros((pitch, ch), F32)
        x0_ref[south + lead : south + lead + ext, :] = jnp.where(even, b_ref[i].astype(F32), a_ref[i].astype(F32))
        src = jnp.where(top, REACH - 1 - i, i)
        flip_ref[0:ext, :] = jnp.where(even, a_ref[src].astype(F32), b_ref[src].astype(F32))
        turned = jnp.dot(mirror, flip_ref[0:wide0, :].astype(BF), preferred_element_type=F32)
        x0_ref[north : north + pitch, :] = jnp.zeros((pitch, ch), F32)
        x0_ref[north + lead : north + lead + wide0, :] = turned

    def relay(src_ref):
        def one(i, carry):
            at = line(i - HALO) + near
            for a in range(4):
                parts = [
                    src_ref[pl.ds(at + 4 * a + j, octets, stride=OUTS), :].astype(ROLLED) for j in range(groups)
                ]
                for gr, part in enumerate(regroup(parts, width)):
                    relaid_ref[gr, a, pl.ds(pl.multiple_of(i * octets, 16), octets), :] = part.astype(BF)
            return carry

        lax.fori_loop(0, rows + 2 * HALO, one, 0)

    def conv(b):
        def one(gr, carry):
            parts = []
            for r in range(TAPS):
                for a in range(4):
                    parts.append(relaid_ref[gr, a, r * octets : (r + rows) * octets, :])
            acc_ref[gr] = jnp.dot(jnp.concatenate(parts, axis=1), w_ref[b, gr], preferred_element_type=F32)
            return carry

        lax.fori_loop(0, groups, one, 0)

    def gelu_twice(h):
        z = h * h
        p = jnp.full_like(z, ERF_POLY[-1])
        for coef in ERF_POLY[-2::-1]:
            p = p * z + jnp.asarray(coef, z.dtype)
        return h + h * jnp.tanh(h * p)

    def norm(b, val):
        val = val + cbias_ref[b : b + 1, :]
        cen = val - jnp.mean(val, axis=-1, keepdims=True)
        var = jnp.mean(cen * cen, axis=-1, keepdims=True)
        return (cen * lax.rsqrt(var + 1e-6) * gain_ref[b : b + 1, :] + nbias_ref[b : b + 1, :]).astype(BF)

    def mlp(b, parts):
        n = parts[0].shape[0]
        normed = jnp.concatenate([norm(b, part) for part in parts], axis=0)
        tile = 48 if n % 48 == 0 else 64
        branch = None
        half_hid = inw_ref.shape[2] // 2
        for c in range(0, 2 * half_hid, half_hid):
            hid = jnp.dot(normed, inw_ref[b, :, c : c + half_hid], preferred_element_type=F32)
            bias = inb_ref[b : b + 1, c : c + half_hid]
            act = [gelu_twice((hid[i : i + tile] + bias).astype(BF)) for i in range(0, hid.shape[0], tile)]
            part = jnp.dot(jnp.concatenate(act, axis=0), outw_ref[b, c : c + half_hid, :], preferred_element_type=F32)
            branch = part if branch is None else branch + part
        scale = scale_ref[b : b + 1, :]
        branch = branch * (0.5 * scale) + outb_ref[b : b + 1, :] * scale
        return [branch[i * n : (i + 1) * n] for i in range(len(parts))]

    def rounded(val):
        return val.astype(BF).astype(F32)

    def inner(b, src_ref):
        step = next(d for d in (8, 6, 4, 3, 2, 1) if rows % d == 0)
        n = step * octets

        def one(t, carry):
            for half in range(2):
                parts = [
                    acc_ref[gr, pl.ds(pl.multiple_of(t * n, 16), n), half * ch : (half + 1) * ch]
                    for gr in range(groups)
                ]
                for j, branch in enumerate(mlp(b, regroup(parts, width))):
                    for i in range(step):
                        at = line(t * step + i) + base + half * groups + j
                        spot = pl.ds(at, octets, stride=OUTS)
                        x1_ref[spot, :] = rounded(src_ref[spot, :] + branch[i * octets : (i + 1) * octets])
            return carry

        lax.fori_loop(0, rows // step, one, 0)

    relay(x0_ref)
    copies[0].wait()
    conv(0)
    inner(0, x0_ref)
    for side in range(2):
        first = lead if side == 0 else base + cols - HALO
        sums = [jnp.zeros((rows, ch), F32) for _ in range(HALO)]
        for r in range(TAPS):
            for c in range(TAPS + HALO - 1):
                cells = x0_ref[pl.ds((REACH - HALO + r) * pitch + first + c, rows, stride=pitch), :]
                for i in range(HALO):
                    if 0 <= c - i < TAPS:
                        tap = TAPS * r + c - i
                        sums[i] = sums[i] + cells * k_ref[0, tap : tap + 1, :]
        start = near if side == 0 else base + cols
        for i, branch in enumerate(mlp(0, sums)):
            spot = pl.ds(REACH * pitch + start + i, rows, stride=pitch)
            x1_ref[spot, :] = rounded(x0_ref[spot, :] + branch)
    piece = wide0 // 3
    for side in range(2):
        first = (0 if side == 0 else rows + HALO) * pitch
        for c in range(0, wide0, piece):
            sums = [jnp.zeros((piece, ch), F32) for _ in range(HALO)]
            for s in range(TAPS):
                at = first + lead + s + c
                lines = [x0_ref[at + i * pitch : at + i * pitch + piece, :] for i in range(TAPS + HALO - 1)]
                for r in range(TAPS):
                    tap = TAPS * r + s
                    if side == 1:
                        tap = jnp.where(top, TAPS * TAPS - 1 - tap, tap)
                    weight = k_ref[0, pl.ds(tap, 1), :]
                    for i in range(HALO):
                        sums[i] = sums[i] + lines[i + r] * weight
            for i in range(HALO):
                strip_ref[side * HALO + i, c : c + piece, :] = sums[i]
    for side in range(2):
        branches = mlp(0, [strip_ref[side * HALO + i] for i in range(HALO)])
        for i, branch in enumerate(branches):
            row = i - HALO if side == 0 else rows + i
            at = (row + REACH) * pitch + near
            new = rounded(x0_ref[at : at + wide0, :] + branch)
            if side == 0:
                new = jnp.where(bottom, 0.0, new)
            x1_ref[at : at + wide0, :] = new

    relay(x1_ref)
    copies[1].wait()
    conv(1)
    inner(1, x1_ref)

    def finish(i, carry):
        out_ref[i] = x1_ref[pl.ds(line(i) + base, cols), :].astype(BF) * mask_ref[i]
        return carry

    lax.fori_loop(0, rows, finish, 0)


def shards(
    fields,
    wet_mask,
    conv_kernel,
    conv_bias,
    norm_gain,
    norm_bias,
    in_weight,
    in_bias,
    out_weight,
    out_bias,
    layer_scale,
):
    rows, cols, ch = fields.shape
    left, right, got_a, got_b = exchange(fields, wet_mask)
    mask = jnp.broadcast_to(wet_mask.astype(BF)[:, :, None], fields.shape)
    state = fields * mask
    taps = tap_matrices(conv_kernel)
    groups, depth, lanes = taps.shape[1:]
    hid = in_weight.shape[2]
    octets = cols // OUTS
    cells = rows * cols
    whole = pltpu.VMEM(((rows + 2 * REACH) * (cols + 24), ch), F32)
    vmem = pl.BlockSpec(memory_space=pltpu.VMEM)
    return pl.pallas_call(
        both_blocks,
        in_specs=[vmem] * 7 + [pl.BlockSpec(memory_space=pl.ANY)] + [vmem] * 8,
        out_specs=vmem,
        out_shape=jax.ShapeDtypeStruct(fields.shape, BF),
        scratch_shapes=[
            whole,
            whole,
            pltpu.VMEM((groups, 4, (rows + 2 * HALO) * octets, ch), BF),
            pltpu.VMEM((2, groups, depth, lanes), BF),
            pltpu.VMEM((groups, rows * octets, lanes), F32),
            pltpu.VMEM((2 * HALO, cols + 16, ch), F32),
            pltpu.VMEM((cols + 24, ch), F32),
            pltpu.SemaphoreType.DMA((2,)),
        ],
        compiler_params=pltpu.CompilerParams(vmem_limit_bytes=VMEM_LIMIT),
        cost_estimate=pl.CostEstimate(
            flops=4 * cells * (4 * ch * hid + 8 * ch * 2 * ch), bytes_accessed=6 * cells * ch, transcendentals=2 * cells * hid
        ),
        name="both_blocks",
    )(
        state,
        mask,
        left,
        right,
        got_a,
        got_b,
        conv_kernel,
        taps,
        conv_bias,
        norm_gain,
        norm_bias,
        in_weight,
        in_bias,
        out_weight,
        out_bias,
        layer_scale,
    )


def solution(mesh):
    return jax.shard_map(
        shards,
        mesh=mesh,
        in_specs=(P("lat", "lon", None), P("lat", "lon")) + (P(),) * 9,
        out_specs=P("lat", "lon", None),
        check_vma=False,
    )
```

```python
import functools

import jax
import jax.numpy as jnp
from jax import lax
from jax.experimental import pallas as pl
from jax.experimental.pallas import tpu as pltpu
from jax.sharding import PartitionSpec as P

BF = jnp.bfloat16
F32 = jnp.float32
TAPS = 7
HALO = 3
REACH = 2 * HALO
OUTS = 8
BASE = 8
VMEM_LIMIT = 30 * 1024 * 1024
ERF_POLY = (0.7975078797359708, 0.03700565107996738, -0.0003515176683895368)


def partners(nlat, nlon, parity):
    route = []
    for lat in range(nlat):
        for lon in range(nlon):
            here = lat * nlon + lon
            if lat % 2 == parity:
                there = here + nlon if lat + 1 < nlat else lat * nlon + nlon - 1 - lon
            elif lat > 0:
                there = here - nlon
            else:
                continue
            route.append((here, there))
    return route


def exchange(fields, wet_mask):
    nlat, nlon = lax.axis_size("lat"), lax.axis_size("lon")
    lat = lax.axis_index("lat")
    rows, cols = wet_mask.shape

    def edge(r0, r1, c0, c1):
        return fields[r0:r1, c0:c1] * wet_mask[r0:r1, c0:c1].astype(BF)[:, :, None]

    up = [(i, (i + 1) % nlon) for i in range(nlon)]
    down = [(j, i) for i, j in up]
    left = lax.ppermute(edge(0, rows, cols - REACH, cols), "lon", up)
    right = lax.ppermute(edge(0, rows, 0, REACH), "lon", down)
    first = jnp.concatenate([left[:REACH], edge(0, REACH, 0, cols), right[:REACH]], axis=1)
    last = jnp.concatenate([left[rows - REACH :], edge(rows - REACH, rows, 0, cols), right[rows - REACH :]], axis=1)
    even = lat % 2 == 0
    got_a = lax.ppermute(jnp.where(even, last, first), ("lat", "lon"), partners(nlat, nlon, 0))
    got_b = lax.ppermute(jnp.where(even, first, last), ("lat", "lon"), partners(nlat, nlon, 1))
    return left, right, got_a, got_b


def regroup(parts, width):
    parts = list(parts)
    ch = parts[0].shape[-1]
    block = lax.broadcasted_iota(jnp.int32, parts[0].shape, parts[0].ndim - 1) // width
    step = 1
    while step < len(parts):
        low = (block & step) == 0
        for i in range(len(parts)):
            if not i & step:
                x, y = parts[i], parts[i + step]
                parts[i] = jnp.where(low, x, pltpu.roll(y, step * width, x.ndim - 1))
                parts[i + step] = jnp.where(low, pltpu.roll(x, ch - step * width, x.ndim - 1), y)
        step *= 2
    return parts


def tap_kernel(k_ref, w_ref, kv_ref):
    ch = k_ref.shape[2]
    lanes = w_ref.shape[3]
    width = lanes // OUTS
    groups = ch // width
    gr = pl.program_id(1)

    @pl.when(gr == 0)
    def _():
        down = [k_ref[0, pl.ds(s, TAPS, stride=TAPS), :] for s in range(TAPS - 1, -1, -1)]
        down.append(jnp.zeros((TAPS, ch), F32))
        halves = [regroup(down[i : i + groups], width) for i in range(0, OUTS, groups)]
        out_col = lax.broadcasted_iota(jnp.int32, (TAPS, lanes), 1) // width
        for g in range(groups):
            line = jnp.concatenate([half[g] for half in halves], axis=1)
            for p in range(2 * OUTS):
                turned = pltpu.roll(line, (p - TAPS + 1) * width % lanes, 1)
                seen = (out_col <= p) & (out_col >= p - TAPS + 1)
                kv_ref[g, p, 0:TAPS, :] = jnp.where(seen, turned, 0.0)

    lane = lax.broadcasted_iota(jnp.int32, (width, lanes), 1)
    own = (lane % width) == lax.broadcasted_iota(jnp.int32, (width, lanes), 0)
    for r in range(TAPS):
        for p in range(2 * OUTS):
            vec = kv_ref[gr, p, r : r + 1, :]
            at = (r * 2 * OUTS + p) * width
            w_ref[0, 0, at : at + width, :] = jnp.where(own, vec, 0.0).astype(BF)


def tap_matrices(conv_kernel):
    blocks, taps, ch = conv_kernel.shape
    lanes = 2 * ch
    width = lanes // OUTS
    groups = ch // width
    depth = TAPS * 2 * OUTS * width
    return pl.pallas_call(
        tap_kernel,
        grid=(blocks, groups),
        in_specs=[pl.BlockSpec((1, taps, ch), lambda b, g: (b, 0, 0))],
        out_specs=pl.BlockSpec((1, 1, depth, lanes), lambda b, g: (b, g, 0, 0)),
        out_shape=jax.ShapeDtypeStruct((blocks, groups, depth, lanes), BF),
        scratch_shapes=[pltpu.VMEM((groups, 2 * OUTS, 8, lanes), F32)],
        compiler_params=pltpu.CompilerParams(vmem_limit_bytes=24 * 1024 * 1024),
        cost_estimate=pl.CostEstimate(
            flops=0, bytes_accessed=2 * blocks * groups * depth * lanes, transcendentals=0
        ),
        name="tap_matrices",
    )(conv_kernel)


class Sizes:
    def __init__(self, rows, cols, ch):
        self.rows, self.cols, self.ch = rows, cols, ch
        self.width = 2 * ch // OUTS
        self.groups = ch // self.width
        self.octets = cols // OUTS
        self.pitch = cols + 24
        self.lines = (rows + 2 * REACH) * self.pitch
        self.wide0 = cols + 16

    def line(self, row):
        return pl.multiple_of((row + REACH) * self.pitch, 8)


def place():
    lat = lax.axis_index("lat")
    return lat % 2 == 0, lat == lax.axis_size("lat") - 1, lat == 0


def relay(size, src_ref, relaid_ref):
    def one(i, carry):
        at = size.line(i - HALO) + BASE - HALO
        for a in range(4):
            parts = [
                src_ref[pl.ds(at + 4 * a + j, size.octets, stride=OUTS), :].astype(BF) for j in range(size.groups)
            ]
            for gr, part in enumerate(regroup(parts, size.width)):
                relaid_ref[gr, a, pl.ds(pl.multiple_of(i * size.octets, 16), size.octets), :] = part
        return carry

    lax.fori_loop(0, size.rows + 2 * HALO, one, 0)


def conv(size, relaid_ref, w_ref, acc_ref):
    octets, rows = size.octets, size.rows

    def one(gr, carry):
        parts = []
        for r in range(TAPS):
            for a in range(4):
                parts.append(relaid_ref[gr, a, r * octets : (r + rows) * octets, :])
        acc_ref[gr] = jnp.dot(jnp.concatenate(parts, axis=1), w_ref[0, gr], preferred_element_type=F32)
        return carry

    lax.fori_loop(0, size.groups, one, 0)


def conv0_kernel(size, x_ref, left_ref, right_ref, a_ref, b_ref, w_ref, x0_ref, acc_ref, relaid_ref, flip_ref):
    rows, cols, ch, pitch, wide0 = size.rows, size.cols, size.ch, size.pitch, size.wide0
    base, ext, lead = BASE, cols + 2 * REACH, BASE - REACH
    line = size.line
    even, top, _ = place()

    def fill(i, carry):
        at = line(i)
        x0_ref[pl.ds(at, base), :] = jnp.zeros((base, ch), F32)
        x0_ref[pl.ds(at + lead, REACH), :] = left_ref[i].astype(F32)
        x0_ref[pl.ds(at + base, cols), :] = x_ref[i].astype(F32)
        x0_ref[pl.ds(at + base + cols, 16), :] = jnp.zeros((16, ch), F32)
        x0_ref[pl.ds(at + base + cols, REACH), :] = right_ref[i].astype(F32)
        return carry

    lax.fori_loop(0, rows, fill, 0)
    flip_ref[...] = jnp.zeros(flip_ref.shape, F32)
    at = lax.broadcasted_iota(jnp.int32, (wide0, wide0), 0)
    to = lax.broadcasted_iota(jnp.int32, (wide0, wide0), 1)
    mirror = jnp.where(to == jnp.where(top, ext - 1 - at, at), 1.0, 0.0).astype(BF)
    for i in range(REACH):
        south, north = i * pitch, (rows + REACH + i) * pitch
        x0_ref[south : south + pitch, :] = jnp.zeros((pitch, ch), F32)
        x0_ref[south + lead : south + lead + ext, :] = jnp.where(even, b_ref[i].astype(F32), a_ref[i].astype(F32))
        src = jnp.where(top, REACH - 1 - i, i)
        flip_ref[0:ext, :] = jnp.where(even, a_ref[src].astype(F32), b_ref[src].astype(F32))
        turned = jnp.dot(mirror, flip_ref[0:wide0, :].astype(BF), preferred_element_type=F32)
        x0_ref[north : north + pitch, :] = jnp.zeros((pitch, ch), F32)
        x0_ref[north + lead : north + lead + wide0, :] = turned
    relay(size, x0_ref, relaid_ref)
    conv(size, relaid_ref, w_ref, acc_ref)


def conv1_kernel(size, x1_ref, w_ref, acc_ref, relaid_ref):
    relay(size, x1_ref, relaid_ref)
    conv(size, relaid_ref, w_ref, acc_ref)


def gelu_twice(h):
    z = h * h
    p = jnp.full_like(z, ERF_POLY[-1])
    for coef in ERF_POLY[-2::-1]:
        p = p * z + jnp.asarray(coef, z.dtype)
    return h + h * jnp.tanh(h * p)


def norm(b, params, val):
    cbias_ref, gain_ref, nbias_ref = params[:3]
    val = val + cbias_ref[b : b + 1, :]
    cen = val - jnp.mean(val, axis=-1, keepdims=True)
    var = jnp.mean(cen * cen, axis=-1, keepdims=True)
    return (cen * lax.rsqrt(var + 1e-6) * gain_ref[b : b + 1, :] + nbias_ref[b : b + 1, :]).astype(BF)


def mlp(b, params, parts):
    inw_ref, inb_ref, outw_ref, outb_ref, scale_ref = params[3:]
    n = parts[0].shape[0]
    normed = jnp.concatenate([norm(b, params, part) for part in parts], axis=0)
    tile = 48 if n % 48 == 0 else 64
    branch = None
    half_hid = inw_ref.shape[2] // 2
    for c in range(0, 2 * half_hid, half_hid):
        hid = jnp.dot(normed, inw_ref[b, :, c : c + half_hid], preferred_element_type=F32)
        bias = inb_ref[b : b + 1, c : c + half_hid]
        act = [gelu_twice((hid[i : i + tile] + bias).astype(BF)) for i in range(0, hid.shape[0], tile)]
        part = jnp.dot(jnp.concatenate(act, axis=0), outw_ref[b, c : c + half_hid, :], preferred_element_type=F32)
        branch = part if branch is None else branch + part
    scale = scale_ref[b : b + 1, :]
    branch = branch * (0.5 * scale) + outb_ref[b : b + 1, :] * scale
    return [branch[i * n : (i + 1) * n] for i in range(len(parts))]

def rounded(val):
    return val.astype(BF).astype(F32)


def rounded(val):
    return val.astype(BF).astype(F32)


def inner(size, b, params, acc_ref, src_ref, dst_ref):
    rows, octets, groups, ch = size.rows, size.octets, size.groups, size.ch
    step = next(d for d in (8, 6, 4, 3, 2, 1) if rows % d == 0)
    n = step * octets

    def one(t, carry):
        for half in range(2):
            parts = [
                acc_ref[gr, pl.ds(pl.multiple_of(t * n, 16), n), half * ch : (half + 1) * ch] for gr in range(groups)
            ]
            for j, branch in enumerate(mlp(b, params, regroup(parts, size.width))):
                for i in range(step):
                    at = size.line(t * step + i) + BASE + half * groups + j
                    spot = pl.ds(at, octets, stride=OUTS)
                    dst_ref[spot, :] = rounded(src_ref[spot, :] + branch[i * octets : (i + 1) * octets])
        return carry

    lax.fori_loop(0, rows // step, one, 0)


def mlp0_kernel(size, acc_ref, x0_ref, k_ref, *refs):
    params, (x1_ref, strip_ref) = refs[:8], refs[8:]
    rows, cols, ch, pitch, wide0 = size.rows, size.cols, size.ch, size.pitch, size.wide0
    base, lead, near = BASE, BASE - REACH, BASE - HALO
    _, top, bottom = place()

    def clear(i, carry):
        at = size.line(i)
        x1_ref[pl.ds(at, base), :] = jnp.zeros((base, ch), F32)
        x1_ref[pl.ds(at + base + cols, 16), :] = jnp.zeros((16, ch), F32)
        return carry

    lax.fori_loop(0, rows, clear, 0)
    inner(size, 0, params, acc_ref, x0_ref, x1_ref)
    for side in range(2):
        first = lead if side == 0 else base + cols - HALO
        sums = [jnp.zeros((rows, ch), F32) for _ in range(HALO)]
        for r in range(TAPS):
            for c in range(TAPS + HALO - 1):
                cells = x0_ref[pl.ds((REACH - HALO + r) * pitch + first + c, rows, stride=pitch), :]
                for i in range(HALO):
                    if 0 <= c - i < TAPS:
                        tap = TAPS * r + c - i
                        sums[i] = sums[i] + cells * k_ref[0, tap : tap + 1, :]
        start = near if side == 0 else base + cols
        for i, branch in enumerate(mlp(0, params, sums)):
            spot = pl.ds(REACH * pitch + start + i, rows, stride=pitch)
            x1_ref[spot, :] = rounded(x0_ref[spot, :] + branch)
    piece = wide0 // 3
    for side in range(2):
        first = (0 if side == 0 else rows + HALO) * pitch
        for c in range(0, wide0, piece):
            sums = [jnp.zeros((piece, ch), F32) for _ in range(HALO)]
            for s in range(TAPS):
                at = first + lead + s + c
                lines = [x0_ref[at + i * pitch : at + i * pitch + piece, :] for i in range(TAPS + HALO - 1)]
                for r in range(TAPS):
                    tap = TAPS * r + s
                    if side == 1:
                        tap = jnp.where(top, TAPS * TAPS - 1 - tap, tap)
                    weight = k_ref[0, pl.ds(tap, 1), :]
                    for i in range(HALO):
                        sums[i] = sums[i] + lines[i + r] * weight
            for i in range(HALO):
                strip_ref[side * HALO + i, c : c + piece, :] = sums[i]
    for side in range(2):
        branches = mlp(0, params, [strip_ref[side * HALO + i] for i in range(HALO)])
        for i, branch in enumerate(branches):
            row = i - HALO if side == 0 else rows + i
            at = (row + REACH) * pitch + near
            new = rounded(x0_ref[at : at + wide0, :] + branch)
            if side == 0:
                new = jnp.where(bottom, 0.0, new)
            x1_ref[at : at + wide0, :] = new


def mlp1_kernel(size, acc_ref, x1_ref, mask_ref, *refs):
    params, (out_ref, x2_ref) = refs[:8], refs[8:]
    inner(size, 1, params, acc_ref, x1_ref, x2_ref)

    def finish(i, carry):
        out_ref[i] = x2_ref[pl.ds(size.line(i) + BASE, size.cols), :].astype(BF) * mask_ref[i]
        return carry

    lax.fori_loop(0, size.rows, finish, 0)


def shards(
    fields,
    wet_mask,
    conv_kernel,
    conv_bias,
    norm_gain,
    norm_bias,
    in_weight,
    in_bias,
    out_weight,
    out_bias,
    layer_scale,
):
    rows, cols, ch = fields.shape
    left, right, got_a, got_b = exchange(fields, wet_mask)
    mask = jnp.broadcast_to(wet_mask.astype(BF)[:, :, None], fields.shape)
    state = fields * mask
    taps = tap_matrices(conv_kernel)
    groups, depth, lanes = taps.shape[1:]
    hid = in_weight.shape[2]
    size = Sizes(rows, cols, ch)
    cells = rows * cols
    vmem = pl.BlockSpec(memory_space=pltpu.VMEM)
    relaid = pltpu.VMEM((groups, 4, (rows + 2 * HALO) * size.octets, ch), BF)
    padded = jax.ShapeDtypeStruct((size.lines, ch), F32)
    sums = jax.ShapeDtypeStruct((groups, rows * size.octets, lanes), F32)

    def call(kernel, ins, out_shape, scratch, flops):
        def spec(value):
            if value is not taps:
                return vmem
            block = 0 if kernel is conv0_kernel else 1
            return pl.BlockSpec((1, groups, depth, lanes), lambda i: (block, 0, 0, 0))

        several = isinstance(out_shape, tuple)
        return pl.pallas_call(
            functools.partial(kernel, size),
            grid=(1,),
            in_specs=[spec(value) for value in ins],
            out_specs=(vmem,) * len(out_shape) if several else vmem,
            out_shape=out_shape,
            scratch_shapes=scratch,
            compiler_params=pltpu.CompilerParams(vmem_limit_bytes=VMEM_LIMIT),
            cost_estimate=pl.CostEstimate(flops=flops, bytes_accessed=6 * cells * ch, transcendentals=cells * hid),
            name=kernel.__name__,
        )(*ins)

    conv_flops = 2 * cells * ch * depth // OUTS * 2
    mlp_flops = 4 * cells * ch * hid
    params = (conv_bias, norm_gain, norm_bias, in_weight, in_bias, out_weight, out_bias, layer_scale)
    x0, acc = call(
        conv0_kernel,
        (state, left, right, got_a, got_b, taps),
        (padded, sums),
        [relaid, pltpu.VMEM((cols + 24, ch), F32)],
        conv_flops,
    )
    strips = pltpu.VMEM((2 * HALO, cols + 16, ch), F32)
    x1 = call(mlp0_kernel, (acc, x0, conv_kernel) + params, padded, [strips], mlp_flops)
    acc = call(conv1_kernel, (x1, taps), sums, [relaid], conv_flops)
    whole = pltpu.VMEM((size.lines, ch), F32)
    return call(mlp1_kernel, (acc, x1, mask) + params, jax.ShapeDtypeStruct(fields.shape, BF), [whole], mlp_flops)


def solution(mesh):
    return jax.shard_map(
        shards,
        mesh=mesh,
        in_specs=(P("lat", "lon", None), P("lat", "lon")) + (P(),) * 9,
        out_specs=P("lat", "lon", None),
        check_vma=False,
    )
```

```python
import functools

import jax
import jax.numpy as jnp
from jax import lax
from jax.experimental import pallas as pl
from jax.experimental.pallas import tpu as pltpu
from jax.sharding import PartitionSpec as P

BF = jnp.bfloat16
F32 = jnp.float32
TAPS = 7
HALO = 3
REACH = 2 * HALO
OUTS = 8
BASE = 8
VMEM_LIMIT = 16 * 1024 * 1024
ERF_POLY = (0.7975078797359708, 0.03700565107996738, -0.0003515176683895368)


def partners(nlat, nlon, parity):
    route = []
    for lat in range(nlat):
        for lon in range(nlon):
            here = lat * nlon + lon
            if lat % 2 == parity:
                there = here + nlon if lat + 1 < nlat else lat * nlon + nlon - 1 - lon
            elif lat > 0:
                there = here - nlon
            else:
                continue
            route.append((here, there))
    return route


def exchange(fields, wet_mask):
    nlat, nlon = lax.axis_size("lat"), lax.axis_size("lon")
    lat = lax.axis_index("lat")
    rows, cols = wet_mask.shape

    def edge(r0, r1, c0, c1):
        return fields[r0:r1, c0:c1] * wet_mask[r0:r1, c0:c1].astype(BF)[:, :, None]

    up = [(i, (i + 1) % nlon) for i in range(nlon)]
    down = [(j, i) for i, j in up]
    left = lax.ppermute(edge(0, rows, cols - REACH, cols), "lon", up)
    right = lax.ppermute(edge(0, rows, 0, REACH), "lon", down)
    first = jnp.concatenate([left[:REACH], edge(0, REACH, 0, cols), right[:REACH]], axis=1)
    last = jnp.concatenate([left[rows - REACH :], edge(rows - REACH, rows, 0, cols), right[rows - REACH :]], axis=1)
    even = lat % 2 == 0
    got_a = lax.ppermute(jnp.where(even, last, first), ("lat", "lon"), partners(nlat, nlon, 0))
    got_b = lax.ppermute(jnp.where(even, first, last), ("lat", "lon"), partners(nlat, nlon, 1))
    return left, right, got_a, got_b


def regroup(parts, width):
    parts = list(parts)
    ch = parts[0].shape[-1]
    block = lax.broadcasted_iota(jnp.int32, parts[0].shape, parts[0].ndim - 1) // width
    step = 1
    while step < len(parts):
        low = (block & step) == 0
        for i in range(len(parts)):
            if not i & step:
                x, y = parts[i], parts[i + step]
                parts[i] = jnp.where(low, x, pltpu.roll(y, step * width, x.ndim - 1))
                parts[i + step] = jnp.where(low, pltpu.roll(x, ch - step * width, x.ndim - 1), y)
        step *= 2
    return parts


def tap_kernel(k_ref, w_ref, kv_ref):
    ch = k_ref.shape[2]
    lanes = w_ref.shape[3]
    width = lanes // OUTS
    groups = ch // width
    gr = pl.program_id(1)

    @pl.when(gr == 0)
    def _():
        down = [k_ref[0, pl.ds(s, TAPS, stride=TAPS), :] for s in range(TAPS - 1, -1, -1)]
        down.append(jnp.zeros((TAPS, ch), F32))
        halves = [regroup(down[i : i + groups], width) for i in range(0, OUTS, groups)]
        out_col = lax.broadcasted_iota(jnp.int32, (TAPS, lanes), 1) // width
        for g in range(groups):
            line = jnp.concatenate([half[g] for half in halves], axis=1)
            for p in range(2 * OUTS):
                turned = pltpu.roll(line, (p - TAPS + 1) * width % lanes, 1)
                seen = (out_col <= p) & (out_col >= p - TAPS + 1)
                kv_ref[g, p, 0:TAPS, :] = jnp.where(seen, turned, 0.0)

    lane = lax.broadcasted_iota(jnp.int32, (width, lanes), 1)
    own = (lane % width) == lax.broadcasted_iota(jnp.int32, (width, lanes), 0)
    for r in range(TAPS):
        for p in range(2 * OUTS):
            vec = kv_ref[gr, p, r : r + 1, :]
            at = (r * 2 * OUTS + p) * width
            w_ref[0, 0, at : at + width, :] = jnp.where(own, vec, 0.0).astype(BF)


def tap_matrices(conv_kernel):
    blocks, taps, ch = conv_kernel.shape
    lanes = 2 * ch
    width = lanes // OUTS
    groups = ch // width
    depth = TAPS * 2 * OUTS * width
    return pl.pallas_call(
        tap_kernel,
        grid=(blocks, groups),
        in_specs=[pl.BlockSpec((1, taps, ch), lambda b, g: (b, 0, 0))],
        out_specs=pl.BlockSpec((1, 1, depth, lanes), lambda b, g: (b, g, 0, 0)),
        out_shape=jax.ShapeDtypeStruct((blocks, groups, depth, lanes), BF),
        scratch_shapes=[pltpu.VMEM((groups, 2 * OUTS, 8, lanes), F32)],
        compiler_params=pltpu.CompilerParams(vmem_limit_bytes=24 * 1024 * 1024),
        cost_estimate=pl.CostEstimate(
            flops=0, bytes_accessed=2 * blocks * groups * depth * lanes, transcendentals=0
        ),
        name="tap_matrices",
    )(conv_kernel)


class Sizes:
    def __init__(self, rows, cols, ch):
        self.rows, self.cols, self.ch = rows, cols, ch
        self.width = 2 * ch // OUTS
        self.groups = ch // self.width
        self.octets = cols // OUTS
        self.pitch = cols + 24
        self.lines = (rows + 2 * REACH) * self.pitch
        self.wide0 = cols + 16

    def line(self, row):
        return pl.multiple_of((row + REACH) * self.pitch, 8)


def place():
    lat = lax.axis_index("lat")
    return lat % 2 == 0, lat == lax.axis_size("lat") - 1, lat == 0


def relay(size, src_ref, relaid_ref):
    def one(i, carry):
        at = size.line(i - HALO) + BASE - HALO
        for a in range(4):
            parts = [
                src_ref[pl.ds(at + 4 * a + j, size.octets, stride=OUTS), :].astype(BF) for j in range(size.groups)
            ]
            for gr, part in enumerate(regroup(parts, size.width)):
                relaid_ref[gr, a, pl.ds(pl.multiple_of(i * size.octets, 16), size.octets), :] = part
        return carry

    lax.fori_loop(0, size.rows + 2 * HALO, one, 0)


def conv(size, relaid_ref, w_ref, acc_ref):
    octets, rows = size.octets, size.rows

    for gr in range(size.groups):
        parts = []
        for r in range(TAPS):
            for a in range(4):
                parts.append(relaid_ref[gr, a, r * octets : (r + rows) * octets, :])
        acc_ref[gr] = jnp.dot(jnp.concatenate(parts, axis=1), w_ref[0, gr], preferred_element_type=F32)


def conv0_kernel(size, x_ref, left_ref, right_ref, a_ref, b_ref, w_ref, x0_ref, acc_ref, relaid_ref, flip_ref):
    rows, cols, ch, pitch, wide0 = size.rows, size.cols, size.ch, size.pitch, size.wide0
    base, ext, lead = BASE, cols + 2 * REACH, BASE - REACH
    line = size.line
    even, top, _ = place()

    def fill(i, carry):
        at = line(i)
        x0_ref[pl.ds(at, base), :] = jnp.zeros((base, ch), F32)
        x0_ref[pl.ds(at + lead, REACH), :] = left_ref[i].astype(F32)
        x0_ref[pl.ds(at + base, cols), :] = x_ref[i].astype(F32)
        x0_ref[pl.ds(at + base + cols, 16), :] = jnp.zeros((16, ch), F32)
        x0_ref[pl.ds(at + base + cols, REACH), :] = right_ref[i].astype(F32)
        return carry

    lax.fori_loop(0, rows, fill, 0)
    flip_ref[...] = jnp.zeros(flip_ref.shape, F32)
    at = lax.broadcasted_iota(jnp.int32, (wide0, wide0), 0)
    to = lax.broadcasted_iota(jnp.int32, (wide0, wide0), 1)
    mirror = jnp.where(to == jnp.where(top, ext - 1 - at, at), 1.0, 0.0).astype(BF)
    for i in range(REACH):
        south, north = i * pitch, (rows + REACH + i) * pitch
        x0_ref[south : south + pitch, :] = jnp.zeros((pitch, ch), F32)
        x0_ref[south + lead : south + lead + ext, :] = jnp.where(even, b_ref[i].astype(F32), a_ref[i].astype(F32))
        src = jnp.where(top, REACH - 1 - i, i)
        flip_ref[0:ext, :] = jnp.where(even, a_ref[src].astype(F32), b_ref[src].astype(F32))
        turned = jnp.dot(mirror, flip_ref[0:wide0, :].astype(BF), preferred_element_type=F32)
        x0_ref[north : north + pitch, :] = jnp.zeros((pitch, ch), F32)
        x0_ref[north + lead : north + lead + wide0, :] = turned
    relay(size, x0_ref, relaid_ref)
    conv(size, relaid_ref, w_ref, acc_ref)


def conv1_kernel(size, x1_ref, w_ref, acc_ref, relaid_ref):
    relay(size, x1_ref, relaid_ref)
    conv(size, relaid_ref, w_ref, acc_ref)


def gelu_twice(h):
    z = h * h
    p = jnp.full_like(z, ERF_POLY[-1])
    for coef in ERF_POLY[-2::-1]:
        p = p * z + jnp.asarray(coef, z.dtype)
    return h + h * jnp.tanh(h * p)


def norm(b, params, val):
    cbias_ref, gain_ref, nbias_ref = params[:3]
    val = val + cbias_ref[b : b + 1, :]
    cen = val - jnp.mean(val, axis=-1, keepdims=True)
    var = jnp.mean(cen * cen, axis=-1, keepdims=True)
    return (cen * lax.rsqrt(var + 1e-6) * gain_ref[b : b + 1, :] + nbias_ref[b : b + 1, :]).astype(BF)


def mlp(b, params, parts):
    inw_ref, inb_ref, outw_ref, outb_ref, scale_ref = params[3:]
    n = parts[0].shape[0]
    normed = jnp.concatenate([norm(b, params, part) for part in parts], axis=0)
    tile = 48 if n % 48 == 0 else 64
    branch = None
    half_hid = inw_ref.shape[2] // 2
    for c in range(0, 2 * half_hid, half_hid):
        hid = jnp.dot(normed, inw_ref[b, :, c : c + half_hid], preferred_element_type=F32)
        bias = inb_ref[b : b + 1, c : c + half_hid]
        act = [gelu_twice((hid[i : i + tile] + bias).astype(BF)) for i in range(0, hid.shape[0], tile)]
        part = jnp.dot(jnp.concatenate(act, axis=0), outw_ref[b, c : c + half_hid, :], preferred_element_type=F32)
        branch = part if branch is None else branch + part
    scale = scale_ref[b : b + 1, :]
    branch = branch * (0.5 * scale) + outb_ref[b : b + 1, :] * scale
    return [branch[i * n : (i + 1) * n] for i in range(len(parts))]

def rounded(val):
    return val.astype(BF).astype(F32)


def rounded(val):
    return val.astype(BF).astype(F32)


def inner(size, b, params, acc_ref, src_ref, dst_ref):
    rows, octets, groups, ch = size.rows, size.octets, size.groups, size.ch
    step = next(d for d in (8, 6, 4, 3, 2, 1) if rows % d == 0)
    n = step * octets

    def one(t, carry):
        for half in range(2):
            parts = [
                acc_ref[gr, pl.ds(pl.multiple_of(t * n, 16), n), half * ch : (half + 1) * ch] for gr in range(groups)
            ]
            for j, branch in enumerate(mlp(b, params, regroup(parts, size.width))):
                for i in range(step):
                    at = size.line(t * step + i) + BASE + half * groups + j
                    spot = pl.ds(at, octets, stride=OUTS)
                    dst_ref[spot, :] = rounded(src_ref[spot, :] + branch[i * octets : (i + 1) * octets])
        return carry

    lax.fori_loop(0, rows // step, one, 0)


def mlp0_kernel(size, acc_ref, x0_ref, k_ref, *refs):
    params, (x1_ref, strip_ref) = refs[:8], refs[8:]
    rows, cols, ch, pitch, wide0 = size.rows, size.cols, size.ch, size.pitch, size.wide0
    base, lead, near = BASE, BASE - REACH, BASE - HALO
    _, top, bottom = place()

    def clear(i, carry):
        at = size.line(i)
        x1_ref[pl.ds(at, base), :] = jnp.zeros((base, ch), F32)
        x1_ref[pl.ds(at + base + cols, 16), :] = jnp.zeros((16, ch), F32)
        return carry

    lax.fori_loop(0, rows, clear, 0)
    inner(size, 0, params, acc_ref, x0_ref, x1_ref)
    for side in range(2):
        first = lead if side == 0 else base + cols - HALO
        sums = [jnp.zeros((rows, ch), F32) for _ in range(HALO)]
        for r in range(TAPS):
            for c in range(TAPS + HALO - 1):
                cells = x0_ref[pl.ds((REACH - HALO + r) * pitch + first + c, rows, stride=pitch), :]
                for i in range(HALO):
                    if 0 <= c - i < TAPS:
                        tap = TAPS * r + c - i
                        sums[i] = sums[i] + cells * k_ref[0, tap : tap + 1, :]
        start = near if side == 0 else base + cols
        for i, branch in enumerate(mlp(0, params, sums)):
            spot = pl.ds(REACH * pitch + start + i, rows, stride=pitch)
            x1_ref[spot, :] = rounded(x0_ref[spot, :] + branch)
    piece = wide0 // 3
    for side in range(2):
        first = (0 if side == 0 else rows + HALO) * pitch
        for c in range(0, wide0, piece):
            sums = [jnp.zeros((piece, ch), F32) for _ in range(HALO)]
            for s in range(TAPS):
                at = first + lead + s + c
                lines = [x0_ref[at + i * pitch : at + i * pitch + piece, :] for i in range(TAPS + HALO - 1)]
                for r in range(TAPS):
                    tap = TAPS * r + s
                    if side == 1:
                        tap = jnp.where(top, TAPS * TAPS - 1 - tap, tap)
                    weight = k_ref[0, pl.ds(tap, 1), :]
                    for i in range(HALO):
                        sums[i] = sums[i] + lines[i + r] * weight
            for i in range(HALO):
                strip_ref[side * HALO + i, c : c + piece, :] = sums[i]
    for side in range(2):
        branches = mlp(0, params, [strip_ref[side * HALO + i] for i in range(HALO)])
        for i, branch in enumerate(branches):
            row = i - HALO if side == 0 else rows + i
            at = (row + REACH) * pitch + near
            new = rounded(x0_ref[at : at + wide0, :] + branch)
            if side == 0:
                new = jnp.where(bottom, 0.0, new)
            x1_ref[at : at + wide0, :] = new


def mlp1_kernel(size, acc_ref, x1_ref, mask_ref, *refs):
    params, (out_ref, x2_ref) = refs[:8], refs[8:]
    inner(size, 1, params, acc_ref, x1_ref, x2_ref)

    def finish(i, carry):
        out_ref[i] = x2_ref[pl.ds(size.line(i) + BASE, size.cols), :].astype(BF) * mask_ref[i]
        return carry

    lax.fori_loop(0, size.rows, finish, 0)


def shards(
    fields,
    wet_mask,
    conv_kernel,
    conv_bias,
    norm_gain,
    norm_bias,
    in_weight,
    in_bias,
    out_weight,
    out_bias,
    layer_scale,
):
    rows, cols, ch = fields.shape
    left, right, got_a, got_b = exchange(fields, wet_mask)
    mask = jnp.broadcast_to(wet_mask.astype(BF)[:, :, None], fields.shape)
    state = fields * mask
    taps = tap_matrices(conv_kernel)
    groups, depth, lanes = taps.shape[1:]
    hid = in_weight.shape[2]
    size = Sizes(rows, cols, ch)
    cells = rows * cols
    vmem = pl.BlockSpec(memory_space=pltpu.VMEM)
    relaid = pltpu.VMEM((groups, 4, (rows + 2 * HALO) * size.octets, ch), BF)
    padded = jax.ShapeDtypeStruct((size.lines, ch), F32)
    sums = jax.ShapeDtypeStruct((groups, rows * size.octets, lanes), F32)

    def call(kernel, ins, out_shape, scratch, flops):
        def spec(value):
            if value is not taps:
                return vmem
            block = 0 if kernel is conv0_kernel else 1
            return pl.BlockSpec((1, groups, depth, lanes), lambda i: (block, 0, 0, 0))

        several = isinstance(out_shape, tuple)
        return pl.pallas_call(
            functools.partial(kernel, size),
            grid=(1,),
            in_specs=[spec(value) for value in ins],
            out_specs=(vmem,) * len(out_shape) if several else vmem,
            out_shape=out_shape,
            scratch_shapes=scratch,
            compiler_params=pltpu.CompilerParams(vmem_limit_bytes=VMEM_LIMIT),
            cost_estimate=pl.CostEstimate(flops=flops, bytes_accessed=6 * cells * ch, transcendentals=cells * hid),
            name=kernel.__name__,
        )(*ins)

    conv_flops = 2 * cells * ch * depth // OUTS * 2
    mlp_flops = 4 * cells * ch * hid
    params = (conv_bias, norm_gain, norm_bias, in_weight, in_bias, out_weight, out_bias, layer_scale)
    x0, acc = call(
        conv0_kernel,
        (state, left, right, got_a, got_b, taps),
        (padded, sums),
        [relaid, pltpu.VMEM((cols + 24, ch), F32)],
        conv_flops,
    )
    strips = pltpu.VMEM((2 * HALO, cols + 16, ch), F32)
    x1 = call(mlp0_kernel, (acc, x0, conv_kernel) + params, padded, [strips], mlp_flops)
    acc = call(conv1_kernel, (x1, taps), sums, [relaid], conv_flops)
    whole = pltpu.VMEM((size.lines, ch), F32)
    return call(mlp1_kernel, (acc, x1, mask) + params, jax.ShapeDtypeStruct(fields.shape, BF), [whole], mlp_flops)


def solution(mesh):
    return jax.shard_map(
        shards,
        mesh=mesh,
        in_specs=(P("lat", "lon", None), P("lat", "lon")) + (P(),) * 9,
        out_specs=P("lat", "lon", None),
        check_vma=False,
    )
```

```python
import functools

import jax
import jax.numpy as jnp
from jax import lax
from jax.experimental import pallas as pl
from jax.experimental.pallas import tpu as pltpu
from jax.sharding import PartitionSpec as P

BF = jnp.bfloat16
F32 = jnp.float32
TAPS = 7
HALO = 3
REACH = 2 * HALO
OUTS = 8
BASE = 8
VMEM_LIMIT = 16 * 1024 * 1024
ERF_POLY = (0.7975078797359708, 0.03700565107996738, -0.0003515176683895368)


def partners(nlat, nlon, parity):
    route = []
    for lat in range(nlat):
        for lon in range(nlon):
            here = lat * nlon + lon
            if lat % 2 == parity:
                there = here + nlon if lat + 1 < nlat else lat * nlon + nlon - 1 - lon
            elif lat > 0:
                there = here - nlon
            else:
                continue
            route.append((here, there))
    return route


def exchange(fields, wet_mask):
    nlat, nlon = lax.axis_size("lat"), lax.axis_size("lon")
    lat = lax.axis_index("lat")
    rows, cols = wet_mask.shape

    def edge(r0, r1, c0, c1):
        return fields[r0:r1, c0:c1] * wet_mask[r0:r1, c0:c1].astype(BF)[:, :, None]

    up = [(i, (i + 1) % nlon) for i in range(nlon)]
    down = [(j, i) for i, j in up]
    left = lax.ppermute(edge(0, rows, cols - REACH, cols), "lon", up)
    right = lax.ppermute(edge(0, rows, 0, REACH), "lon", down)
    first = jnp.concatenate([left[:REACH], edge(0, REACH, 0, cols), right[:REACH]], axis=1)
    last = jnp.concatenate([left[rows - REACH :], edge(rows - REACH, rows, 0, cols), right[rows - REACH :]], axis=1)
    even = lat % 2 == 0
    got_a = lax.ppermute(jnp.where(even, last, first), ("lat", "lon"), partners(nlat, nlon, 0))
    got_b = lax.ppermute(jnp.where(even, first, last), ("lat", "lon"), partners(nlat, nlon, 1))
    return left, right, got_a, got_b


def regroup(parts, width):
    parts = list(parts)
    ch = parts[0].shape[-1]
    block = lax.broadcasted_iota(jnp.int32, parts[0].shape, parts[0].ndim - 1) // width
    step = 1
    while step < len(parts):
        low = (block & step) == 0
        for i in range(len(parts)):
            if not i & step:
                x, y = parts[i], parts[i + step]
                parts[i] = jnp.where(low, x, pltpu.roll(y, step * width, x.ndim - 1))
                parts[i + step] = jnp.where(low, pltpu.roll(x, ch - step * width, x.ndim - 1), y)
        step *= 2
    return parts


def tap_kernel(k_ref, w_ref, kv_ref):
    ch = k_ref.shape[2]
    lanes = w_ref.shape[3]
    width = lanes // OUTS
    groups = ch // width
    gr = pl.program_id(1)

    @pl.when(gr == 0)
    def _():
        down = [k_ref[0, pl.ds(s, TAPS, stride=TAPS), :] for s in range(TAPS - 1, -1, -1)]
        down.append(jnp.zeros((TAPS, ch), F32))
        halves = [regroup(down[i : i + groups], width) for i in range(0, OUTS, groups)]
        out_col = lax.broadcasted_iota(jnp.int32, (TAPS, lanes), 1) // width
        for g in range(groups):
            line = jnp.concatenate([half[g] for half in halves], axis=1)
            for p in range(2 * OUTS):
                turned = pltpu.roll(line, (p - TAPS + 1) * width % lanes, 1)
                seen = (out_col <= p) & (out_col >= p - TAPS + 1)
                kv_ref[g, p, 0:TAPS, :] = jnp.where(seen, turned, 0.0)

    lane = lax.broadcasted_iota(jnp.int32, (width, lanes), 1)
    own = (lane % width) == lax.broadcasted_iota(jnp.int32, (width, lanes), 0)
    for r in range(TAPS):
        for p in range(2 * OUTS):
            vec = kv_ref[gr, p, r : r + 1, :]
            at = (r * 2 * OUTS + p) * width
            w_ref[0, 0, at : at + width, :] = jnp.where(own, vec, 0.0).astype(BF)


def tap_matrices(conv_kernel):
    blocks, taps, ch = conv_kernel.shape
    lanes = 2 * ch
    width = lanes // OUTS
    groups = ch // width
    depth = TAPS * 2 * OUTS * width
    return pl.pallas_call(
        tap_kernel,
        grid=(blocks, groups),
        in_specs=[pl.BlockSpec((1, taps, ch), lambda b, g: (b, 0, 0))],
        out_specs=pl.BlockSpec((1, 1, depth, lanes), lambda b, g: (b, g, 0, 0)),
        out_shape=jax.ShapeDtypeStruct((blocks, groups, depth, lanes), BF),
        scratch_shapes=[pltpu.VMEM((groups, 2 * OUTS, 8, lanes), F32)],
        compiler_params=pltpu.CompilerParams(vmem_limit_bytes=24 * 1024 * 1024),
        cost_estimate=pl.CostEstimate(
            flops=0, bytes_accessed=2 * blocks * groups * depth * lanes, transcendentals=0
        ),
        name="tap_matrices",
    )(conv_kernel)


class Sizes:
    def __init__(self, rows, cols, ch):
        self.rows, self.cols, self.ch = rows, cols, ch
        self.width = 2 * ch // OUTS
        self.groups = ch // self.width
        self.octets = cols // OUTS
        self.each = self.octets + 8
        self.pitch = OUTS * self.each
        self.lines = (rows + 2 * REACH) * self.pitch + 8
        self.wide0 = cols + 16
        self.plain = cols + 24

    def spot(self, row, o):
        return pl.multiple_of((row + REACH) * self.pitch, 8) + o * self.each + 8


def ordering(size, undo=False):
    shape = (size.cols, size.cols)
    by_octet = lax.broadcasted_iota(jnp.int32, shape, 1 if undo else 0)
    plain = lax.broadcasted_iota(jnp.int32, shape, 0 if undo else 1)
    same = plain == by_octet % size.octets * OUTS + by_octet // size.octets
    return jnp.where(same, 1.0, 0.0).astype(BF)


def put_row(size, dst_ref, row, val):
    for o in range(OUTS):
        dst_ref[pl.ds(size.spot(row, o), size.octets), :] = val[o * size.octets : (o + 1) * size.octets]


def put_ends(size, dst_ref, row, before, after):
    n = before.shape[0]
    dst_ref[pl.ds(size.spot(row, OUTS - n) - 1, n, stride=size.each), :] = before
    dst_ref[pl.ds(size.spot(row, 0) + size.octets, n, stride=size.each), :] = after


def place():
    lat = lax.axis_index("lat")
    return lat % 2 == 0, lat == lax.axis_size("lat") - 1, lat == 0


def relay(size, src_ref, relaid_ref):
    blank = jnp.zeros((size.octets, size.ch), BF)

    def one(i, carry):
        for a in range(4):
            parts = []
            for col in range(4 * a - HALO, 4 * a - HALO + 4):
                if col < OUTS + HALO:
                    at = size.spot(i - HALO, col % OUTS) + col // OUTS
                    parts.append(src_ref[pl.ds(at, size.octets), :].astype(BF))
                else:
                    parts.append(blank)
            for gr, part in enumerate(regroup(parts, size.width)):
                relaid_ref[gr, a, pl.ds(pl.multiple_of(i * size.octets, 16), size.octets), :] = part
        return carry

    lax.fori_loop(0, size.rows + 2 * HALO, one, 0)


def conv(size, relaid_ref, w_ref, acc_ref):
    octets, rows = size.octets, size.rows

    for gr in range(size.groups):
        parts = []
        for r in range(TAPS):
            for a in range(4):
                parts.append(relaid_ref[gr, a, r * octets : (r + rows) * octets, :])
        acc_ref[gr] = jnp.dot(jnp.concatenate(parts, axis=1), w_ref[0, gr], preferred_element_type=F32)


def conv0_kernel(size, x_ref, left_ref, right_ref, a_ref, b_ref, w_ref, x0_ref, edge_ref, acc_ref, relaid_ref, flip_ref):
    rows, cols, ch, wide0 = size.rows, size.cols, size.ch, size.wide0
    ext, lead = cols + 2 * REACH, BASE - REACH
    even, top, _ = place()
    order = ordering(size)

    def fill(i, carry):
        both = jnp.concatenate([x_ref[2 * i], x_ref[2 * i + 1]], axis=1)
        both = jnp.dot(order, both, preferred_element_type=F32)
        for h in range(2):
            put_row(size, x0_ref, 2 * i + h, both[:, h * ch : (h + 1) * ch])
            put_ends(size, x0_ref, 2 * i + h, left_ref[2 * i + h].astype(F32), right_ref[2 * i + h].astype(F32))
        return carry

    lax.fori_loop(0, rows // 2, fill, 0)

    edge_ref[...] = jnp.zeros(edge_ref.shape, F32)
    flip_ref[...] = jnp.zeros(flip_ref.shape, F32)
    at = lax.broadcasted_iota(jnp.int32, (wide0, wide0), 0)
    to = lax.broadcasted_iota(jnp.int32, (wide0, wide0), 1)
    mirror = jnp.where(to == jnp.where(top, ext - 1 - at, at), 1.0, 0.0).astype(BF)
    for i in range(REACH):
        edge_ref[0, i, lead : lead + ext, :] = jnp.where(even, b_ref[i].astype(F32), a_ref[i].astype(F32))
        src = jnp.where(top, REACH - 1 - i, i)
        flip_ref[0:ext, :] = jnp.where(even, a_ref[src].astype(F32), b_ref[src].astype(F32))
        turned = jnp.dot(mirror, flip_ref[0:wide0, :].astype(BF), preferred_element_type=F32)
        edge_ref[1, HALO + i, lead : lead + wide0, :] = turned
    for i in range(HALO):
        for side, slot, row in ((0, REACH + i, i), (1, i, rows - HALO + i)):
            edge_ref[side, slot, lead:BASE, :] = left_ref[row].astype(F32)
            edge_ref[side, slot, BASE : BASE + cols, :] = x_ref[row].astype(F32)
            edge_ref[side, slot, BASE + cols : BASE + cols + REACH, :] = right_ref[row].astype(F32)
    for i in range(HALO):
        lines = [edge_ref[0, HALO + i], edge_ref[1, HALO + i]]
        both = jnp.concatenate([line[BASE : BASE + cols].astype(BF) for line in lines], axis=1)
        both = jnp.dot(order, both, preferred_element_type=F32)
        for side, row in ((0, i - HALO), (1, rows + i)):
            put_row(size, x0_ref, row, both[:, side * ch : (side + 1) * ch])
            put_ends(
                size,
                x0_ref,
                row,
                edge_ref[side, HALO + i, lead:BASE, :],
                edge_ref[side, HALO + i, BASE + cols : BASE + cols + REACH, :],
            )
    relay(size, x0_ref, relaid_ref)
    conv(size, relaid_ref, w_ref, acc_ref)


def conv1_kernel(size, x1_ref, w_ref, acc_ref, relaid_ref):
    relay(size, x1_ref, relaid_ref)
    conv(size, relaid_ref, w_ref, acc_ref)


def gelu_twice(h):
    z = h * h
    p = jnp.full_like(z, ERF_POLY[-1])
    for coef in ERF_POLY[-2::-1]:
        p = p * z + jnp.asarray(coef, z.dtype)
    return h + h * jnp.tanh(h * p)


def norm(b, params, val):
    cbias_ref, gain_ref, nbias_ref = params[:3]
    val = val + cbias_ref[b : b + 1, :]
    share = 1.0 / val.shape[-1]
    cen = val - jnp.sum(val, axis=-1, keepdims=True) * share
    var = jnp.sum(cen * cen, axis=-1, keepdims=True) * share
    return (cen * lax.rsqrt(var + 1e-6) * gain_ref[b : b + 1, :] + nbias_ref[b : b + 1, :]).astype(BF)


def mlp(b, params, parts):
    inw_ref, inb_ref, outw_ref, outb_ref, scale_ref = params[3:]
    n = parts[0].shape[0]
    normed = jnp.concatenate([norm(b, params, part) for part in parts], axis=0)
    tile = 48 if n % 48 == 0 else 64
    branch = None
    half_hid = inw_ref.shape[2] // 2
    for c in range(0, 2 * half_hid, half_hid):
        hid = jnp.dot(normed, inw_ref[b, :, c : c + half_hid], preferred_element_type=F32)
        bias = inb_ref[b : b + 1, c : c + half_hid]
        act = [gelu_twice((hid[i : i + tile] + bias).astype(BF)) for i in range(0, hid.shape[0], tile)]
        part = jnp.dot(jnp.concatenate(act, axis=0), outw_ref[b, c : c + half_hid, :], preferred_element_type=F32)
        branch = part if branch is None else branch + part
    scale = scale_ref[b : b + 1, :]
    branch = branch * (0.5 * scale) + outb_ref[b : b + 1, :] * scale
    return [branch[i * n : (i + 1) * n] for i in range(len(parts))]

def rounded(val):
    return val.astype(BF).astype(F32)


def rounded(val):
    return val.astype(BF).astype(F32)


def inner(size, b, params, acc_ref, src_ref, keep):
    rows, octets, groups, ch = size.rows, size.octets, size.groups, size.ch
    step = next(d for d in (8, 6, 4, 3, 2, 1) if rows % d == 0)
    n = step * octets

    def one(t, carry):
        for half in range(2):
            parts = [
                acc_ref[gr, pl.ds(pl.multiple_of(t * n, 16), n), half * ch : (half + 1) * ch] for gr in range(groups)
            ]
            for j, branch in enumerate(mlp(b, params, regroup(parts, size.width))):
                for i in range(step):
                    row, o = t * step + i, half * groups + j
                    old = src_ref[pl.ds(size.spot(row, o), octets), :]
                    keep(row, o, old + branch[i * octets : (i + 1) * octets])
        return carry

    lax.fori_loop(0, rows // step, one, 0)


def mlp0_kernel(size, acc_ref, x0_ref, edge_ref, k_ref, *refs):
    params, (x1_ref, strip_ref, side_ref) = refs[:8], refs[8:]
    rows, cols, ch, wide0, octets = size.rows, size.cols, size.ch, size.wide0, size.octets
    lead, near = BASE - REACH, BASE - HALO
    _, top, bottom = place()

    def keep(row, o, new):
        x1_ref[pl.ds(size.spot(row, o), octets), :] = rounded(new)

    inner(size, 0, params, acc_ref, x0_ref, keep)

    def column(col, first, count):
        return pl.ds(size.spot(first, col % OUTS) + col // OUTS, count, stride=size.pitch)

    for start in (-HALO, cols):
        for c in range(TAPS + HALO - 1):
            side_ref[c, 0 : rows + 2 * HALO, :] = x0_ref[column(start - HALO + c, -HALO, rows + 2 * HALO), :]
        sums = [jnp.zeros((rows, ch), F32) for _ in range(HALO)]
        for r in range(TAPS):
            for c in range(TAPS + HALO - 1):
                cells = side_ref[c, r : r + rows, :]
                for i in range(HALO):
                    if 0 <= c - i < TAPS:
                        tap = TAPS * r + c - i
                        sums[i] = sums[i] + cells * k_ref[0, tap : tap + 1, :]
        for i, branch in enumerate(mlp(0, params, sums)):
            at = column(start + i, 0, rows)
            x1_ref[at, :] = rounded(x0_ref[at, :] + branch)

    piece = wide0 // 3
    for side in range(2):
        for c in range(0, wide0, piece):
            sums = [jnp.zeros((piece, ch), F32) for _ in range(HALO)]
            for s in range(TAPS):
                at = lead + s + c
                lines = [edge_ref[side, i, at : at + piece, :] for i in range(TAPS + HALO - 1)]
                for r in range(TAPS):
                    tap = TAPS * r + s
                    if side == 1:
                        tap = jnp.where(top, TAPS * TAPS - 1 - tap, tap)
                    weight = k_ref[0, pl.ds(tap, 1), :]
                    for i in range(HALO):
                        sums[i] = sums[i] + lines[i + r] * weight
            for i in range(HALO):
                strip_ref[side, i, c : c + piece, :] = sums[i]
    for side in range(2):
        branches = mlp(0, params, [strip_ref[side, i] for i in range(HALO)])
        for i, branch in enumerate(branches):
            new = rounded(edge_ref[side, HALO + i, near : near + wide0, :] + branch)
            if side == 0:
                new = jnp.where(bottom, 0.0, new)
            strip_ref[side, i] = new
    order = ordering(size)
    for i in range(HALO):
        both = jnp.concatenate([strip_ref[side, i, HALO : HALO + cols, :].astype(BF) for side in range(2)], axis=1)
        both = jnp.dot(order, both, preferred_element_type=F32)
        for side, row in ((0, i - HALO), (1, rows + i)):
            put_row(size, x1_ref, row, both[:, side * ch : (side + 1) * ch])
            put_ends(
                size,
                x1_ref,
                row,
                strip_ref[side, i, 0:HALO, :],
                strip_ref[side, i, HALO + cols : 2 * HALO + cols, :],
            )


def mlp1_kernel(size, acc_ref, x1_ref, mask_ref, *refs):
    params, (out_ref, x2_ref) = refs[:8], refs[8:]
    ch, octets = size.ch, size.octets

    def keep(row, o, new):
        x2_ref[row, o * octets : (o + 1) * octets, :] = new.astype(BF)

    inner(size, 1, params, acc_ref, x1_ref, keep)
    back = ordering(size, undo=True)

    def finish(i, carry):
        both = jnp.concatenate([x2_ref[2 * i], x2_ref[2 * i + 1]], axis=1)
        both = jnp.dot(back, both, preferred_element_type=F32).astype(BF)
        for h in range(2):
            out_ref[2 * i + h] = both[:, h * ch : (h + 1) * ch] * mask_ref[2 * i + h]
        return carry

    lax.fori_loop(0, size.rows // 2, finish, 0)


def shards(
    fields,
    wet_mask,
    conv_kernel,
    conv_bias,
    norm_gain,
    norm_bias,
    in_weight,
    in_bias,
    out_weight,
    out_bias,
    layer_scale,
):
    rows, cols, ch = fields.shape
    left, right, got_a, got_b = exchange(fields, wet_mask)
    mask = jnp.broadcast_to(wet_mask.astype(BF)[:, :, None], fields.shape)
    state = fields * mask
    taps = tap_matrices(conv_kernel)
    groups, depth, lanes = taps.shape[1:]
    hid = in_weight.shape[2]
    size = Sizes(rows, cols, ch)
    cells = rows * cols
    vmem = pl.BlockSpec(memory_space=pltpu.VMEM)
    relaid = pltpu.VMEM((groups, 4, (rows + 2 * HALO) * size.octets, ch), BF)
    padded = jax.ShapeDtypeStruct((size.lines, ch), F32)
    sums = jax.ShapeDtypeStruct((groups, rows * size.octets, lanes), F32)

    def call(kernel, ins, out_shape, scratch, flops):
        def spec(value):
            if value is not taps:
                return vmem
            block = 0 if kernel is conv0_kernel else 1
            return pl.BlockSpec((1, groups, depth, lanes), lambda i: (block, 0, 0, 0))

        several = isinstance(out_shape, tuple)
        return pl.pallas_call(
            functools.partial(kernel, size),
            grid=(1,),
            in_specs=[spec(value) for value in ins],
            out_specs=(vmem,) * len(out_shape) if several else vmem,
            out_shape=out_shape,
            scratch_shapes=scratch,
            compiler_params=pltpu.CompilerParams(vmem_limit_bytes=VMEM_LIMIT),
            cost_estimate=pl.CostEstimate(flops=flops, bytes_accessed=6 * cells * ch, transcendentals=cells * hid),
            name=kernel.__name__,
        )(*ins)

    conv_flops = 2 * cells * ch * depth // OUTS * 2
    mlp_flops = 4 * cells * ch * hid
    params = (conv_bias, norm_gain, norm_bias, in_weight, in_bias, out_weight, out_bias, layer_scale)
    edges = jax.ShapeDtypeStruct((2, TAPS + HALO - 1, size.plain, ch), F32)
    x0, edge, acc = call(
        conv0_kernel,
        (state, left, right, got_a, got_b, taps),
        (padded, edges, sums),
        [relaid, pltpu.VMEM((size.plain, ch), F32)],
        conv_flops,
    )
    strips = pltpu.VMEM((2, HALO, size.wide0, ch), F32)
    sides = pltpu.VMEM((TAPS + HALO - 1, rows + 8, ch), F32)
    x1 = call(mlp0_kernel, (acc, x0, edge, conv_kernel) + params, padded, [strips, sides], mlp_flops)
    acc = call(conv1_kernel, (x1, taps), sums, [relaid], conv_flops)
    last = pltpu.VMEM(fields.shape, BF)
    return call(mlp1_kernel, (acc, x1, mask) + params, jax.ShapeDtypeStruct(fields.shape, BF), [last], mlp_flops)


def solution(mesh):
    return jax.shard_map(
        shards,
        mesh=mesh,
        in_specs=(P("lat", "lon", None), P("lat", "lon")) + (P(),) * 9,
        out_specs=P("lat", "lon", None),
        check_vma=False,
    )
```

```python
import functools

import jax
import jax.numpy as jnp
from jax import lax
from jax.experimental import pallas as pl
from jax.experimental.pallas import tpu as pltpu
from jax.sharding import PartitionSpec as P

BF = jnp.bfloat16
F32 = jnp.float32
TAPS = 7
HALO = 3
REACH = 2 * HALO
OUTS = 8
BASE = 8
VMEM_LIMIT = 16 * 1024 * 1024
ERF_POLY = (0.7975078797359708, 0.03700565107996738, -0.0003515176683895368)


def partners(nlat, nlon, parity):
    route = []
    for lat in range(nlat):
        for lon in range(nlon):
            here = lat * nlon + lon
            if lat % 2 == parity:
                there = here + nlon if lat + 1 < nlat else lat * nlon + nlon - 1 - lon
            elif lat > 0:
                there = here - nlon
            else:
                continue
            route.append((here, there))
    return route


def exchange(fields, wet_mask):
    nlat, nlon = lax.axis_size("lat"), lax.axis_size("lon")
    lat = lax.axis_index("lat")
    rows, cols = wet_mask.shape

    def edge(r0, r1, c0, c1):
        return fields[r0:r1, c0:c1] * wet_mask[r0:r1, c0:c1].astype(BF)[:, :, None]

    up = [(i, (i + 1) % nlon) for i in range(nlon)]
    down = [(j, i) for i, j in up]
    left = lax.ppermute(edge(0, rows, cols - REACH, cols), "lon", up)
    right = lax.ppermute(edge(0, rows, 0, REACH), "lon", down)
    first = jnp.concatenate([left[:REACH], edge(0, REACH, 0, cols), right[:REACH]], axis=1)
    last = jnp.concatenate([left[rows - REACH :], edge(rows - REACH, rows, 0, cols), right[rows - REACH :]], axis=1)
    even = lat % 2 == 0
    got_a = lax.ppermute(jnp.where(even, last, first), ("lat", "lon"), partners(nlat, nlon, 0))
    got_b = lax.ppermute(jnp.where(even, first, last), ("lat", "lon"), partners(nlat, nlon, 1))
    return left, right, got_a, got_b


def regroup(parts, width):
    parts = list(parts)
    ch = parts[0].shape[-1]
    block = lax.broadcasted_iota(jnp.int32, parts[0].shape, parts[0].ndim - 1) // width
    step = 1
    while step < len(parts):
        low = (block & step) == 0
        for i in range(len(parts)):
            if not i & step:
                x, y = parts[i], parts[i + step]
                parts[i] = jnp.where(low, x, pltpu.roll(y, step * width, x.ndim - 1))
                parts[i + step] = jnp.where(low, pltpu.roll(x, ch - step * width, x.ndim - 1), y)
        step *= 2
    return parts


def tap_kernel(k_ref, inw_ref, cbias_ref, gain_ref, nbias_ref, w_ref, spread_ref, lines_ref, kv_ref):
    ch = k_ref.shape[2]
    lanes = w_ref.shape[3]
    width = lanes // OUTS
    groups = ch // width
    gr = pl.program_id(1)

    @pl.when(gr == 0)
    def _():
        block = lax.broadcasted_iota(jnp.int32, (1, ch), 1) // width
        for n, ref in enumerate((cbias_ref, gain_ref, nbias_ref)):
            for g in range(groups):
                line = jnp.zeros((1, ch), F32)
                for j in range(groups):
                    line = jnp.where(block == j, pltpu.roll(ref[0], (j - g) * width % ch, 1), line)
                lines_ref[0, n * groups + g : n * groups + g + 1, :] = line
        down = [k_ref[0, pl.ds(s, TAPS, stride=TAPS), :] for s in range(TAPS - 1, -1, -1)]
        down.append(jnp.zeros((TAPS, ch), F32))
        halves = [regroup(down[i : i + groups], width) for i in range(0, OUTS, groups)]
        out_col = lax.broadcasted_iota(jnp.int32, (TAPS, lanes), 1) // width
        for g in range(groups):
            line = jnp.concatenate([half[g] for half in halves], axis=1)
            for p in range(2 * OUTS):
                turned = pltpu.roll(line, (p - TAPS + 1) * width % lanes, 1)
                seen = (out_col <= p) & (out_col >= p - TAPS + 1)
                kv_ref[g, p, 0:TAPS, :] = jnp.where(seen, turned, 0.0)

    lane = lax.broadcasted_iota(jnp.int32, (width, lanes), 1)
    own = (lane % width) == lax.broadcasted_iota(jnp.int32, (width, lanes), 0)
    for r in range(TAPS):
        for p in range(2 * OUTS):
            vec = kv_ref[gr, p, r : r + 1, :]
            at = (r * 2 * OUTS + p) * width
            w_ref[0, 0, at : at + width, :] = jnp.where(own, vec, 0.0).astype(BF)
    mine = inw_ref[0]
    for o in range(groups):
        for j in range(groups):
            spread_ref[0, o, j * width : (j + 1) * width, :] = mine if j == o else jnp.zeros_like(mine)


def tap_matrices(conv_kernel, in_weight, conv_bias, norm_gain, norm_bias):
    blocks, taps, ch = conv_kernel.shape
    hid = in_weight.shape[2]
    lanes = 2 * ch
    width = lanes // OUTS
    groups = ch // width
    depth = TAPS * 2 * OUTS * width
    return pl.pallas_call(
        tap_kernel,
        grid=(blocks, groups),
        in_specs=[
            pl.BlockSpec((1, taps, ch), lambda b, g: (b, 0, 0)),
            pl.BlockSpec((1, width, hid), lambda b, g: (b, g, 0)),
        ]
        + [pl.BlockSpec((1, 1, ch), lambda b, g: (b, 0, 0))] * 3,
        out_specs=(
            pl.BlockSpec((1, 1, depth, lanes), lambda b, g: (b, g, 0, 0)),
            pl.BlockSpec((1, groups, ch, hid), lambda b, g: (b, 0, g, 0)),
            pl.BlockSpec((1, 3 * groups, ch), lambda b, g: (b, 0, 0)),
        ),
        out_shape=(
            jax.ShapeDtypeStruct((blocks, groups, depth, lanes), BF),
            jax.ShapeDtypeStruct((blocks, groups, groups * ch, hid), BF),
            jax.ShapeDtypeStruct((blocks, 3 * groups, ch), F32),
        ),
        scratch_shapes=[pltpu.VMEM((groups, 2 * OUTS, 8, lanes), F32)],
        compiler_params=pltpu.CompilerParams(vmem_limit_bytes=24 * 1024 * 1024),
        cost_estimate=pl.CostEstimate(
            flops=0, bytes_accessed=2 * blocks * groups * depth * lanes, transcendentals=0
        ),
        name="tap_matrices",
    )(conv_kernel, in_weight, conv_bias[:, None], norm_gain[:, None], norm_bias[:, None])


class Sizes:
    def __init__(self, rows, cols, ch):
        self.rows, self.cols, self.ch = rows, cols, ch
        self.width = 2 * ch // OUTS
        self.groups = ch // self.width
        self.octets = cols // OUTS
        self.pitch = cols + 24
        self.lines = (rows + 2 * REACH) * self.pitch
        self.wide0 = cols + 16

    def line(self, row):
        return pl.multiple_of((row + REACH) * self.pitch, 8)


def place():
    lat = lax.axis_index("lat")
    return lat % 2 == 0, lat == lax.axis_size("lat") - 1, lat == 0


def relay(size, src_ref, relaid_ref):
    octets, groups, width, ch = size.octets, size.groups, size.width, size.ch
    lines = size.rows + 2 * HALO
    step = next(d for d in (6, 4, 3, 2, 1) if lines % d == 0)
    shape = (groups * ch, groups * ch)
    old = lax.broadcasted_iota(jnp.int32, shape, 0)
    new = lax.broadcasted_iota(jnp.int32, shape, 1)
    order = jnp.where(new == old % ch // width * ch + old // ch * width + old % width, 1.0, 0.0).astype(BF)

    def one(q, carry):
        cells = []
        for a in range(4):
            for i in range(step):
                at = size.line(q * step + i - HALO) + BASE - HALO + 4 * a
                parts = [src_ref[pl.ds(at + j, octets, stride=OUTS), :].astype(BF) for j in range(groups)]
                cells.append(jnp.concatenate(parts, axis=1))
        moved = jnp.dot(jnp.concatenate(cells, axis=0), order, preferred_element_type=F32).astype(BF)
        n = step * octets
        for a in range(4):
            for gr in range(groups):
                relaid_ref[gr, a, pl.ds(pl.multiple_of(q * n, 16), n), :] = moved[
                    a * n : (a + 1) * n, gr * ch : (gr + 1) * ch
                ]
        return carry

    lax.fori_loop(0, lines // step, one, 0)


def conv(size, relaid_ref, w_ref, acc_ref):
    octets, rows = size.octets, size.rows

    for gr in range(size.groups):
        parts = []
        for r in range(TAPS):
            for a in range(4):
                parts.append(relaid_ref[gr, a, r * octets : (r + rows) * octets, :])
        acc_ref[gr] = jnp.dot(jnp.concatenate(parts, axis=1), w_ref[0, gr], preferred_element_type=F32)


def conv0_kernel(size, x_ref, left_ref, right_ref, a_ref, b_ref, w_ref, x0_ref, acc_ref, relaid_ref, flip_ref):
    rows, cols, ch, pitch, wide0 = size.rows, size.cols, size.ch, size.pitch, size.wide0
    base, ext, lead = BASE, cols + 2 * REACH, BASE - REACH
    line = size.line
    even, top, _ = place()

    def fill(i, carry):
        at = line(i)
        x0_ref[pl.ds(at, base), :] = jnp.zeros((base, ch), F32)
        x0_ref[pl.ds(at + lead, REACH), :] = left_ref[i].astype(F32)
        x0_ref[pl.ds(at + base, cols), :] = x_ref[i].astype(F32)
        x0_ref[pl.ds(at + base + cols, 16), :] = jnp.zeros((16, ch), F32)
        x0_ref[pl.ds(at + base + cols, REACH), :] = right_ref[i].astype(F32)
        return carry

    lax.fori_loop(0, rows, fill, 0)
    flip_ref[...] = jnp.zeros(flip_ref.shape, F32)
    at = lax.broadcasted_iota(jnp.int32, (wide0, wide0), 0)
    to = lax.broadcasted_iota(jnp.int32, (wide0, wide0), 1)
    mirror = jnp.where(to == jnp.where(top, ext - 1 - at, at), 1.0, 0.0).astype(BF)
    for i in range(REACH):
        south, north = i * pitch, (rows + REACH + i) * pitch
        x0_ref[south : south + pitch, :] = jnp.zeros((pitch, ch), F32)
        x0_ref[south + lead : south + lead + ext, :] = jnp.where(even, b_ref[i].astype(F32), a_ref[i].astype(F32))
        src = jnp.where(top, REACH - 1 - i, i)
        flip_ref[0:ext, :] = jnp.where(even, a_ref[src].astype(F32), b_ref[src].astype(F32))
        turned = jnp.dot(mirror, flip_ref[0:wide0, :].astype(BF), preferred_element_type=F32)
        x0_ref[north : north + pitch, :] = jnp.zeros((pitch, ch), F32)
        x0_ref[north + lead : north + lead + wide0, :] = turned
    relay(size, x0_ref, relaid_ref)
    conv(size, relaid_ref, w_ref, acc_ref)


def conv1_kernel(size, x1_ref, w_ref, acc_ref, relaid_ref):
    relay(size, x1_ref, relaid_ref)
    conv(size, relaid_ref, w_ref, acc_ref)


def gelu_twice(h):
    z = h * h
    p = jnp.full_like(z, ERF_POLY[-1])
    for coef in ERF_POLY[-2::-1]:
        p = p * z + jnp.asarray(coef, z.dtype)
    return h + h * jnp.tanh(h * p)


def norm(b, params, val):
    cbias_ref, gain_ref, nbias_ref = params[:3]
    val = val + cbias_ref[b : b + 1, :]
    cen = val - jnp.mean(val, axis=-1, keepdims=True)
    var = jnp.mean(cen * cen, axis=-1, keepdims=True)
    return (cen * lax.rsqrt(var + 1e-6) * gain_ref[b : b + 1, :] + nbias_ref[b : b + 1, :]).astype(BF)


def project(b, params, normed, weight_ref, index):
    inb_ref, outw_ref, outb_ref, scale_ref = params[4:8]
    rows = normed.shape[0]
    tile = 48 if rows % 48 == 0 else 64
    branch = None
    half_hid = outw_ref.shape[1] // 2
    for c in range(0, 2 * half_hid, half_hid):
        hid = jnp.dot(normed, weight_ref[index + (slice(None), slice(c, c + half_hid))], preferred_element_type=F32)
        bias = inb_ref[b : b + 1, c : c + half_hid]
        act = [gelu_twice((hid[i : i + tile] + bias).astype(BF)) for i in range(0, rows, tile)]
        part = jnp.dot(jnp.concatenate(act, axis=0), outw_ref[b, c : c + half_hid, :], preferred_element_type=F32)
        branch = part if branch is None else branch + part
    scale = scale_ref[b : b + 1, :]
    return branch * (0.5 * scale) + outb_ref[b : b + 1, :] * scale


def mlp(b, params, parts):
    n = parts[0].shape[0]
    normed = jnp.concatenate([norm(b, params, part) for part in parts], axis=0)
    branch = project(b, params, normed, params[3], (b,))
    return [branch[i * n : (i + 1) * n] for i in range(len(parts))]


def block_sums(size, val):
    ch = size.ch
    row = lax.broadcasted_iota(jnp.int32, (2 * ch, ch), 0) % ch
    col = lax.broadcasted_iota(jnp.int32, (2 * ch, ch), 1)
    ones = jnp.where(row // size.width == col // size.width, 1.0, 0.0).astype(BF)
    high = val.astype(BF)
    low = (val - high.astype(F32)).astype(BF)
    return jnp.dot(jnp.concatenate([high, low], axis=1), ones, preferred_element_type=F32)


def norm_grouped(size, lines_ref, parts):
    groups = size.groups
    share = 1.0 / size.ch

    def line(n, gr):
        return lines_ref[0, n * groups + gr : n * groups + gr + 1, :]

    vals = [part + line(0, gr) for gr, part in enumerate(parts)]
    mean = block_sums(size, sum(vals[1:], vals[0])) * share
    cens = [val - mean for val in vals]
    squares = [cen * cen for cen in cens]
    inv = lax.rsqrt(block_sums(size, sum(squares[1:], squares[0])) * share + 1e-6)
    normed = [(cen * inv * line(1, gr) + line(2, gr)).astype(BF) for gr, cen in enumerate(cens)]
    return jnp.concatenate(normed, axis=1)


def rounded(val):
    return val.astype(BF).astype(F32)


def rounded(val):
    return val.astype(BF).astype(F32)


def inner(size, b, params, acc_ref, src_ref, dst_ref):
    rows, octets, groups, ch = size.rows, size.octets, size.groups, size.ch
    spread_ref, lines_ref = params[8:]
    step = next(d for d in (24, 16, 12, 8, 6, 4, 3, 2, 1) if rows % d == 0)
    n = step * octets

    def one(t, carry):
        for half in range(2):
            parts = [
                acc_ref[gr, pl.ds(pl.multiple_of(t * n, 16), n), half * ch : (half + 1) * ch] for gr in range(groups)
            ]
            normed = norm_grouped(size, lines_ref, parts)
            for j in range(groups):
                branch = project(b, params, normed, spread_ref, (0, j))
                for i in range(step):
                    at = size.line(t * step + i) + BASE + half * groups + j
                    spot = pl.ds(at, octets, stride=OUTS)
                    dst_ref[spot, :] = rounded(src_ref[spot, :] + branch[i * octets : (i + 1) * octets])
        return carry

    lax.fori_loop(0, rows // step, one, 0)


def mlp0_kernel(size, acc_ref, x0_ref, k_ref, *refs):
    params, (x1_ref, strip_ref) = refs[:10], refs[10:]
    rows, cols, ch, pitch, wide0 = size.rows, size.cols, size.ch, size.pitch, size.wide0
    base, lead, near = BASE, BASE - REACH, BASE - HALO
    _, top, bottom = place()

    def clear(i, carry):
        at = size.line(i)
        x1_ref[pl.ds(at, base), :] = jnp.zeros((base, ch), F32)
        x1_ref[pl.ds(at + base + cols, 16), :] = jnp.zeros((16, ch), F32)
        return carry

    lax.fori_loop(0, rows, clear, 0)
    inner(size, 0, params, acc_ref, x0_ref, x1_ref)
    for side in range(2):
        first = lead if side == 0 else base + cols - HALO
        sums = [jnp.zeros((rows, ch), F32) for _ in range(HALO)]
        for r in range(TAPS):
            for c in range(TAPS + HALO - 1):
                cells = x0_ref[pl.ds((REACH - HALO + r) * pitch + first + c, rows, stride=pitch), :]
                for i in range(HALO):
                    if 0 <= c - i < TAPS:
                        tap = TAPS * r + c - i
                        sums[i] = sums[i] + cells * k_ref[0, tap : tap + 1, :]
        start = near if side == 0 else base + cols
        for i, branch in enumerate(mlp(0, params, sums)):
            spot = pl.ds(REACH * pitch + start + i, rows, stride=pitch)
            x1_ref[spot, :] = rounded(x0_ref[spot, :] + branch)
    piece = wide0 // 3
    for side in range(2):
        first = (0 if side == 0 else rows + HALO) * pitch
        for c in range(0, wide0, piece):
            sums = [jnp.zeros((piece, ch), F32) for _ in range(HALO)]
            for s in range(TAPS):
                at = first + lead + s + c
                lines = [x0_ref[at + i * pitch : at + i * pitch + piece, :] for i in range(TAPS + HALO - 1)]
                for r in range(TAPS):
                    tap = TAPS * r + s
                    if side == 1:
                        tap = jnp.where(top, TAPS * TAPS - 1 - tap, tap)
                    weight = k_ref[0, pl.ds(tap, 1), :]
                    for i in range(HALO):
                        sums[i] = sums[i] + lines[i + r] * weight
            for i in range(HALO):
                strip_ref[side * HALO + i, c : c + piece, :] = sums[i]
    for side in range(2):
        branches = mlp(0, params, [strip_ref[side * HALO + i] for i in range(HALO)])
        for i, branch in enumerate(branches):
            row = i - HALO if side == 0 else rows + i
            at = (row + REACH) * pitch + near
            new = rounded(x0_ref[at : at + wide0, :] + branch)
            if side == 0:
                new = jnp.where(bottom, 0.0, new)
            x1_ref[at : at + wide0, :] = new


def mlp1_kernel(size, acc_ref, x1_ref, mask_ref, *refs):
    params, (out_ref, x2_ref) = refs[:10], refs[10:]
    inner(size, 1, params, acc_ref, x1_ref, x2_ref)

    def finish(i, carry):
        out_ref[i] = x2_ref[pl.ds(size.line(i) + BASE, size.cols), :].astype(BF) * mask_ref[i]
        return carry

    lax.fori_loop(0, size.rows, finish, 0)


def shards(
    fields,
    wet_mask,
    conv_kernel,
    conv_bias,
    norm_gain,
    norm_bias,
    in_weight,
    in_bias,
    out_weight,
    out_bias,
    layer_scale,
):
    rows, cols, ch = fields.shape
    left, right, got_a, got_b = exchange(fields, wet_mask)
    mask = jnp.broadcast_to(wet_mask.astype(BF)[:, :, None], fields.shape)
    state = fields * mask
    taps, spread, lines = tap_matrices(conv_kernel, in_weight, conv_bias, norm_gain, norm_bias)
    groups, depth, width = taps.shape[1:]
    hid = in_weight.shape[2]
    size = Sizes(rows, cols, ch)
    cells = rows * cols
    vmem = pl.BlockSpec(memory_space=pltpu.VMEM)
    relaid = pltpu.VMEM((groups, 4, (rows + 2 * HALO) * size.octets, ch), BF)
    padded = jax.ShapeDtypeStruct((size.lines, ch), F32)
    sums = jax.ShapeDtypeStruct((groups, rows * size.octets, width), F32)

    def call(kernel, ins, out_shape, scratch, flops):
        def spec(value):
            if value is not taps and value is not spread and value is not lines:
                return vmem
            block = 0 if kernel in (conv0_kernel, mlp0_kernel) else 1
            return pl.BlockSpec((1,) + value.shape[1:], lambda i: (block,) + (0,) * (value.ndim - 1))

        several = isinstance(out_shape, tuple)
        return pl.pallas_call(
            functools.partial(kernel, size),
            grid=(1,),
            in_specs=[spec(value) for value in ins],
            out_specs=(vmem,) * len(out_shape) if several else vmem,
            out_shape=out_shape,
            scratch_shapes=scratch,
            compiler_params=pltpu.CompilerParams(vmem_limit_bytes=VMEM_LIMIT),
            cost_estimate=pl.CostEstimate(flops=flops, bytes_accessed=6 * cells * ch, transcendentals=cells * hid),
            name=kernel.__name__,
        )(*ins)

    conv_flops = 2 * cells * ch * depth // OUTS * 2
    mlp_flops = 4 * cells * ch * hid
    params = (conv_bias, norm_gain, norm_bias, in_weight, in_bias, out_weight, out_bias, layer_scale, spread, lines)
    x0, acc = call(
        conv0_kernel,
        (state, left, right, got_a, got_b, taps),
        (padded, sums),
        [relaid, pltpu.VMEM((cols + 24, ch), F32)],
        conv_flops,
    )
    strips = pltpu.VMEM((2 * HALO, cols + 16, ch), F32)
    x1 = call(mlp0_kernel, (acc, x0, conv_kernel) + params, padded, [strips], mlp_flops)
    acc = call(conv1_kernel, (x1, taps), sums, [relaid], conv_flops)
    whole = pltpu.VMEM((size.lines, ch), F32)
    return call(mlp1_kernel, (acc, x1, mask) + params, jax.ShapeDtypeStruct(fields.shape, BF), [whole], mlp_flops)


def solution(mesh):
    return jax.shard_map(
        shards,
        mesh=mesh,
        in_specs=(P("lat", "lon", None), P("lat", "lon")) + (P(),) * 9,
        out_specs=P("lat", "lon", None),
        check_vma=False,
    )
```

```python
import functools

import jax
import jax.numpy as jnp
from jax import lax
from jax.experimental import pallas as pl
from jax.experimental.pallas import tpu as pltpu
from jax.sharding import PartitionSpec as P

BF = jnp.bfloat16
F32 = jnp.float32
TAPS = 7
HALO = 3
REACH = 2 * HALO
OUTS = 8
BASE = 8
VMEM_LIMIT = 16 * 1024 * 1024
ERF_POLY = (0.7975078797359708, 0.03700565107996738, -0.0003515176683895368)


def partners(nlat, nlon, parity):
    route = []
    for lat in range(nlat):
        for lon in range(nlon):
            here = lat * nlon + lon
            if lat % 2 == parity:
                there = here + nlon if lat + 1 < nlat else lat * nlon + nlon - 1 - lon
            elif lat > 0:
                there = here - nlon
            else:
                continue
            route.append((here, there))
    return route


def exchange(fields, wet_mask):
    nlat, nlon = lax.axis_size("lat"), lax.axis_size("lon")
    lat = lax.axis_index("lat")
    rows, cols = wet_mask.shape

    def edge(r0, r1, c0, c1):
        return fields[r0:r1, c0:c1] * wet_mask[r0:r1, c0:c1].astype(BF)[:, :, None]

    up = [(i, (i + 1) % nlon) for i in range(nlon)]
    down = [(j, i) for i, j in up]
    left = lax.ppermute(edge(0, rows, cols - REACH, cols), "lon", up)
    right = lax.ppermute(edge(0, rows, 0, REACH), "lon", down)
    first = jnp.concatenate([left[:REACH], edge(0, REACH, 0, cols), right[:REACH]], axis=1)
    last = jnp.concatenate([left[rows - REACH :], edge(rows - REACH, rows, 0, cols), right[rows - REACH :]], axis=1)
    even = lat % 2 == 0
    got_a = lax.ppermute(jnp.where(even, last, first), ("lat", "lon"), partners(nlat, nlon, 0))
    got_b = lax.ppermute(jnp.where(even, first, last), ("lat", "lon"), partners(nlat, nlon, 1))
    return left, right, got_a, got_b


def regroup(parts, width):
    parts = list(parts)
    ch = parts[0].shape[-1]
    block = lax.broadcasted_iota(jnp.int32, parts[0].shape, parts[0].ndim - 1) // width
    step = 1
    while step < len(parts):
        low = (block & step) == 0
        for i in range(len(parts)):
            if not i & step:
                x, y = parts[i], parts[i + step]
                parts[i] = jnp.where(low, x, pltpu.roll(y, step * width, x.ndim - 1))
                parts[i + step] = jnp.where(low, pltpu.roll(x, ch - step * width, x.ndim - 1), y)
        step *= 2
    return parts


def tap_kernel(k_ref, inw_ref, cbias_ref, gain_ref, nbias_ref, w_ref, spread_ref, lines_ref, kv_ref):
    ch = k_ref.shape[2]
    lanes = w_ref.shape[3]
    width = lanes // OUTS
    groups = ch // width
    gr = pl.program_id(1)

    @pl.when(gr == 0)
    def _():
        block = lax.broadcasted_iota(jnp.int32, (1, ch), 1) // width
        for n, ref in enumerate((cbias_ref, gain_ref, nbias_ref)):
            for g in range(groups):
                line = jnp.zeros((1, ch), F32)
                for j in range(groups):
                    line = jnp.where(block == j, pltpu.roll(ref[pl.ds(pl.program_id(0), 1), :], (j - g) * width % ch, 1), line)
                lines_ref[0, n * groups + g : n * groups + g + 1, :] = line
        down = [k_ref[0, pl.ds(s, TAPS, stride=TAPS), :] for s in range(TAPS - 1, -1, -1)]
        down.append(jnp.zeros((TAPS, ch), F32))
        halves = [regroup(down[i : i + groups], width) for i in range(0, OUTS, groups)]
        out_col = lax.broadcasted_iota(jnp.int32, (TAPS, lanes), 1) // width
        for g in range(groups):
            line = jnp.concatenate([half[g] for half in halves], axis=1)
            for p in range(2 * OUTS):
                turned = pltpu.roll(line, (p - TAPS + 1) * width % lanes, 1)
                seen = (out_col <= p) & (out_col >= p - TAPS + 1)
                kv_ref[g, p, 0:TAPS, :] = jnp.where(seen, turned, 0.0)

    lane = lax.broadcasted_iota(jnp.int32, (width, lanes), 1)
    own = (lane % width) == lax.broadcasted_iota(jnp.int32, (width, lanes), 0)
    for r in range(TAPS):
        for p in range(2 * OUTS):
            vec = kv_ref[gr, p, r : r + 1, :]
            at = (r * 2 * OUTS + p) * width
            w_ref[0, 0, at : at + width, :] = jnp.where(own, vec, 0.0).astype(BF)
    mine = inw_ref[0]
    for o in range(groups):
        for j in range(groups):
            spread_ref[0, o, j * width : (j + 1) * width, :] = mine if j == o else jnp.zeros_like(mine)


def tap_matrices(conv_kernel, in_weight, conv_bias, norm_gain, norm_bias):
    blocks, taps, ch = conv_kernel.shape
    hid = in_weight.shape[2]
    lanes = 2 * ch
    width = lanes // OUTS
    groups = ch // width
    depth = TAPS * 2 * OUTS * width
    return pl.pallas_call(
        tap_kernel,
        grid=(blocks, groups),
        in_specs=[
            pl.BlockSpec((1, taps, ch), lambda b, g: (b, 0, 0)),
            pl.BlockSpec((1, width, hid), lambda b, g: (b, g, 0)),
        ]
        + [pl.BlockSpec((blocks, ch), lambda b, g: (0, 0))] * 3,
        out_specs=(
            pl.BlockSpec((1, 1, depth, lanes), lambda b, g: (b, g, 0, 0)),
            pl.BlockSpec((1, groups, ch, hid), lambda b, g: (b, 0, g, 0)),
            pl.BlockSpec((1, 3 * groups, ch), lambda b, g: (b, 0, 0)),
        ),
        out_shape=(
            jax.ShapeDtypeStruct((blocks, groups, depth, lanes), BF),
            jax.ShapeDtypeStruct((blocks, groups, groups * ch, hid), BF),
            jax.ShapeDtypeStruct((blocks, 3 * groups, ch), F32),
        ),
        scratch_shapes=[pltpu.VMEM((groups, 2 * OUTS, 8, lanes), F32)],
        compiler_params=pltpu.CompilerParams(vmem_limit_bytes=24 * 1024 * 1024),
        cost_estimate=pl.CostEstimate(
            flops=0, bytes_accessed=2 * blocks * groups * depth * lanes, transcendentals=0
        ),
        name="tap_matrices",
    )(conv_kernel, in_weight, conv_bias, norm_gain, norm_bias)


class Sizes:
    def __init__(self, rows, cols, ch):
        self.rows, self.cols, self.ch = rows, cols, ch
        self.width = 2 * ch // OUTS
        self.groups = ch // self.width
        self.octets = cols // OUTS
        self.pitch = cols + 24
        self.lines = (rows + 2 * REACH) * self.pitch
        self.wide0 = cols + 16

    def line(self, row):
        return pl.multiple_of((row + REACH) * self.pitch, 8)


def place():
    lat = lax.axis_index("lat")
    return lat % 2 == 0, lat == lax.axis_size("lat") - 1, lat == 0


def relay(size, src_ref, relaid_ref):
    octets, groups, width, ch = size.octets, size.groups, size.width, size.ch
    lines = size.rows + 2 * HALO
    step = next(d for d in (6, 4, 3, 2, 1) if lines % d == 0)
    shape = (groups * ch, groups * ch)
    old = lax.broadcasted_iota(jnp.int32, shape, 0)
    new = lax.broadcasted_iota(jnp.int32, shape, 1)
    order = jnp.where(new == old % ch // width * ch + old // ch * width + old % width, 1.0, 0.0).astype(BF)

    def one(q, carry):
        cells = []
        for a in range(4):
            for i in range(step):
                at = size.line(q * step + i - HALO) + BASE - HALO + 4 * a
                parts = [src_ref[pl.ds(at + j, octets, stride=OUTS), :].astype(BF) for j in range(groups)]
                cells.append(jnp.concatenate(parts, axis=1))
        moved = jnp.dot(jnp.concatenate(cells, axis=0), order, preferred_element_type=F32).astype(BF)
        n = step * octets
        for a in range(4):
            for gr in range(groups):
                relaid_ref[gr, a, pl.ds(pl.multiple_of(q * n, 16), n), :] = moved[
                    a * n : (a + 1) * n, gr * ch : (gr + 1) * ch
                ]
        return carry

    lax.fori_loop(0, lines // step, one, 0)


def conv(size, relaid_ref, w_ref, acc_ref, beside=()):
    octets, rows = size.octets, size.rows

    for gr in range(size.groups):
        parts = []
        for r in range(TAPS):
            for a in range(4):
                parts.append(relaid_ref[gr, a, r * octets : (r + rows) * octets, :])
        acc_ref[gr] = jnp.dot(jnp.concatenate(parts, axis=1), w_ref[0, gr], preferred_element_type=F32)
        for work in beside[gr :: size.groups]:
            work()


def column_strip(size, start, x0_ref, k_ref, strip_ref):
    rows, pitch = size.rows, size.pitch
    sums = [jnp.zeros((rows, size.ch), F32) for _ in range(HALO)]
    for r in range(TAPS):
        for c in range(TAPS + HALO - 1):
            at = (REACH - HALO + r) * pitch + BASE + start - HALO + c
            cells = x0_ref[pl.ds(at, rows, stride=pitch), :]
            for i in range(HALO):
                if 0 <= c - i < TAPS:
                    tap = TAPS * r + c - i
                    sums[i] = sums[i] + cells * k_ref[0, tap : tap + 1, :]
    for i in range(HALO):
        strip_ref[i] = sums[i]


def row_strip(size, side, c, piece, top, x0_ref, k_ref, strip_ref):
    pitch, lead = size.pitch, BASE - REACH
    first = (0 if side == 0 else size.rows + HALO) * pitch
    sums = [jnp.zeros((piece, size.ch), F32) for _ in range(HALO)]
    for s in range(TAPS):
        at = first + lead + s + c
        lines = [x0_ref[at + i * pitch : at + i * pitch + piece, :] for i in range(TAPS + HALO - 1)]
        for r in range(TAPS):
            tap = TAPS * r + s
            if side == 1:
                tap = jnp.where(top, TAPS * TAPS - 1 - tap, tap)
            weight = k_ref[0, pl.ds(tap, 1), :]
            for i in range(HALO):
                sums[i] = sums[i] + lines[i + r] * weight
    for i in range(HALO):
        strip_ref[side * HALO + i, c : c + piece, :] = sums[i]


def conv0_kernel(size, *refs):
    x_ref, mask_ref, left_ref, right_ref, a_ref, b_ref, w_ref, k_ref = refs[:8]
    x0_ref, acc_ref, row_ref, col_ref, relaid_ref, flip_ref = refs[8:]
    rows, cols, ch, pitch, wide0 = size.rows, size.cols, size.ch, size.pitch, size.wide0
    base, ext, lead = BASE, cols + 2 * REACH, BASE - REACH
    line = size.line
    even, top, _ = place()

    def fill(i, carry):
        at = line(i)
        x0_ref[pl.ds(at, base), :] = jnp.zeros((base, ch), F32)
        x0_ref[pl.ds(at + lead, REACH), :] = left_ref[i].astype(F32)
        x0_ref[pl.ds(at + base, cols), :] = (x_ref[i] * mask_ref[i]).astype(F32)
        x0_ref[pl.ds(at + base + cols, 16), :] = jnp.zeros((16, ch), F32)
        x0_ref[pl.ds(at + base + cols, REACH), :] = right_ref[i].astype(F32)
        return carry

    lax.fori_loop(0, rows, fill, 0)
    flip_ref[...] = jnp.zeros(flip_ref.shape, F32)
    at = lax.broadcasted_iota(jnp.int32, (wide0, wide0), 0)
    to = lax.broadcasted_iota(jnp.int32, (wide0, wide0), 1)
    mirror = jnp.where(to == jnp.where(top, ext - 1 - at, at), 1.0, 0.0).astype(BF)
    for i in range(REACH):
        south, north = i * pitch, (rows + REACH + i) * pitch
        x0_ref[south : south + pitch, :] = jnp.zeros((pitch, ch), F32)
        x0_ref[south + lead : south + lead + ext, :] = jnp.where(even, b_ref[i].astype(F32), a_ref[i].astype(F32))
        src = jnp.where(top, REACH - 1 - i, i)
        flip_ref[0:ext, :] = jnp.where(even, a_ref[src].astype(F32), b_ref[src].astype(F32))
        turned = jnp.dot(mirror, flip_ref[0:wide0, :].astype(BF), preferred_element_type=F32)
        x0_ref[north : north + pitch, :] = jnp.zeros((pitch, ch), F32)
        x0_ref[north + lead : north + lead + wide0, :] = turned
    relay(size, x0_ref, relaid_ref)
    piece = wide0 // 3
    beside = [functools.partial(column_strip, size, -HALO, x0_ref, k_ref, col_ref.at[0])]
    beside.append(functools.partial(column_strip, size, cols, x0_ref, k_ref, col_ref.at[1]))
    for side in range(2):
        for c in range(0, wide0, piece):
            beside.append(functools.partial(row_strip, size, side, c, piece, top, x0_ref, k_ref, row_ref))
    conv(size, relaid_ref, w_ref, acc_ref, beside)


def conv1_kernel(size, x1_ref, w_ref, acc_ref, relaid_ref):
    relay(size, x1_ref, relaid_ref)
    conv(size, relaid_ref, w_ref, acc_ref)


def gelu_twice(h):
    z = h * h
    p = jnp.full_like(z, ERF_POLY[-1])
    for coef in ERF_POLY[-2::-1]:
        p = p * z + jnp.asarray(coef, z.dtype)
    return h + h * jnp.tanh(h * p)


def norm(b, params, val):
    cbias_ref, gain_ref, nbias_ref = params[:3]
    val = val + cbias_ref[b : b + 1, :]
    cen = val - jnp.mean(val, axis=-1, keepdims=True)
    var = jnp.mean(cen * cen, axis=-1, keepdims=True)
    return (cen * lax.rsqrt(var + 1e-6) * gain_ref[b : b + 1, :] + nbias_ref[b : b + 1, :]).astype(BF)


def project(b, params, normed, weight_ref, index):
    inb_ref, outw_ref, outb_ref, scale_ref = params[4:8]
    rows = normed.shape[0]
    tile = 48 if rows % 48 == 0 else 64
    branch = None
    half_hid = outw_ref.shape[1] // 2
    for c in range(0, 2 * half_hid, half_hid):
        hid = jnp.dot(normed, weight_ref[index + (slice(None), slice(c, c + half_hid))], preferred_element_type=F32)
        bias = inb_ref[b : b + 1, c : c + half_hid]
        act = [gelu_twice((hid[i : i + tile] + bias).astype(BF)) for i in range(0, rows, tile)]
        part = jnp.dot(jnp.concatenate(act, axis=0), outw_ref[b, c : c + half_hid, :], preferred_element_type=F32)
        branch = part if branch is None else branch + part
    scale = scale_ref[b : b + 1, :]
    return branch * (0.5 * scale) + outb_ref[b : b + 1, :] * scale


def mlp(b, params, parts):
    n = parts[0].shape[0]
    normed = jnp.concatenate([norm(b, params, part) for part in parts], axis=0)
    branch = project(b, params, normed, params[3], (b,))
    return [branch[i * n : (i + 1) * n] for i in range(len(parts))]


def block_sums(size, val):
    ch = size.ch
    row = lax.broadcasted_iota(jnp.int32, (2 * ch, ch), 0) % ch
    col = lax.broadcasted_iota(jnp.int32, (2 * ch, ch), 1)
    ones = jnp.where(row // size.width == col // size.width, 1.0, 0.0).astype(BF)
    high = val.astype(BF)
    low = (val - high.astype(F32)).astype(BF)
    return jnp.dot(jnp.concatenate([high, low], axis=1), ones, preferred_element_type=F32)


def norm_grouped(size, lines_ref, parts):
    groups = size.groups
    share = 1.0 / size.ch

    def line(n, gr):
        return lines_ref[0, n * groups + gr : n * groups + gr + 1, :]

    vals = [part + line(0, gr) for gr, part in enumerate(parts)]
    mean = block_sums(size, sum(vals[1:], vals[0])) * share
    cens = [val - mean for val in vals]
    squares = [cen * cen for cen in cens]
    inv = lax.rsqrt(block_sums(size, sum(squares[1:], squares[0])) * share + 1e-6)
    normed = [(cen * inv * line(1, gr) + line(2, gr)).astype(BF) for gr, cen in enumerate(cens)]
    return jnp.concatenate(normed, axis=1)


def rounded(val):
    return val.astype(BF).astype(F32)


def rounded(val):
    return val.astype(BF).astype(F32)


def inner(size, b, params, acc_ref, src_ref, dst_ref):
    rows, octets, groups, ch = size.rows, size.octets, size.groups, size.ch
    spread_ref, lines_ref = params[8:]
    step = next(d for d in (24, 16, 12, 8, 6, 4, 3, 2, 1) if rows % d == 0)
    n = step * octets

    def one(t, carry):
        for half in range(2):
            parts = [
                acc_ref[gr, pl.ds(pl.multiple_of(t * n, 16), n), half * ch : (half + 1) * ch] for gr in range(groups)
            ]
            normed = norm_grouped(size, lines_ref, parts)
            for j in range(groups):
                branch = project(b, params, normed, spread_ref, (0, j))
                for i in range(step):
                    at = size.line(t * step + i) + BASE + half * groups + j
                    spot = pl.ds(at, octets, stride=OUTS)
                    dst_ref[spot, :] = rounded(src_ref[spot, :] + branch[i * octets : (i + 1) * octets])
        return carry

    lax.fori_loop(0, rows // step, one, 0)


def mlp0_kernel(size, acc_ref, x0_ref, row_ref, col_ref, *refs):
    params, x1_ref = refs[:10], refs[10]
    rows, cols, ch, pitch, wide0 = size.rows, size.cols, size.ch, size.pitch, size.wide0
    base, near = BASE, BASE - HALO
    _, _, bottom = place()

    def clear(i, carry):
        at = size.line(i)
        x1_ref[pl.ds(at, base), :] = jnp.zeros((base, ch), F32)
        x1_ref[pl.ds(at + base + cols, 16), :] = jnp.zeros((16, ch), F32)
        return carry

    lax.fori_loop(0, rows, clear, 0)
    inner(size, 0, params, acc_ref, x0_ref, x1_ref)
    for side, start in enumerate((-HALO, cols)):
        for i, branch in enumerate(mlp(0, params, [col_ref[side, i] for i in range(HALO)])):
            spot = pl.ds(REACH * pitch + BASE + start + i, rows, stride=pitch)
            x1_ref[spot, :] = rounded(x0_ref[spot, :] + branch)
    for side in range(2):
        branches = mlp(0, params, [row_ref[side * HALO + i] for i in range(HALO)])
        for i, branch in enumerate(branches):
            row = i - HALO if side == 0 else rows + i
            at = (row + REACH) * pitch + near
            new = rounded(x0_ref[at : at + wide0, :] + branch)
            if side == 0:
                new = jnp.where(bottom, 0.0, new)
            x1_ref[at : at + wide0, :] = new


def mlp1_kernel(size, acc_ref, x1_ref, mask_ref, *refs):
    params, (out_ref, x2_ref) = refs[:10], refs[10:]
    inner(size, 1, params, acc_ref, x1_ref, x2_ref)

    def finish(i, carry):
        out_ref[i] = x2_ref[pl.ds(size.line(i) + BASE, size.cols), :].astype(BF) * mask_ref[i]
        return carry

    lax.fori_loop(0, size.rows, finish, 0)


def shards(
    fields,
    wet_mask,
    conv_kernel,
    conv_bias,
    norm_gain,
    norm_bias,
    in_weight,
    in_bias,
    out_weight,
    out_bias,
    layer_scale,
):
    rows, cols, ch = fields.shape
    left, right, got_a, got_b = exchange(fields, wet_mask)
    conv_kernel, whole_mask, left, right = lax.optimization_barrier((conv_kernel, wet_mask, left, right))
    mask = jnp.broadcast_to(whole_mask.astype(BF)[:, :, None], fields.shape)
    taps, spread, lines = tap_matrices(conv_kernel, in_weight, conv_bias, norm_gain, norm_bias)
    groups, depth, width = taps.shape[1:]
    hid = in_weight.shape[2]
    size = Sizes(rows, cols, ch)
    cells = rows * cols
    vmem = pl.BlockSpec(memory_space=pltpu.VMEM)
    relaid = pltpu.VMEM((groups, 4, (rows + 2 * HALO) * size.octets, ch), BF)
    padded = jax.ShapeDtypeStruct((size.lines, ch), F32)
    sums = jax.ShapeDtypeStruct((groups, rows * size.octets, width), F32)

    def call(kernel, ins, out_shape, scratch, flops):
        def spec(value):
            if value is not taps and value is not spread and value is not lines:
                return vmem
            block = 0 if kernel in (conv0_kernel, mlp0_kernel) else 1
            return pl.BlockSpec((1,) + value.shape[1:], lambda i: (block,) + (0,) * (value.ndim - 1))

        several = isinstance(out_shape, tuple)
        return pl.pallas_call(
            functools.partial(kernel, size),
            grid=(1,),
            in_specs=[spec(value) for value in ins],
            out_specs=(vmem,) * len(out_shape) if several else vmem,
            out_shape=out_shape,
            scratch_shapes=scratch,
            compiler_params=pltpu.CompilerParams(vmem_limit_bytes=VMEM_LIMIT),
            cost_estimate=pl.CostEstimate(flops=flops, bytes_accessed=6 * cells * ch, transcendentals=cells * hid),
            name=kernel.__name__,
        )(*ins)

    conv_flops = 2 * cells * ch * depth // OUTS * 2
    mlp_flops = 4 * cells * ch * hid
    params = (conv_bias, norm_gain, norm_bias, in_weight, in_bias, out_weight, out_bias, layer_scale, spread, lines)
    row_strips = jax.ShapeDtypeStruct((2 * HALO, size.wide0, ch), F32)
    col_strips = jax.ShapeDtypeStruct((2, HALO, rows, ch), F32)
    x0, acc, row_sums, col_sums = call(
        conv0_kernel,
        (fields, mask, left, right, got_a, got_b, taps, conv_kernel),
        (padded, sums, row_strips, col_strips),
        [relaid, pltpu.VMEM((cols + 24, ch), F32)],
        conv_flops,
    )
    x1 = call(mlp0_kernel, (acc, x0, row_sums, col_sums) + params, padded, [], mlp_flops)
    acc = call(conv1_kernel, (x1, taps), sums, [relaid], conv_flops)
    whole = pltpu.VMEM((size.lines, ch), F32)
    return call(mlp1_kernel, (acc, x1, mask) + params, jax.ShapeDtypeStruct(fields.shape, BF), [whole], mlp_flops)


def solution(mesh):
    return jax.shard_map(
        shards,
        mesh=mesh,
        in_specs=(P("lat", "lon", None), P("lat", "lon")) + (P(),) * 9,
        out_specs=P("lat", "lon", None),
        check_vma=False,
    )
```

```python
import functools

import jax
import jax.numpy as jnp
from jax import lax
from jax.experimental import pallas as pl
from jax.experimental.pallas import tpu as pltpu
from jax.sharding import PartitionSpec as P

BF = jnp.bfloat16
F32 = jnp.float32
TAPS = 7
HALO = 3
REACH = 2 * HALO
OUTS = 8
BASE = 8
VMEM_LIMIT = 16 * 1024 * 1024
ERF_POLY = (0.7975078797359708, 0.03700565107996738, -0.0003515176683895368)


def partners(nlat, nlon, parity):
    route = []
    for lat in range(nlat):
        for lon in range(nlon):
            here = lat * nlon + lon
            if lat % 2 == parity:
                there = here + nlon if lat + 1 < nlat else lat * nlon + nlon - 1 - lon
            elif lat > 0:
                there = here - nlon
            else:
                continue
            route.append((here, there))
    return route


def edge(fields, wet_mask, r0, r1, c0, c1):
    return fields[r0:r1, c0:c1] * wet_mask[r0:r1, c0:c1].astype(BF)[:, :, None]


def exchange_columns(fields, wet_mask):
    nlon = lax.axis_size("lon")
    rows, cols = wet_mask.shape
    up = [(i, (i + 1) % nlon) for i in range(nlon)]
    down = [(j, i) for i, j in up]
    left = lax.ppermute(edge(fields, wet_mask, 0, rows, cols - REACH, cols), "lon", up)
    right = lax.ppermute(edge(fields, wet_mask, 0, rows, 0, REACH), "lon", down)
    return left, right


def exchange_rows(fields, wet_mask, left, right):
    nlat, nlon = lax.axis_size("lat"), lax.axis_size("lon")
    rows, cols = wet_mask.shape
    first = jnp.concatenate([left[:REACH], edge(fields, wet_mask, 0, REACH, 0, cols), right[:REACH]], axis=1)
    last = edge(fields, wet_mask, rows - REACH, rows, 0, cols)
    last = jnp.concatenate([left[rows - REACH :], last, right[rows - REACH :]], axis=1)
    even = lax.axis_index("lat") % 2 == 0
    got_a = lax.ppermute(jnp.where(even, last, first), ("lat", "lon"), partners(nlat, nlon, 0))
    got_b = lax.ppermute(jnp.where(even, first, last), ("lat", "lon"), partners(nlat, nlon, 1))
    return got_a, got_b


def regroup(parts, width):
    parts = list(parts)
    ch = parts[0].shape[-1]
    block = lax.broadcasted_iota(jnp.int32, parts[0].shape, parts[0].ndim - 1) // width
    step = 1
    while step < len(parts):
        low = (block & step) == 0
        for i in range(len(parts)):
            if not i & step:
                x, y = parts[i], parts[i + step]
                parts[i] = jnp.where(low, x, pltpu.roll(y, step * width, x.ndim - 1))
                parts[i + step] = jnp.where(low, pltpu.roll(x, ch - step * width, x.ndim - 1), y)
        step *= 2
    return parts


def tap_kernel(blocks, small_ref, inw_ref, w_ref, spread_ref, lines_ref, kv_ref):
    ch = small_ref.shape[1]
    lanes = w_ref.shape[3]
    width = lanes // OUTS
    groups = ch // width
    b, gr = pl.program_id(0), pl.program_id(1)

    @pl.when(gr == 0)
    def _():
        block = lax.broadcasted_iota(jnp.int32, (1, ch), 1) // width
        for n in range(3):
            vec = small_ref[pl.ds(blocks * (TAPS * TAPS + n) + b, 1), :]
            for g in range(groups):
                line = jnp.zeros((1, ch), F32)
                for j in range(groups):
                    line = jnp.where(block == j, pltpu.roll(vec, (j - g) * width % ch, 1), line)
                lines_ref[0, n * groups + g : n * groups + g + 1, :] = line
        down = [small_ref[pl.ds(b * TAPS * TAPS + s, TAPS, stride=TAPS), :] for s in range(TAPS - 1, -1, -1)]
        down.append(jnp.zeros((TAPS, ch), F32))
        halves = [regroup(down[i : i + groups], width) for i in range(0, OUTS, groups)]
        out_col = lax.broadcasted_iota(jnp.int32, (TAPS, lanes), 1) // width
        for g in range(groups):
            line = jnp.concatenate([half[g] for half in halves], axis=1)
            for p in range(2 * OUTS):
                turned = pltpu.roll(line, (p - TAPS + 1) * width % lanes, 1)
                seen = (out_col <= p) & (out_col >= p - TAPS + 1)
                kv_ref[g, p, 0:TAPS, :] = jnp.where(seen, turned, 0.0)

    lane = lax.broadcasted_iota(jnp.int32, (width, lanes), 1)
    own = (lane % width) == lax.broadcasted_iota(jnp.int32, (width, lanes), 0)
    for r in range(TAPS):
        for p in range(2 * OUTS):
            vec = kv_ref[gr, p, r : r + 1, :]
            at = (r * 2 * OUTS + p) * width
            w_ref[0, 0, at : at + width, :] = jnp.where(own, vec, 0.0).astype(BF)
    mine = inw_ref[b, pl.ds(pl.multiple_of(gr * width, width), width), :]
    for o in range(groups):
        for j in range(groups):
            spread_ref[0, o, j * width : (j + 1) * width, :] = mine if j == o else jnp.zeros_like(mine)


def tap_matrices(blocks, small, in_weight):
    ch = small.shape[1]
    hid = in_weight.shape[2]
    lanes = 2 * ch
    width = lanes // OUTS
    groups = ch // width
    depth = TAPS * 2 * OUTS * width
    return pl.pallas_call(
        functools.partial(tap_kernel, blocks),
        grid=(blocks, groups),
        in_specs=[pl.BlockSpec(memory_space=pltpu.VMEM)] * 2,
        out_specs=(
            pl.BlockSpec((1, 1, depth, lanes), lambda b, g: (b, g, 0, 0)),
            pl.BlockSpec((1, groups, ch, hid), lambda b, g: (b, 0, g, 0)),
            pl.BlockSpec((1, 3 * groups, ch), lambda b, g: (b, 0, 0)),
        ),
        out_shape=(
            jax.ShapeDtypeStruct((blocks, groups, depth, lanes), BF),
            jax.ShapeDtypeStruct((blocks, groups, groups * ch, hid), BF),
            jax.ShapeDtypeStruct((blocks, 3 * groups, ch), F32),
        ),
        scratch_shapes=[pltpu.VMEM((groups, 2 * OUTS, 8, lanes), F32)],
        compiler_params=pltpu.CompilerParams(vmem_limit_bytes=24 * 1024 * 1024),
        cost_estimate=pl.CostEstimate(
            flops=0, bytes_accessed=2 * blocks * groups * depth * lanes, transcendentals=0
        ),
        name="tap_matrices",
    )(small, in_weight)


class Sizes:
    def __init__(self, rows, cols, ch):
        self.rows, self.cols, self.ch = rows, cols, ch
        self.width = 2 * ch // OUTS
        self.groups = ch // self.width
        self.octets = cols // OUTS
        self.pitch = cols + 24
        self.lines = (rows + 2 * REACH) * self.pitch
        self.wide0 = cols + 16

    def line(self, row, above=REACH):
        return pl.multiple_of((row + above) * self.pitch, 8)


def place():
    lat = lax.axis_index("lat")
    return lat % 2 == 0, lat == lax.axis_size("lat") - 1, lat == 0


def relay(size, lines, start, relaid_ref, first=0):
    octets, groups, width, ch = size.octets, size.groups, size.width, size.ch
    step = next(d for d in (6, 4, 3, 2, 1) if lines % d == 0)
    shape = (groups * ch, groups * ch)
    old = lax.broadcasted_iota(jnp.int32, shape, 0)
    new = lax.broadcasted_iota(jnp.int32, shape, 1)
    order = jnp.where(new == old % ch // width * ch + old // ch * width + old % width, 1.0, 0.0).astype(BF)

    def one(q, carry):
        cells = []
        for a in range(4):
            for i in range(step):
                src_ref, at = start(q * step + i)
                at = at + BASE - HALO + 4 * a
                parts = [src_ref[pl.ds(at + j, octets, stride=OUTS), :].astype(BF) for j in range(groups)]
                cells.append(jnp.concatenate(parts, axis=1))
        moved = jnp.dot(jnp.concatenate(cells, axis=0), order, preferred_element_type=F32).astype(BF)
        n = step * octets
        for a in range(4):
            for gr in range(groups):
                relaid_ref[gr, a, pl.ds(pl.multiple_of(first * octets + q * n, 16), n), :] = moved[
                    a * n : (a + 1) * n, gr * ch : (gr + 1) * ch
                ]
        return carry

    lax.fori_loop(0, lines // step, one, 0)


def conv(size, relaid_ref, ends_ref, w_ref, acc_ref, beside=()):
    octets, rows = size.octets, size.rows

    for gr in range(size.groups):
        parts = []
        for r in range(TAPS):
            for a in range(4):
                low, high = max(HALO - r, 0), max(r - HALO, 0)
                rows_in = [relaid_ref[gr, a, high * octets : (rows - low) * octets, :]]
                if low:
                    rows_in.insert(0, ends_ref[gr, a, (HALO - low) * octets : HALO * octets, :])
                if high:
                    rows_in.append(ends_ref[gr, a, HALO * octets : (HALO + high) * octets, :])
                parts.append(jnp.concatenate(rows_in, axis=0))
        acc_ref[gr] = jnp.dot(jnp.concatenate(parts, axis=1), w_ref[0, gr], preferred_element_type=F32)
        for work in beside[gr :: size.groups]:
            work()


def column_strip(size, side, x0_ref, edge_ref, k_ref, side_ref, strip_ref):
    rows, pitch = size.rows, size.pitch
    start = BASE + (-HALO if side == 0 else size.cols) - HALO
    north = (TAPS + HALO - 1 + HALO) * pitch
    for c in range(TAPS + HALO - 1):
        side_ref[side, c, 0:HALO, :] = edge_ref[pl.ds(HALO * pitch + start + c, HALO, stride=pitch), :]
        side_ref[side, c, HALO : HALO + rows, :] = x0_ref[pl.ds(start + c, rows, stride=pitch), :]
        side_ref[side, c, HALO + rows : 2 * HALO + rows, :] = edge_ref[pl.ds(north + start + c, HALO, stride=pitch), :]
    sums = [jnp.zeros((rows, size.ch), F32) for _ in range(HALO)]
    for r in range(TAPS):
        for c in range(TAPS + HALO - 1):
            cells = side_ref[side, c, r : r + rows, :]
            for i in range(HALO):
                if 0 <= c - i < TAPS:
                    tap = TAPS * r + c - i
                    sums[i] = sums[i] + cells * k_ref[tap : tap + 1, :]
    for i in range(HALO):
        strip_ref[side, i] = sums[i]


def row_strip(size, side, c, piece, top, edge_ref, k_ref, strip_ref):
    pitch, lead = size.pitch, BASE - REACH
    lines_in = TAPS + HALO - 1
    first = side * lines_in * pitch
    sums = [jnp.zeros((piece, size.ch), F32) for _ in range(HALO)]
    for s in range(TAPS):
        at = first + lead + s + c
        lines = [edge_ref[at + i * pitch : at + i * pitch + piece, :] for i in range(lines_in)]
        for r in range(TAPS):
            tap = TAPS * r + s
            if side == 1:
                tap = jnp.where(top, TAPS * TAPS - 1 - tap, tap)
            weight = k_ref[pl.ds(tap, 1), :]
            for i in range(HALO):
                sums[i] = sums[i] + lines[i + r] * weight
    for i in range(HALO):
        strip_ref[side * HALO + i, c : c + piece, :] = sums[i]


def lay_kernel(size, x_ref, mask_ref, left_ref, right_ref, x0_ref, relaid_ref):
    rows, cols, ch, pitch = size.rows, size.cols, size.ch, size.pitch
    lead = BASE - REACH

    def fill(i, carry):
        at = size.line(i, 0)
        x0_ref[pl.ds(at, BASE), :] = jnp.zeros((BASE, ch), F32)
        x0_ref[pl.ds(at + lead, REACH), :] = left_ref[i].astype(F32)
        x0_ref[pl.ds(at + BASE, cols), :] = (x_ref[i] * mask_ref[i]).astype(F32)
        x0_ref[pl.ds(at + BASE + cols, 16), :] = jnp.zeros((16, ch), F32)
        x0_ref[pl.ds(at + BASE + cols, REACH), :] = right_ref[i].astype(F32)
        return carry

    lax.fori_loop(0, rows, fill, 0)
    relay(size, rows, lambda i: (x0_ref, size.line(i, 0)), relaid_ref)


def conv0_kernel(size, x0_ref, relaid_ref, a_ref, b_ref, w_ref, k_ref, *refs):
    edge_ref, acc_ref, row_ref, col_ref, ends_ref, flip_ref, side_ref = refs
    rows, cols, ch, pitch, wide0 = size.rows, size.cols, size.ch, size.pitch, size.wide0
    ext, lead = cols + 2 * REACH, BASE - REACH
    even, top, _ = place()
    lines_in = TAPS + HALO - 1

    flip_ref[...] = jnp.zeros(flip_ref.shape, F32)
    at = lax.broadcasted_iota(jnp.int32, (wide0, wide0), 0)
    to = lax.broadcasted_iota(jnp.int32, (wide0, wide0), 1)
    mirror = jnp.where(to == jnp.where(top, ext - 1 - at, at), 1.0, 0.0).astype(BF)
    edge_ref[0 : REACH * pitch, :] = jnp.zeros((REACH * pitch, ch), F32)
    north = (lines_in + HALO) * pitch
    edge_ref[north : north + REACH * pitch, :] = jnp.zeros((REACH * pitch, ch), F32)
    turned = []
    for i in range(0, REACH, 2):
        for h in range(2):
            south = (i + h) * pitch + lead
            edge_ref[south : south + ext, :] = jnp.where(even, b_ref[i + h].astype(F32), a_ref[i + h].astype(F32))
            src = jnp.where(top, REACH - 1 - i - h, i + h)
            flip_ref[i + h, 0:ext, :] = jnp.where(even, a_ref[src].astype(F32), b_ref[src].astype(F32))
        both = jnp.concatenate([flip_ref[i + h, 0:wide0, :].astype(BF) for h in range(2)], axis=1)
        turned.append(jnp.dot(mirror, both, preferred_element_type=F32))
    for i in range(REACH):
        put = north + i * pitch + lead
        edge_ref[put : put + wide0, :] = turned[i // 2][:, i % 2 * ch : (i % 2 + 1) * ch]
    for i in range(HALO):
        for slot, row in ((REACH + i, i), (lines_in + i, rows - HALO + i)):
            edge_ref[slot * pitch : (slot + 1) * pitch, :] = x0_ref[row * pitch : (row + 1) * pitch, :]

    def start(i):
        return edge_ref, pl.multiple_of(jnp.where(i < HALO, HALO + i, lines_in + i) * pitch, 8)

    relay(size, 2 * HALO, start, ends_ref)
    piece = wide0 // 3
    beside = [
        functools.partial(column_strip, size, side, x0_ref, edge_ref, k_ref, side_ref, col_ref) for side in range(2)
    ]
    for side in range(2):
        for c in range(0, wide0, piece):
            beside.append(functools.partial(row_strip, size, side, c, piece, top, edge_ref, k_ref, row_ref))
    conv(size, relaid_ref, ends_ref, w_ref, acc_ref, beside)


def conv1_kernel(size, x1_ref, w_ref, acc_ref, relaid_ref, ends_ref):
    relay(size, size.rows, lambda i: (x1_ref, size.line(i)), relaid_ref)

    def start(i):
        return x1_ref, size.line(jnp.where(i < HALO, i - HALO, size.rows - HALO + i))

    relay(size, 2 * HALO, start, ends_ref)
    conv(size, relaid_ref, ends_ref, w_ref, acc_ref)


def gelu_twice(h):
    z = h * h
    p = jnp.full_like(z, ERF_POLY[-1])
    for coef in ERF_POLY[-2::-1]:
        p = p * z + jnp.asarray(coef, z.dtype)
    return h + h * jnp.tanh(h * p)


def norm(b, params, val):
    cbias_ref, gain_ref, nbias_ref = params[:3]
    val = val + cbias_ref[b : b + 1, :]
    cen = val - jnp.mean(val, axis=-1, keepdims=True)
    var = jnp.mean(cen * cen, axis=-1, keepdims=True)
    return (cen * lax.rsqrt(var + 1e-6) * gain_ref[b : b + 1, :] + nbias_ref[b : b + 1, :]).astype(BF)


def project(b, params, normed, weight_ref, index):
    inb_ref, outw_ref, outb_ref, scale_ref = params[4:8]
    rows = normed.shape[0]
    tile = 48 if rows % 48 == 0 else 64
    branch = None
    half_hid = outw_ref.shape[1] // 2
    for c in range(0, 2 * half_hid, half_hid):
        hid = jnp.dot(normed, weight_ref[index + (slice(None), slice(c, c + half_hid))], preferred_element_type=F32)
        bias = inb_ref[b : b + 1, c : c + half_hid]
        act = [gelu_twice((hid[i : i + tile] + bias).astype(BF)) for i in range(0, rows, tile)]
        part = jnp.dot(jnp.concatenate(act, axis=0), outw_ref[b, c : c + half_hid, :], preferred_element_type=F32)
        branch = part if branch is None else branch + part
    scale = scale_ref[b : b + 1, :]
    return branch * (0.5 * scale) + outb_ref[b : b + 1, :] * scale


def mlp(b, params, parts):
    n = parts[0].shape[0]
    normed = jnp.concatenate([norm(b, params, part) for part in parts], axis=0)
    branch = project(b, params, normed, params[3], (b,))
    return [branch[i * n : (i + 1) * n] for i in range(len(parts))]


def block_sums(size, val):
    ch = size.ch
    row = lax.broadcasted_iota(jnp.int32, (2 * ch, ch), 0) % ch
    col = lax.broadcasted_iota(jnp.int32, (2 * ch, ch), 1)
    ones = jnp.where(row // size.width == col // size.width, 1.0, 0.0).astype(BF)
    high = val.astype(BF)
    low = (val - high.astype(F32)).astype(BF)
    return jnp.dot(jnp.concatenate([high, low], axis=1), ones, preferred_element_type=F32)


def norm_grouped(size, lines_ref, parts):
    groups = size.groups
    share = 1.0 / size.ch

    def line(n, gr):
        return lines_ref[0, n * groups + gr : n * groups + gr + 1, :]

    vals = [part + line(0, gr) for gr, part in enumerate(parts)]
    mean = block_sums(size, sum(vals[1:], vals[0])) * share
    cens = [val - mean for val in vals]
    squares = [cen * cen for cen in cens]
    inv = lax.rsqrt(block_sums(size, sum(squares[1:], squares[0])) * share + 1e-6)
    normed = [(cen * inv * line(1, gr) + line(2, gr)).astype(BF) for gr, cen in enumerate(cens)]
    return jnp.concatenate(normed, axis=1)


def rounded(val):
    return val.astype(BF).astype(F32)


def rounded(val):
    return val.astype(BF).astype(F32)


def inner(size, b, params, acc_ref, src_ref, above, dst_ref):
    rows, octets, groups, ch = size.rows, size.octets, size.groups, size.ch
    spread_ref, lines_ref = params[8:]
    step = next(d for d in (24, 16, 12, 8, 6, 4, 3, 2, 1) if rows % d == 0)
    n = step * octets

    def one(t, carry):
        for half in range(2):
            parts = [
                acc_ref[gr, pl.ds(pl.multiple_of(t * n, 16), n), half * ch : (half + 1) * ch] for gr in range(groups)
            ]
            normed = norm_grouped(size, lines_ref, parts)
            for j in range(groups):
                branch = project(b, params, normed, spread_ref, (0, j))
                for i in range(step):
                    at = BASE + half * groups + j
                    old = src_ref[pl.ds(size.line(t * step + i, above) + at, octets, stride=OUTS), :]
                    new = rounded(old + branch[i * octets : (i + 1) * octets])
                    dst_ref[pl.ds(size.line(t * step + i) + at, octets, stride=OUTS), :] = new
        return carry

    lax.fori_loop(0, rows // step, one, 0)


def mlp0_kernel(size, acc_ref, x0_ref, edge_ref, row_ref, col_ref, *refs):
    params, x1_ref = refs[:10], refs[10]
    rows, cols, ch, pitch, wide0 = size.rows, size.cols, size.ch, size.pitch, size.wide0
    base, near = BASE, BASE - HALO
    _, _, bottom = place()

    def clear(i, carry):
        at = size.line(i)
        x1_ref[pl.ds(at, base), :] = jnp.zeros((base, ch), F32)
        x1_ref[pl.ds(at + base + cols, 16), :] = jnp.zeros((16, ch), F32)
        return carry

    lax.fori_loop(0, rows, clear, 0)
    inner(size, 0, params, acc_ref, x0_ref, 0, x1_ref)
    for side, start in enumerate((-HALO, cols)):
        for i, branch in enumerate(mlp(0, params, [col_ref[side, i] for i in range(HALO)])):
            old = x0_ref[pl.ds(BASE + start + i, rows, stride=pitch), :]
            x1_ref[pl.ds(REACH * pitch + BASE + start + i, rows, stride=pitch), :] = rounded(old + branch)
    for side in range(2):
        branches = mlp(0, params, [row_ref[side * HALO + i] for i in range(HALO)])
        for i, branch in enumerate(branches):
            row = i - HALO if side == 0 else rows + i
            at = (row + REACH) * pitch + near
            here = (side * (TAPS + HALO - 1) + HALO + i) * pitch + near
            new = rounded(edge_ref[here : here + wide0, :] + branch)
            if side == 0:
                new = jnp.where(bottom, 0.0, new)
            x1_ref[at : at + wide0, :] = new


def mlp1_kernel(size, acc_ref, x1_ref, mask_ref, *refs):
    params, (out_ref, x2_ref) = refs[:10], refs[10:]
    inner(size, 1, params, acc_ref, x1_ref, REACH, x2_ref)

    def finish(i, carry):
        out_ref[i] = x2_ref[pl.ds(size.line(i) + BASE, size.cols), :].astype(BF) * mask_ref[i]
        return carry

    lax.fori_loop(0, size.rows, finish, 0)


def shards(
    fields,
    wet_mask,
    conv_kernel,
    conv_bias,
    norm_gain,
    norm_bias,
    in_weight,
    in_bias,
    out_weight,
    out_bias,
    layer_scale,
):
    rows, cols, ch = fields.shape
    left, right = exchange_columns(fields, wet_mask)
    mask = jnp.broadcast_to(wet_mask.astype(BF)[:, :, None], fields.shape)
    small = jnp.concatenate([conv_kernel.reshape(-1, ch), conv_bias, norm_gain, norm_bias])
    taps, spread, lines = tap_matrices(conv_kernel.shape[0], small, in_weight)
    left, right, taps, spread, lines = lax.optimization_barrier((left, right, taps, spread, lines))
    got_a, got_b = exchange_rows(fields, wet_mask, left, right)
    groups, depth, width = taps.shape[1:]
    hid = in_weight.shape[2]
    size = Sizes(rows, cols, ch)
    cells = rows * cols
    vmem = pl.BlockSpec(memory_space=pltpu.VMEM)
    relaid = jax.ShapeDtypeStruct((groups, 4, rows * size.octets, ch), BF)
    ends = pltpu.VMEM((groups, 4, 2 * HALO * size.octets, ch), BF)
    own = jax.ShapeDtypeStruct((rows * size.pitch, ch), F32)
    padded = jax.ShapeDtypeStruct((size.lines, ch), F32)
    sums = jax.ShapeDtypeStruct((groups, rows * size.octets, width), F32)

    def call(kernel, ins, out_shape, scratch, flops):
        def spec(value):
            if value is not taps and value is not spread and value is not lines:
                return vmem
            block = 0 if kernel in (conv0_kernel, mlp0_kernel) else 1
            return pl.BlockSpec((1,) + value.shape[1:], lambda i: (block,) + (0,) * (value.ndim - 1))

        several = isinstance(out_shape, tuple)
        return pl.pallas_call(
            functools.partial(kernel, size),
            grid=(1,),
            in_specs=[spec(value) for value in ins],
            out_specs=(vmem,) * len(out_shape) if several else vmem,
            out_shape=out_shape,
            scratch_shapes=scratch,
            compiler_params=pltpu.CompilerParams(vmem_limit_bytes=VMEM_LIMIT),
            cost_estimate=pl.CostEstimate(flops=flops, bytes_accessed=6 * cells * ch, transcendentals=cells * hid),
            name=kernel.__name__,
        )(*ins)

    conv_flops = 2 * cells * ch * depth // OUTS * 2
    mlp_flops = 4 * cells * ch * hid
    params = (conv_bias, norm_gain, norm_bias, in_weight, in_bias, out_weight, out_bias, layer_scale, spread, lines)
    row_strips = jax.ShapeDtypeStruct((2 * HALO, size.wide0, ch), F32)
    col_strips = jax.ShapeDtypeStruct((2, HALO, rows, ch), F32)
    lines_in = TAPS + HALO - 1
    edges = jax.ShapeDtypeStruct((2 * lines_in * size.pitch, ch), F32)
    x0, moved = call(lay_kernel, (fields, mask, left, right), (own, relaid), [], conv_flops // 4)
    edge, acc, row_sums, col_sums = call(
        conv0_kernel,
        (x0, moved, got_a, got_b, taps, small),
        (edges, sums, row_strips, col_strips),
        [ends, pltpu.VMEM((REACH, cols + 24, ch), F32), pltpu.VMEM((2, lines_in, rows + 8, ch), F32)],
        conv_flops,
    )
    x1 = call(mlp0_kernel, (acc, x0, edge, row_sums, col_sums) + params, padded, [], mlp_flops)
    acc = call(conv1_kernel, (x1, taps), sums, [pltpu.VMEM(relaid.shape, BF), ends], conv_flops)
    whole = pltpu.VMEM((size.lines, ch), F32)
    return call(mlp1_kernel, (acc, x1, mask) + params, jax.ShapeDtypeStruct(fields.shape, BF), [whole], mlp_flops)


def solution(mesh):
    return jax.shard_map(
        shards,
        mesh=mesh,
        in_specs=(P("lat", "lon", None), P("lat", "lon")) + (P(),) * 9,
        out_specs=P("lat", "lon", None),
        check_vma=False,
    )
```

```python
import functools

import jax
import jax.numpy as jnp
from jax import lax
from jax.experimental import pallas as pl
from jax.experimental.pallas import tpu as pltpu
from jax.sharding import PartitionSpec as P

BF = jnp.bfloat16
F32 = jnp.float32
TAPS = 7
HALO = 3
REACH = 2 * HALO
OUTS = 8
BASE = 8
VMEM_LIMIT = 16 * 1024 * 1024
ERF_POLY = (0.7975078797359708, 0.03700565107996738, -0.0003515176683895368)


def partners(nlat, nlon, parity):
    route = []
    for lat in range(nlat):
        for lon in range(nlon):
            here = lat * nlon + lon
            if lat % 2 == parity:
                there = here + nlon if lat + 1 < nlat else lat * nlon + nlon - 1 - lon
            elif lat > 0:
                there = here - nlon
            else:
                continue
            route.append((here, there))
    return route


def edge(fields, wet_mask, r0, r1, c0, c1):
    return jnp.where(wet_mask[r0:r1, c0:c1][:, :, None] != 0, fields[r0:r1, c0:c1], jnp.zeros((), BF))


def exchange_columns(fields, wet_mask):
    nlon = lax.axis_size("lon")
    rows, cols = wet_mask.shape
    up = [(i, (i + 1) % nlon) for i in range(nlon)]
    down = [(j, i) for i, j in up]
    left = lax.ppermute(edge(fields, wet_mask, 0, rows, cols - REACH, cols), "lon", up)
    right = lax.ppermute(edge(fields, wet_mask, 0, rows, 0, REACH), "lon", down)
    return left, right


def exchange_rows(fields, wet_mask, left, right):
    nlat, nlon = lax.axis_size("lat"), lax.axis_size("lon")
    rows, cols = wet_mask.shape
    first = jnp.concatenate([left[:REACH], edge(fields, wet_mask, 0, REACH, 0, cols), right[:REACH]], axis=1)
    last = edge(fields, wet_mask, rows - REACH, rows, 0, cols)
    last = jnp.concatenate([left[rows - REACH :], last, right[rows - REACH :]], axis=1)
    even = lax.axis_index("lat") % 2 == 0
    got_a = lax.ppermute(jnp.where(even, last, first), ("lat", "lon"), partners(nlat, nlon, 0))
    got_b = lax.ppermute(jnp.where(even, first, last), ("lat", "lon"), partners(nlat, nlon, 1))
    return got_a, got_b


def regroup(parts, width):
    parts = list(parts)
    ch = parts[0].shape[-1]
    block = lax.broadcasted_iota(jnp.int32, parts[0].shape, parts[0].ndim - 1) // width
    step = 1
    while step < len(parts):
        low = (block & step) == 0
        for i in range(len(parts)):
            if not i & step:
                x, y = parts[i], parts[i + step]
                parts[i] = jnp.where(low, x, pltpu.roll(y, step * width, x.ndim - 1))
                parts[i + step] = jnp.where(low, pltpu.roll(x, ch - step * width, x.ndim - 1), y)
        step *= 2
    return parts


def tap_kernel(blocks, small_ref, inw_ref, w_ref, spread_ref, lines_ref, kv_ref):
    ch = small_ref.shape[1]
    lanes = w_ref.shape[3]
    width = lanes // OUTS
    groups = ch // width
    b, gr = pl.program_id(0), pl.program_id(1)

    @pl.when(gr == 0)
    def _():
        block = lax.broadcasted_iota(jnp.int32, (1, ch), 1) // width
        for n in range(3):
            vec = small_ref[pl.ds(blocks * (TAPS * TAPS + n) + b, 1), :]
            for g in range(groups):
                line = jnp.zeros((1, ch), F32)
                for j in range(groups):
                    line = jnp.where(block == j, pltpu.roll(vec, (j - g) * width % ch, 1), line)
                lines_ref[0, n * groups + g : n * groups + g + 1, :] = line
        down = [small_ref[pl.ds(b * TAPS * TAPS + s, TAPS, stride=TAPS), :] for s in range(TAPS - 1, -1, -1)]
        down.append(jnp.zeros((TAPS, ch), F32))
        halves = [regroup(down[i : i + groups], width) for i in range(0, OUTS, groups)]
        out_col = lax.broadcasted_iota(jnp.int32, (TAPS, lanes), 1) // width
        for g in range(groups):
            line = jnp.concatenate([half[g] for half in halves], axis=1)
            for p in range(2 * OUTS):
                turned = pltpu.roll(line, (p - TAPS + 1) * width % lanes, 1)
                seen = (out_col <= p) & (out_col >= p - TAPS + 1)
                kv_ref[g, p, 0:TAPS, :] = jnp.where(seen, turned, 0.0)

    lane = lax.broadcasted_iota(jnp.int32, (width, lanes), 1)
    own = (lane % width) == lax.broadcasted_iota(jnp.int32, (width, lanes), 0)
    for r in range(TAPS):
        for p in range(2 * OUTS):
            vec = kv_ref[gr, p, r : r + 1, :]
            at = (r * 2 * OUTS + p) * width
            w_ref[0, 0, at : at + width, :] = jnp.where(own, vec, 0.0).astype(BF)
    mine = inw_ref[b, pl.ds(pl.multiple_of(gr * width, width), width), :]
    for o in range(groups):
        for j in range(groups):
            spread_ref[0, o, j * width : (j + 1) * width, :] = mine if j == o else jnp.zeros_like(mine)


def tap_matrices(blocks, small, in_weight):
    ch = small.shape[1]
    hid = in_weight.shape[2]
    lanes = 2 * ch
    width = lanes // OUTS
    groups = ch // width
    depth = TAPS * 2 * OUTS * width
    return pl.pallas_call(
        functools.partial(tap_kernel, blocks),
        grid=(blocks, groups),
        in_specs=[pl.BlockSpec(memory_space=pltpu.VMEM)] * 2,
        out_specs=(
            pl.BlockSpec((1, 1, depth, lanes), lambda b, g: (b, g, 0, 0)),
            pl.BlockSpec((1, groups, ch, hid), lambda b, g: (b, 0, g, 0)),
            pl.BlockSpec((1, 3 * groups, ch), lambda b, g: (b, 0, 0)),
        ),
        out_shape=(
            jax.ShapeDtypeStruct((blocks, groups, depth, lanes), BF),
            jax.ShapeDtypeStruct((blocks, groups, groups * ch, hid), BF),
            jax.ShapeDtypeStruct((blocks, 3 * groups, ch), F32),
        ),
        scratch_shapes=[pltpu.VMEM((groups, 2 * OUTS, 8, lanes), F32)],
        compiler_params=pltpu.CompilerParams(vmem_limit_bytes=24 * 1024 * 1024),
        cost_estimate=pl.CostEstimate(
            flops=0, bytes_accessed=2 * blocks * groups * depth * lanes, transcendentals=0
        ),
        name="tap_matrices",
    )(small, in_weight)


class Sizes:
    def __init__(self, rows, cols, ch):
        self.rows, self.cols, self.ch = rows, cols, ch
        self.width = 2 * ch // OUTS
        self.groups = ch // self.width
        self.octets = cols // OUTS
        self.pitch = cols + 24
        self.lines = (rows + 2 * REACH) * self.pitch
        self.wide0 = cols + 16

    def line(self, row, above=REACH):
        return pl.multiple_of((row + above) * self.pitch, 8)


def place():
    lat = lax.axis_index("lat")
    return lat % 2 == 0, lat == lax.axis_size("lat") - 1, lat == 0


def relay(size, lines, start, relaid_ref, first=0):
    octets, groups, width, ch = size.octets, size.groups, size.width, size.ch
    step = next(d for d in (6, 4, 3, 2, 1) if lines % d == 0)
    shape = (groups * ch, groups * ch)
    old = lax.broadcasted_iota(jnp.int32, shape, 0)
    new = lax.broadcasted_iota(jnp.int32, shape, 1)
    order = jnp.where(new == old % ch // width * ch + old // ch * width + old % width, 1.0, 0.0).astype(BF)

    def one(q, carry):
        cells = []
        for a in range(4):
            for i in range(step):
                src_ref, at = start(q * step + i)
                at = at + BASE - HALO + 4 * a
                parts = [src_ref[pl.ds(at + j, octets, stride=OUTS), :].astype(BF) for j in range(groups)]
                cells.append(jnp.concatenate(parts, axis=1))
        moved = jnp.dot(jnp.concatenate(cells, axis=0), order, preferred_element_type=F32).astype(BF)
        n = step * octets
        for a in range(4):
            for gr in range(groups):
                relaid_ref[gr, a, pl.ds(pl.multiple_of(first * octets + q * n, 16), n), :] = moved[
                    a * n : (a + 1) * n, gr * ch : (gr + 1) * ch
                ]
        return carry

    lax.fori_loop(0, lines // step, one, 0)


def conv(size, gr, first, count, relaid_ref, ends_ref, w_ref, acc_ref):
    octets, rows = size.octets, size.rows
    parts = []
    for r in range(TAPS):
        for a in range(4):
            low, high = first + r - HALO, first + r - HALO + count
            rows_in = [relaid_ref[gr, a, max(low, 0) * octets : min(high, rows) * octets, :]]
            if low < 0:
                rows_in.insert(0, ends_ref[gr, a, (HALO + low) * octets : HALO * octets, :])
            if high > rows:
                rows_in.append(ends_ref[gr, a, HALO * octets : (HALO + high - rows) * octets, :])
            parts.append(jnp.concatenate(rows_in, axis=0))
    acc_ref[gr] = jnp.dot(jnp.concatenate(parts, axis=1), w_ref[0, gr], preferred_element_type=F32)


def column_strip(size, side, x0_ref, edge_ref, k_ref, side_ref, strip_ref):
    rows, pitch = size.rows, size.pitch
    start = BASE + (-HALO if side == 0 else size.cols) - HALO
    north = (TAPS + HALO - 1 + HALO) * pitch
    for c in range(TAPS + HALO - 1):
        side_ref[side, c, 0:HALO, :] = edge_ref[pl.ds(HALO * pitch + start + c, HALO, stride=pitch), :]
        side_ref[side, c, HALO : HALO + rows, :] = x0_ref[pl.ds(start + c, rows, stride=pitch), :]
        side_ref[side, c, HALO + rows : 2 * HALO + rows, :] = edge_ref[pl.ds(north + start + c, HALO, stride=pitch), :]
    sums = [jnp.zeros((rows, size.ch), F32) for _ in range(HALO)]
    for r in range(TAPS):
        for c in range(TAPS + HALO - 1):
            cells = side_ref[side, c, r : r + rows, :]
            for i in range(HALO):
                if 0 <= c - i < TAPS:
                    tap = TAPS * r + c - i
                    sums[i] = sums[i] + cells * k_ref[tap : tap + 1, :]
    for i in range(HALO):
        strip_ref[side, i] = sums[i]


def row_strip(size, side, c, piece, top, edge_ref, k_ref, strip_ref):
    pitch, lead = size.pitch, BASE - REACH
    lines_in = TAPS + HALO - 1
    first = side * lines_in * pitch
    sums = [jnp.zeros((piece, size.ch), F32) for _ in range(HALO)]
    for s in range(TAPS):
        at = first + lead + s + c
        lines = [edge_ref[at + i * pitch : at + i * pitch + piece, :] for i in range(lines_in)]
        for r in range(TAPS):
            tap = TAPS * r + s
            if side == 1:
                tap = jnp.where(top, TAPS * TAPS - 1 - tap, tap)
            weight = k_ref[pl.ds(tap, 1), :]
            for i in range(HALO):
                sums[i] = sums[i] + lines[i + r] * weight
    for i in range(HALO):
        strip_ref[side * HALO + i, c : c + piece, :] = sums[i]


def lay_kernel(size, x_ref, mask_ref, left_ref, right_ref, x0_ref, relaid_ref):
    rows, cols, ch, pitch = size.rows, size.cols, size.ch, size.pitch
    lead = BASE - REACH

    def fill(i, carry):
        at = size.line(i, 0)
        x0_ref[pl.ds(at, BASE), :] = jnp.zeros((BASE, ch), F32)
        x0_ref[pl.ds(at + lead, REACH), :] = left_ref[i].astype(F32)
        x0_ref[pl.ds(at + BASE, cols), :] = (x_ref[i] * mask_ref[i]).astype(F32)
        x0_ref[pl.ds(at + BASE + cols, 16), :] = jnp.zeros((16, ch), F32)
        x0_ref[pl.ds(at + BASE + cols, REACH), :] = right_ref[i].astype(F32)
        return carry

    lax.fori_loop(0, rows, fill, 0)
    relay(size, rows, lambda i: (x0_ref, size.line(i, 0)), relaid_ref)


def gelu_twice(h):
    z = h * h
    p = jnp.full_like(z, ERF_POLY[-1])
    for coef in ERF_POLY[-2::-1]:
        p = p * z + jnp.asarray(coef, z.dtype)
    return h + h * jnp.tanh(h * p)


def norm(b, params, val):
    cbias_ref, gain_ref, nbias_ref = params[:3]
    val = val + cbias_ref[b : b + 1, :]
    cen = val - jnp.mean(val, axis=-1, keepdims=True)
    var = jnp.mean(cen * cen, axis=-1, keepdims=True)
    return (cen * lax.rsqrt(var + 1e-6) * gain_ref[b : b + 1, :] + nbias_ref[b : b + 1, :]).astype(BF)


def project(b, params, normed, weight_ref, index):
    inb_ref, outw_ref, outb_ref, scale_ref = params[4:8]
    rows = normed.shape[0]
    tile = 48 if rows % 48 == 0 else 64
    branch = None
    half_hid = outw_ref.shape[1] // 2
    for c in range(0, 2 * half_hid, half_hid):
        hid = jnp.dot(normed, weight_ref[index + (slice(None), slice(c, c + half_hid))], preferred_element_type=F32)
        bias = inb_ref[b : b + 1, c : c + half_hid]
        act = [gelu_twice((hid[i : i + tile] + bias).astype(BF)) for i in range(0, rows, tile)]
        part = jnp.dot(jnp.concatenate(act, axis=0), outw_ref[b, c : c + half_hid, :], preferred_element_type=F32)
        branch = part if branch is None else branch + part
    scale = scale_ref[b : b + 1, :]
    return branch * (0.5 * scale) + outb_ref[b : b + 1, :] * scale


def mlp(b, params, parts):
    n = parts[0].shape[0]
    normed = jnp.concatenate([norm(b, params, part) for part in parts], axis=0)
    branch = project(b, params, normed, params[3], (b,))
    return [branch[i * n : (i + 1) * n] for i in range(len(parts))]


def block_sums(size, val):
    ch = size.ch
    row = lax.broadcasted_iota(jnp.int32, (2 * ch, ch), 0) % ch
    col = lax.broadcasted_iota(jnp.int32, (2 * ch, ch), 1)
    ones = jnp.where(row // size.width == col // size.width, 1.0, 0.0).astype(BF)
    high = val.astype(BF)
    low = (val - high.astype(F32)).astype(BF)
    return jnp.dot(jnp.concatenate([high, low], axis=1), ones, preferred_element_type=F32)


def norm_grouped(size, lines_ref, parts):
    groups = size.groups
    share = 1.0 / size.ch

    def line(n, gr):
        return lines_ref[0, n * groups + gr : n * groups + gr + 1, :]

    vals = [part + line(0, gr) for gr, part in enumerate(parts)]
    mean = block_sums(size, sum(vals[1:], vals[0])) * share
    cens = [val - mean for val in vals]
    squares = [cen * cen for cen in cens]
    inv = lax.rsqrt(block_sums(size, sum(squares[1:], squares[0])) * share + 1e-6)
    normed = [(cen * inv * line(1, gr) + line(2, gr)).astype(BF) for gr, cen in enumerate(cens)]
    return jnp.concatenate(normed, axis=1)


def rounded(val):
    return val.astype(BF).astype(F32)


def rounded(val):
    return val.astype(BF).astype(F32)


def mlp_pieces(size, b, params, first, count, acc_ref, src_ref, above, dst_ref):
    octets, groups, ch = size.octets, size.groups, size.ch
    spread_ref, lines_ref = params[8:]
    for half in range(2):
        parts = [acc_ref[gr, :, half * ch : (half + 1) * ch] for gr in range(groups)]
        normed = norm_grouped(size, lines_ref, parts)
        for j in range(groups):
            branch = project(b, params, normed, spread_ref, (0, j))
            for i in range(count):
                at = BASE + half * groups + j
                old = src_ref[pl.ds(size.line(first + i, above) + at, octets, stride=OUTS), :]
                new = rounded(old + branch[i * octets : (i + 1) * octets])
                dst_ref[pl.ds(size.line(first + i) + at, octets, stride=OUTS), :] = new
            yield


def block(size, b, params, relaid_ref, ends_ref, w_ref, accs, src_ref, above, dst_ref, beside=()):
    count = size.rows // len(accs)
    groups = size.groups
    for c in range(len(accs) + 1):
        if c:
            pieces = mlp_pieces(size, b, params, (c - 1) * count, count, accs[c - 1], src_ref, above, dst_ref)
        else:
            pieces = iter(())
        for gr in range(groups):
            if c < len(accs):
                conv(size, gr, c * count, count, relaid_ref, ends_ref, w_ref, accs[c])
            for work in beside[gr::groups] if c == 0 else ():
                work()
            next(pieces, None)
            next(pieces, None)
        for _ in pieces:
            pass


def block0_kernel(size, x0_ref, relaid_ref, a_ref, b_ref, w_ref, k_ref, *refs):
    params, x1_ref, ends_ref, flip_ref, side_ref, edge_ref, row_ref, col_ref = refs[:10], *refs[10:17]
    accs = refs[17:]
    rows, cols, ch, pitch, wide0 = size.rows, size.cols, size.ch, size.pitch, size.wide0
    ext, lead = cols + 2 * REACH, BASE - REACH
    even, top, bottom = place()
    near = BASE - HALO
    lines_in = TAPS + HALO - 1

    flip_ref[...] = jnp.zeros(flip_ref.shape, F32)
    at = lax.broadcasted_iota(jnp.int32, (wide0, wide0), 0)
    to = lax.broadcasted_iota(jnp.int32, (wide0, wide0), 1)
    mirror = jnp.where(to == jnp.where(top, ext - 1 - at, at), 1.0, 0.0).astype(BF)
    edge_ref[0 : REACH * pitch, :] = jnp.zeros((REACH * pitch, ch), F32)
    north = (lines_in + HALO) * pitch
    edge_ref[north : north + REACH * pitch, :] = jnp.zeros((REACH * pitch, ch), F32)
    turned = []
    for i in range(0, REACH, 2):
        for h in range(2):
            south = (i + h) * pitch + lead
            edge_ref[south : south + ext, :] = jnp.where(even, b_ref[i + h].astype(F32), a_ref[i + h].astype(F32))
            src = jnp.where(top, REACH - 1 - i - h, i + h)
            flip_ref[i + h, 0:ext, :] = jnp.where(even, a_ref[src].astype(F32), b_ref[src].astype(F32))
        both = jnp.concatenate([flip_ref[i + h, 0:wide0, :].astype(BF) for h in range(2)], axis=1)
        turned.append(jnp.dot(mirror, both, preferred_element_type=F32))
    for i in range(REACH):
        put = north + i * pitch + lead
        edge_ref[put : put + wide0, :] = turned[i // 2][:, i % 2 * ch : (i % 2 + 1) * ch]
    for i in range(HALO):
        for slot, row in ((REACH + i, i), (lines_in + i, rows - HALO + i)):
            edge_ref[slot * pitch : (slot + 1) * pitch, :] = x0_ref[row * pitch : (row + 1) * pitch, :]

    def start(i):
        return edge_ref, pl.multiple_of(jnp.where(i < HALO, HALO + i, lines_in + i) * pitch, 8)

    relay(size, 2 * HALO, start, ends_ref)
    piece = wide0 // 3
    beside = [
        functools.partial(column_strip, size, side, x0_ref, edge_ref, k_ref, side_ref, col_ref) for side in range(2)
    ]
    for side in range(2):
        for c in range(0, wide0, piece):
            beside.append(functools.partial(row_strip, size, side, c, piece, top, edge_ref, k_ref, row_ref))

    def clear(i, carry):
        at = size.line(i)
        x1_ref[pl.ds(at, BASE), :] = jnp.zeros((BASE, ch), F32)
        x1_ref[pl.ds(at + BASE + cols, 16), :] = jnp.zeros((16, ch), F32)
        return carry

    lax.fori_loop(0, rows, clear, 0)
    block(size, 0, params, relaid_ref, ends_ref, w_ref, accs, x0_ref, 0, x1_ref, beside)
    for side, start in enumerate((-HALO, cols)):
        for i, branch in enumerate(mlp(0, params, [col_ref[side, i] for i in range(HALO)])):
            old = x0_ref[pl.ds(BASE + start + i, rows, stride=pitch), :]
            x1_ref[pl.ds(REACH * pitch + BASE + start + i, rows, stride=pitch), :] = rounded(old + branch)
    for side in range(2):
        branches = mlp(0, params, [row_ref[side * HALO + i] for i in range(HALO)])
        for i, branch in enumerate(branches):
            row = i - HALO if side == 0 else rows + i
            at = (row + REACH) * pitch + near
            here = (side * (TAPS + HALO - 1) + HALO + i) * pitch + near
            new = rounded(edge_ref[here : here + wide0, :] + branch)
            if side == 0:
                new = jnp.where(bottom, 0.0, new)
            x1_ref[at : at + wide0, :] = new


def block1_kernel(size, x1_ref, w_ref, mask_ref, *refs):
    params, out_ref, relaid_ref, ends_ref, x2_ref = refs[:10], *refs[10:14]
    accs = refs[14:]
    relay(size, size.rows, lambda i: (x1_ref, size.line(i)), relaid_ref)

    def start(i):
        return x1_ref, size.line(jnp.where(i < HALO, i - HALO, size.rows - HALO + i))

    relay(size, 2 * HALO, start, ends_ref)
    block(size, 1, params, relaid_ref, ends_ref, w_ref, accs, x1_ref, REACH, x2_ref)

    def finish(i, carry):
        out_ref[i] = x2_ref[pl.ds(size.line(i) + BASE, size.cols), :].astype(BF) * mask_ref[i]
        return carry

    lax.fori_loop(0, size.rows, finish, 0)


def shards(
    fields,
    wet_mask,
    conv_kernel,
    conv_bias,
    norm_gain,
    norm_bias,
    in_weight,
    in_bias,
    out_weight,
    out_bias,
    layer_scale,
):
    rows, cols, ch = fields.shape
    left, right = exchange_columns(fields, wet_mask)
    mask = jnp.broadcast_to(wet_mask.astype(BF)[:, :, None], fields.shape)
    small = jnp.concatenate([conv_kernel.reshape(-1, ch), conv_bias, norm_gain, norm_bias])
    taps, spread, lines = tap_matrices(conv_kernel.shape[0], small, in_weight)
    left, right, taps, spread, lines = lax.optimization_barrier((left, right, taps, spread, lines))
    got_a, got_b = exchange_rows(fields, wet_mask, left, right)
    groups, depth, width = taps.shape[1:]
    hid = in_weight.shape[2]
    size = Sizes(rows, cols, ch)
    cells = rows * cols
    vmem = pl.BlockSpec(memory_space=pltpu.VMEM)
    relaid = jax.ShapeDtypeStruct((groups, 4, rows * size.octets, ch), BF)
    ends = pltpu.VMEM((groups, 4, 2 * HALO * size.octets, ch), BF)
    own = jax.ShapeDtypeStruct((rows * size.pitch, ch), F32)
    padded = jax.ShapeDtypeStruct((size.lines, ch), F32)
    chunks = 2 if rows % 2 == 0 else 1
    accs = [pltpu.VMEM((groups, rows // chunks * size.octets, width), F32)] * chunks

    def call(kernel, ins, out_shape, scratch, flops):
        def spec(value):
            if value is not taps and value is not spread and value is not lines:
                return vmem
            which = 0 if kernel is block0_kernel else 1
            return pl.BlockSpec((1,) + value.shape[1:], lambda i: (which,) + (0,) * (value.ndim - 1))

        several = isinstance(out_shape, tuple)
        return pl.pallas_call(
            functools.partial(kernel, size),
            grid=(1,),
            in_specs=[spec(value) for value in ins],
            out_specs=(vmem,) * len(out_shape) if several else vmem,
            out_shape=out_shape,
            scratch_shapes=scratch,
            compiler_params=pltpu.CompilerParams(vmem_limit_bytes=VMEM_LIMIT),
            cost_estimate=pl.CostEstimate(flops=flops, bytes_accessed=6 * cells * ch, transcendentals=cells * hid),
            name=kernel.__name__,
        )(*ins)

    conv_flops = 2 * cells * ch * depth // OUTS * 2
    mlp_flops = 4 * cells * ch * hid
    params = (conv_bias, norm_gain, norm_bias, in_weight, in_bias, out_weight, out_bias, layer_scale, spread, lines)
    lines_in = TAPS + HALO - 1
    x0, moved = call(lay_kernel, (fields, mask, left, right), (own, relaid), [], conv_flops // 4)
    x1 = call(
        block0_kernel,
        (x0, moved, got_a, got_b, taps, small) + params,
        padded,
        [
            ends,
            pltpu.VMEM((REACH, cols + 24, ch), F32),
            pltpu.VMEM((2, lines_in, rows + 8, ch), F32),
            pltpu.VMEM((2 * lines_in * size.pitch, ch), F32),
            pltpu.VMEM((2 * HALO, size.wide0, ch), F32),
            pltpu.VMEM((2, HALO, rows, ch), F32),
        ]
        + accs,
        conv_flops + mlp_flops,
    )
    whole = pltpu.VMEM((size.lines, ch), F32)
    return call(
        block1_kernel,
        (x1, taps, mask) + params,
        jax.ShapeDtypeStruct(fields.shape, BF),
        [pltpu.VMEM(relaid.shape, BF), ends, whole] + accs,
        conv_flops + mlp_flops,
    )


def solution(mesh):
    return jax.shard_map(
        shards,
        mesh=mesh,
        in_specs=(P("lat", "lon", None), P("lat", "lon")) + (P(),) * 9,
        out_specs=P("lat", "lon", None),
        check_vma=False,
    )
```

```python
import functools

import jax
import jax.numpy as jnp
from jax import lax
from jax.experimental import pallas as pl
from jax.experimental.pallas import tpu as pltpu
from jax.sharding import PartitionSpec as P

BF = jnp.bfloat16
F32 = jnp.float32
TAPS = 7
HALO = 3
REACH = 2 * HALO
OUTS = 8
BASE = 8
VMEM_LIMIT = 16 * 1024 * 1024
ERF_POLY = (0.7975078797359708, 0.03700565107996738, -0.0003515176683895368)


def partners(nlat, nlon, parity):
    route = []
    for lat in range(nlat):
        for lon in range(nlon):
            here = lat * nlon + lon
            if lat % 2 == parity:
                there = here + nlon if lat + 1 < nlat else lat * nlon + nlon - 1 - lon
            elif lat > 0:
                there = here - nlon
            else:
                continue
            route.append((here, there))
    return route


def edge(fields, wet_mask, r0, r1, c0, c1):
    return fields[r0:r1, c0:c1] * wet_mask[r0:r1, c0:c1].astype(BF)[:, :, None]


def exchange_columns(fields, wet_mask):
    nlon = lax.axis_size("lon")
    rows, cols = wet_mask.shape
    up = [(i, (i + 1) % nlon) for i in range(nlon)]
    down = [(j, i) for i, j in up]
    left = lax.ppermute(edge(fields, wet_mask, 0, rows, cols - REACH, cols), "lon", up)
    right = lax.ppermute(edge(fields, wet_mask, 0, rows, 0, REACH), "lon", down)
    return left, right


def exchange_rows(fields, wet_mask, left, right):
    nlat, nlon = lax.axis_size("lat"), lax.axis_size("lon")
    rows, cols = wet_mask.shape
    first = jnp.concatenate([left[:REACH], edge(fields, wet_mask, 0, REACH, 0, cols), right[:REACH]], axis=1)
    last = edge(fields, wet_mask, rows - REACH, rows, 0, cols)
    last = jnp.concatenate([left[rows - REACH :], last, right[rows - REACH :]], axis=1)
    even = lax.axis_index("lat") % 2 == 0
    got_a = lax.ppermute(jnp.where(even, last, first), ("lat", "lon"), partners(nlat, nlon, 0))
    got_b = lax.ppermute(jnp.where(even, first, last), ("lat", "lon"), partners(nlat, nlon, 1))
    return got_a, got_b


def regroup(parts, width):
    parts = list(parts)
    ch = parts[0].shape[-1]
    block = lax.broadcasted_iota(jnp.int32, parts[0].shape, parts[0].ndim - 1) // width
    step = 1
    while step < len(parts):
        low = (block & step) == 0
        for i in range(len(parts)):
            if not i & step:
                x, y = parts[i], parts[i + step]
                parts[i] = jnp.where(low, x, pltpu.roll(y, step * width, x.ndim - 1))
                parts[i + step] = jnp.where(low, pltpu.roll(x, ch - step * width, x.ndim - 1), y)
        step *= 2
    return parts


def tap_kernel(blocks, small_ref, inw_ref, w_ref, spread_ref, lines_ref, kv_ref):
    ch = small_ref.shape[1]
    lanes = w_ref.shape[3]
    width = lanes // OUTS
    groups = ch // width
    b, gr = pl.program_id(0), pl.program_id(1)

    @pl.when(gr == 0)
    def _():
        block = lax.broadcasted_iota(jnp.int32, (1, ch), 1) // width
        for n in range(3):
            vec = small_ref[pl.ds(blocks * (TAPS * TAPS + n) + b, 1), :]
            for g in range(groups):
                line = jnp.zeros((1, ch), F32)
                for j in range(groups):
                    line = jnp.where(block == j, pltpu.roll(vec, (j - g) * width % ch, 1), line)
                lines_ref[0, n * groups + g : n * groups + g + 1, :] = line
        down = [small_ref[pl.ds(b * TAPS * TAPS + s, TAPS, stride=TAPS), :] for s in range(TAPS - 1, -1, -1)]
        down.append(jnp.zeros((TAPS, ch), F32))
        halves = [regroup(down[i : i + groups], width) for i in range(0, OUTS, groups)]
        out_col = lax.broadcasted_iota(jnp.int32, (TAPS, lanes), 1) // width
        for g in range(groups):
            line = jnp.concatenate([half[g] for half in halves], axis=1)
            for p in range(2 * OUTS):
                turned = pltpu.roll(line, (p - TAPS + 1) * width % lanes, 1)
                seen = (out_col <= p) & (out_col >= p - TAPS + 1)
                kv_ref[g, p, 0:TAPS, :] = jnp.where(seen, turned, 0.0)

    lane = lax.broadcasted_iota(jnp.int32, (width, lanes), 1)
    own = (lane % width) == lax.broadcasted_iota(jnp.int32, (width, lanes), 0)
    for r in range(TAPS):
        for p in range(2 * OUTS):
            vec = kv_ref[gr, p, r : r + 1, :]
            at = (r * 2 * OUTS + p) * width
            w_ref[0, 0, at : at + width, :] = jnp.where(own, vec, 0.0).astype(BF)
    mine = inw_ref[b, pl.ds(pl.multiple_of(gr * width, width), width), :]
    for o in range(groups):
        for j in range(groups):
            spread_ref[0, o, j * width : (j + 1) * width, :] = mine if j == o else jnp.zeros_like(mine)


def tap_matrices(blocks, small, in_weight):
    ch = small.shape[1]
    hid = in_weight.shape[2]
    lanes = 2 * ch
    width = lanes // OUTS
    groups = ch // width
    depth = TAPS * 2 * OUTS * width
    return pl.pallas_call(
        functools.partial(tap_kernel, blocks),
        grid=(blocks, groups),
        in_specs=[pl.BlockSpec(memory_space=pltpu.VMEM)] * 2,
        out_specs=(
            pl.BlockSpec((1, 1, depth, lanes), lambda b, g: (b, g, 0, 0)),
            pl.BlockSpec((1, groups, ch, hid), lambda b, g: (b, 0, g, 0)),
            pl.BlockSpec((1, 3 * groups, ch), lambda b, g: (b, 0, 0)),
        ),
        out_shape=(
            jax.ShapeDtypeStruct((blocks, groups, depth, lanes), BF),
            jax.ShapeDtypeStruct((blocks, groups, groups * ch, hid), BF),
            jax.ShapeDtypeStruct((blocks, 3 * groups, ch), F32),
        ),
        scratch_shapes=[pltpu.VMEM((groups, 2 * OUTS, 8, lanes), F32)],
        compiler_params=pltpu.CompilerParams(vmem_limit_bytes=24 * 1024 * 1024),
        cost_estimate=pl.CostEstimate(
            flops=0, bytes_accessed=2 * blocks * groups * depth * lanes, transcendentals=0
        ),
        name="tap_matrices",
    )(small, in_weight)


class Sizes:
    def __init__(self, rows, cols, ch):
        self.rows, self.cols, self.ch = rows, cols, ch
        self.width = 2 * ch // OUTS
        self.groups = ch // self.width
        self.octets = cols // OUTS
        self.pitch = cols + 24
        self.lines = (rows + 2 * REACH) * self.pitch
        self.wide0 = cols + 16

    def line(self, row, above=REACH):
        return pl.multiple_of((row + above) * self.pitch, 8)


def place():
    lat = lax.axis_index("lat")
    return lat % 2 == 0, lat == lax.axis_size("lat") - 1, lat == 0


def relay(size, lines, start, relaid_ref, first=0):
    octets, groups, width, ch = size.octets, size.groups, size.width, size.ch
    step = next(d for d in (12, 6, 4, 3, 2, 1) if lines % d == 0)
    shape = (groups * ch, groups * ch)
    old = lax.broadcasted_iota(jnp.int32, shape, 0)
    new = lax.broadcasted_iota(jnp.int32, shape, 1)
    order = jnp.where(new == old % ch // width * ch + old // ch * width + old % width, 1.0, 0.0).astype(BF)

    def one(q, carry):
        cells = []
        for a in range(4):
            for i in range(step):
                src_ref, at = start(q * step + i)
                at = at + BASE - HALO + 4 * a
                parts = [src_ref[pl.ds(at + j, octets, stride=OUTS), :].astype(BF) for j in range(groups)]
                cells.append(jnp.concatenate(parts, axis=1))
        moved = jnp.dot(jnp.concatenate(cells, axis=0), order, preferred_element_type=F32).astype(BF)
        n = step * octets
        for a in range(4):
            for gr in range(groups):
                relaid_ref[gr, a, pl.ds(pl.multiple_of(first * octets + q * n, 16), n), :] = moved[
                    a * n : (a + 1) * n, gr * ch : (gr + 1) * ch
                ]
        return carry

    lax.fori_loop(0, lines // step, one, 0)


def conv(size, gr, first, count, relaid_ref, ends_ref, w_ref, acc_ref):
    octets, rows = size.octets, size.rows
    parts = []
    for r in range(TAPS):
        for a in range(4):
            low, high = first + r - HALO, first + r - HALO + count
            rows_in = [relaid_ref[gr, a, max(low, 0) * octets : min(high, rows) * octets, :]]
            if low < 0:
                rows_in.insert(0, ends_ref[gr, a, (HALO + low) * octets : HALO * octets, :])
            if high > rows:
                rows_in.append(ends_ref[gr, a, HALO * octets : (HALO + high - rows) * octets, :])
            parts.append(jnp.concatenate(rows_in, axis=0))
    acc_ref[gr] = jnp.dot(jnp.concatenate(parts, axis=1), w_ref[0, gr], preferred_element_type=F32)


def column_strip(size, side, x0_ref, edge_ref, k_ref, side_ref, strip_ref):
    rows, pitch = size.rows, size.pitch
    start = BASE + (-HALO if side == 0 else size.cols) - HALO
    north = (TAPS + HALO - 1 + HALO) * pitch
    for c in range(TAPS + HALO - 1):
        side_ref[side, c, 0:HALO, :] = edge_ref[pl.ds(HALO * pitch + start + c, HALO, stride=pitch), :]
        side_ref[side, c, HALO : HALO + rows, :] = x0_ref[pl.ds(start + c, rows, stride=pitch), :]
        side_ref[side, c, HALO + rows : 2 * HALO + rows, :] = edge_ref[pl.ds(north + start + c, HALO, stride=pitch), :]
    sums = [jnp.zeros((rows, size.ch), F32) for _ in range(HALO)]
    for r in range(TAPS):
        for c in range(TAPS + HALO - 1):
            cells = side_ref[side, c, r : r + rows, :]
            for i in range(HALO):
                if 0 <= c - i < TAPS:
                    tap = TAPS * r + c - i
                    sums[i] = sums[i] + cells * k_ref[tap : tap + 1, :]
    for i in range(HALO):
        strip_ref[side, i] = sums[i]


def row_strip(size, side, c, piece, top, edge_ref, k_ref, strip_ref):
    pitch, lead = size.pitch, BASE - REACH
    lines_in = TAPS + HALO - 1
    first = side * lines_in * pitch
    sums = [jnp.zeros((piece, size.ch), F32) for _ in range(HALO)]
    for s in range(TAPS):
        at = first + lead + s + c
        lines = [edge_ref[at + i * pitch : at + i * pitch + piece, :] for i in range(lines_in)]
        for r in range(TAPS):
            tap = TAPS * r + s
            if side == 1:
                tap = jnp.where(top, TAPS * TAPS - 1 - tap, tap)
            weight = k_ref[pl.ds(tap, 1), :]
            for i in range(HALO):
                sums[i] = sums[i] + lines[i + r] * weight
    for i in range(HALO):
        strip_ref[side * HALO + i, c : c + piece, :] = sums[i]


def lay_kernel(size, x_ref, mask_ref, left_ref, right_ref, x0_ref, relaid_ref):
    rows, cols, ch, pitch = size.rows, size.cols, size.ch, size.pitch
    lead = BASE - REACH

    def fill(i, carry):
        at = size.line(i, 0)
        x0_ref[pl.ds(at, BASE), :] = jnp.zeros((BASE, ch), F32)
        x0_ref[pl.ds(at + lead, REACH), :] = left_ref[i].astype(F32)
        x0_ref[pl.ds(at + BASE, cols), :] = (x_ref[i] * mask_ref[i]).astype(F32)
        x0_ref[pl.ds(at + BASE + cols, 16), :] = jnp.zeros((16, ch), F32)
        x0_ref[pl.ds(at + BASE + cols, REACH), :] = right_ref[i].astype(F32)
        return carry

    lax.fori_loop(0, rows, fill, 0)
    relay(size, rows, lambda i: (x0_ref, size.line(i, 0)), relaid_ref)


def gelu_twice(h):
    z = h * h
    p = jnp.full_like(z, ERF_POLY[-1])
    for coef in ERF_POLY[-2::-1]:
        p = p * z + jnp.asarray(coef, z.dtype)
    return h + h * jnp.tanh(h * p)


def norm(b, params, val):
    cbias_ref, gain_ref, nbias_ref = params[:3]
    val = val + cbias_ref[b : b + 1, :]
    cen = val - jnp.mean(val, axis=-1, keepdims=True)
    var = jnp.mean(cen * cen, axis=-1, keepdims=True)
    return (cen * lax.rsqrt(var + 1e-6) * gain_ref[b : b + 1, :] + nbias_ref[b : b + 1, :]).astype(BF)


def project(b, params, normed, weight_ref, index):
    inb_ref, outw_ref, outb_ref, scale_ref = params[4:8]
    rows = normed.shape[0]
    tile = 48 if rows % 48 == 0 else 64
    branch = None
    half_hid = outw_ref.shape[1] // 2
    for c in range(0, 2 * half_hid, half_hid):
        hid = jnp.dot(normed, weight_ref[index + (slice(None), slice(c, c + half_hid))], preferred_element_type=F32)
        bias = inb_ref[b : b + 1, c : c + half_hid]
        act = [gelu_twice((hid[i : i + tile] + bias).astype(BF)) for i in range(0, rows, tile)]
        part = jnp.dot(jnp.concatenate(act, axis=0), outw_ref[b, c : c + half_hid, :], preferred_element_type=F32)
        branch = part if branch is None else branch + part
    scale = scale_ref[b : b + 1, :]
    return branch * (0.5 * scale) + outb_ref[b : b + 1, :] * scale


def mlp(b, params, parts):
    normed = jnp.concatenate([norm(b, params, part) for part in parts], axis=0)
    branch = project(b, params, normed, params[3], (b,))
    ends = [0]
    for part in parts:
        ends.append(ends[-1] + part.shape[0])
    return [branch[low:high] for low, high in zip(ends, ends[1:])]


def block_sums(size, val):
    ch = size.ch
    row = lax.broadcasted_iota(jnp.int32, (2 * ch, ch), 0) % ch
    col = lax.broadcasted_iota(jnp.int32, (2 * ch, ch), 1)
    ones = jnp.where(row // size.width == col // size.width, 1.0, 0.0).astype(BF)
    high = val.astype(BF)
    low = (val - high.astype(F32)).astype(BF)
    return jnp.dot(jnp.concatenate([high, low], axis=1), ones, preferred_element_type=F32)


def norm_grouped(size, lines_ref, parts):
    groups = size.groups
    share = 1.0 / size.ch

    def line(n, gr):
        return lines_ref[0, n * groups + gr : n * groups + gr + 1, :]

    vals = [part + line(0, gr) for gr, part in enumerate(parts)]
    mean = block_sums(size, sum(vals[1:], vals[0])) * share
    cens = [val - mean for val in vals]
    squares = [cen * cen for cen in cens]
    inv = lax.rsqrt(block_sums(size, sum(squares[1:], squares[0])) * share + 1e-6)
    normed = [(cen * inv * line(1, gr) + line(2, gr)).astype(BF) for gr, cen in enumerate(cens)]
    return jnp.concatenate(normed, axis=1)


def rounded(val):
    return val.astype(BF).astype(F32)


def rounded(val):
    return val.astype(BF).astype(F32)


def mlp_pieces(size, b, params, first, count, acc_ref, src_ref, above, dst_ref):
    octets, groups, ch = size.octets, size.groups, size.ch
    spread_ref, lines_ref = params[8:]
    for half in range(2):
        parts = [acc_ref[gr, :, half * ch : (half + 1) * ch] for gr in range(groups)]
        normed = norm_grouped(size, lines_ref, parts)
        for j in range(groups):
            branch = project(b, params, normed, spread_ref, (0, j))
            for i in range(count):
                at = BASE + half * groups + j
                old = src_ref[pl.ds(size.line(first + i, above) + at, octets, stride=OUTS), :]
                new = rounded(old + branch[i * octets : (i + 1) * octets])
                dst_ref[pl.ds(size.line(first + i) + at, octets, stride=OUTS), :] = new
            yield


def block(size, b, params, relaid_ref, ends_ref, w_ref, accs, src_ref, above, dst_ref, beside=(), after=None):
    count = size.rows // len(accs)
    groups = size.groups
    for c in range(len(accs) + 1):
        if c:
            pieces = mlp_pieces(size, b, params, (c - 1) * count, count, accs[c - 1], src_ref, above, dst_ref)
        else:
            pieces = iter(())
        for gr in range(groups):
            if c < len(accs):
                conv(size, gr, c * count, count, relaid_ref, ends_ref, w_ref, accs[c])
            for work in beside[gr::groups] if c == 0 else ():
                work()
            next(pieces, None)
            next(pieces, None)
        for _ in pieces:
            pass
        if after is not None and c == len(accs) - 1:
            after()


def block0_kernel(size, x0_ref, relaid_ref, a_ref, b_ref, w_ref, k_ref, *refs):
    params, x1_ref, ends_ref, flip_ref, side_ref, edge_ref, row_ref, col_ref = refs[:10], *refs[10:17]
    accs = refs[17:]
    rows, cols, ch, pitch, wide0 = size.rows, size.cols, size.ch, size.pitch, size.wide0
    ext, lead = cols + 2 * REACH, BASE - REACH
    even, top, bottom = place()
    near = BASE - HALO
    lines_in = TAPS + HALO - 1

    flip_ref[...] = jnp.zeros(flip_ref.shape, F32)
    at = lax.broadcasted_iota(jnp.int32, (wide0, wide0), 0)
    to = lax.broadcasted_iota(jnp.int32, (wide0, wide0), 1)
    mirror = jnp.where(to == jnp.where(top, ext - 1 - at, at), 1.0, 0.0).astype(BF)
    edge_ref[0 : REACH * pitch, :] = jnp.zeros((REACH * pitch, ch), F32)
    north = (lines_in + HALO) * pitch
    edge_ref[north : north + REACH * pitch, :] = jnp.zeros((REACH * pitch, ch), F32)
    turned = []
    for i in range(0, REACH, 2):
        for h in range(2):
            south = (i + h) * pitch + lead
            edge_ref[south : south + ext, :] = jnp.where(even, b_ref[i + h].astype(F32), a_ref[i + h].astype(F32))
            src = jnp.where(top, REACH - 1 - i - h, i + h)
            flip_ref[i + h, 0:ext, :] = jnp.where(even, a_ref[src].astype(F32), b_ref[src].astype(F32))
        both = jnp.concatenate([flip_ref[i + h, 0:wide0, :].astype(BF) for h in range(2)], axis=1)
        turned.append(jnp.dot(mirror, both, preferred_element_type=F32))
    for i in range(REACH):
        put = north + i * pitch + lead
        edge_ref[put : put + wide0, :] = turned[i // 2][:, i % 2 * ch : (i % 2 + 1) * ch]
    for i in range(HALO):
        for slot, row in ((REACH + i, i), (lines_in + i, rows - HALO + i)):
            edge_ref[slot * pitch : (slot + 1) * pitch, :] = x0_ref[row * pitch : (row + 1) * pitch, :]

    def start(i):
        return edge_ref, pl.multiple_of(jnp.where(i < HALO, HALO + i, lines_in + i) * pitch, 8)

    relay(size, 2 * HALO, start, ends_ref)
    piece = wide0 // 3
    beside = [
        functools.partial(column_strip, size, side, x0_ref, edge_ref, k_ref, side_ref, col_ref) for side in range(2)
    ]
    for side in range(2):
        for c in range(0, wide0, piece):
            beside.append(functools.partial(row_strip, size, side, c, piece, top, edge_ref, k_ref, row_ref))

    def clear(i, carry):
        at = size.line(i)
        x1_ref[pl.ds(at, BASE), :] = jnp.zeros((BASE, ch), F32)
        x1_ref[pl.ds(at + BASE + cols, 16), :] = jnp.zeros((16, ch), F32)
        return carry

    lax.fori_loop(0, rows, clear, 0)

    def strips():
        parts = [row_ref[i] for i in range(2 * HALO)] + [col_ref[side, i] for side in range(2) for i in range(HALO)]
        branches = mlp(0, params, parts)
        for n, branch in enumerate(branches[: 2 * HALO]):
            side, i = n // HALO, n % HALO
            row = i - HALO if side == 0 else rows + i
            at = (row + REACH) * pitch + near
            here = (side * lines_in + HALO + i) * pitch + near
            new = rounded(edge_ref[here : here + wide0, :] + branch)
            if side == 0:
                new = jnp.where(bottom, 0.0, new)
            x1_ref[at : at + wide0, :] = new
        for n, branch in enumerate(branches[2 * HALO :]):
            col = n - HALO if n < HALO else cols + n - HALO
            old = x0_ref[pl.ds(BASE + col, rows, stride=pitch), :]
            x1_ref[pl.ds(REACH * pitch + BASE + col, rows, stride=pitch), :] = rounded(old + branch)

    block(size, 0, params, relaid_ref, ends_ref, w_ref, accs, x0_ref, 0, x1_ref, beside, strips)


def block1_kernel(size, x1_ref, w_ref, mask_ref, *refs):
    params, out_ref, relaid_ref, ends_ref, x2_ref = refs[:10], *refs[10:14]
    accs = refs[14:]
    relay(size, size.rows, lambda i: (x1_ref, size.line(i)), relaid_ref)

    def start(i):
        return x1_ref, size.line(jnp.where(i < HALO, i - HALO, size.rows - HALO + i))

    relay(size, 2 * HALO, start, ends_ref)
    block(size, 1, params, relaid_ref, ends_ref, w_ref, accs, x1_ref, REACH, x2_ref)

    def finish(i, carry):
        out_ref[i] = x2_ref[pl.ds(size.line(i) + BASE, size.cols), :].astype(BF) * mask_ref[i]
        return carry

    lax.fori_loop(0, size.rows, finish, 0)


def shards(
    fields,
    wet_mask,
    conv_kernel,
    conv_bias,
    norm_gain,
    norm_bias,
    in_weight,
    in_bias,
    out_weight,
    out_bias,
    layer_scale,
):
    rows, cols, ch = fields.shape
    left, right = exchange_columns(fields, wet_mask)
    mask = jnp.broadcast_to(wet_mask.astype(BF)[:, :, None], fields.shape)
    small = jnp.concatenate([conv_kernel.reshape(-1, ch), conv_bias, norm_gain, norm_bias])
    taps, spread, lines = tap_matrices(conv_kernel.shape[0], small, in_weight)
    left, right, taps, spread, lines = lax.optimization_barrier((left, right, taps, spread, lines))
    got_a, got_b = exchange_rows(fields, wet_mask, left, right)
    groups, depth, width = taps.shape[1:]
    hid = in_weight.shape[2]
    size = Sizes(rows, cols, ch)
    cells = rows * cols
    vmem = pl.BlockSpec(memory_space=pltpu.VMEM)
    relaid = jax.ShapeDtypeStruct((groups, 4, rows * size.octets, ch), BF)
    ends = pltpu.VMEM((groups, 4, 2 * HALO * size.octets, ch), BF)
    own = jax.ShapeDtypeStruct((rows * size.pitch, ch), F32)
    padded = jax.ShapeDtypeStruct((size.lines, ch), F32)
    chunks = next(d for d in (3, 2, 1) if rows % d == 0)
    accs = [pltpu.VMEM((groups, rows // chunks * size.octets, width), F32)] * chunks

    def call(kernel, ins, out_shape, scratch, flops):
        def spec(value):
            if value is not taps and value is not spread and value is not lines:
                return vmem
            which = 0 if kernel is block0_kernel else 1
            return pl.BlockSpec((1,) + value.shape[1:], lambda i: (which,) + (0,) * (value.ndim - 1))

        several = isinstance(out_shape, tuple)
        return pl.pallas_call(
            functools.partial(kernel, size),
            grid=(1,),
            in_specs=[spec(value) for value in ins],
            out_specs=(vmem,) * len(out_shape) if several else vmem,
            out_shape=out_shape,
            scratch_shapes=scratch,
            compiler_params=pltpu.CompilerParams(vmem_limit_bytes=VMEM_LIMIT),
            cost_estimate=pl.CostEstimate(flops=flops, bytes_accessed=6 * cells * ch, transcendentals=cells * hid),
            name=kernel.__name__,
        )(*ins)

    conv_flops = 2 * cells * ch * depth // OUTS * 2
    mlp_flops = 4 * cells * ch * hid
    params = (conv_bias, norm_gain, norm_bias, in_weight, in_bias, out_weight, out_bias, layer_scale, spread, lines)
    lines_in = TAPS + HALO - 1
    x0, moved = call(lay_kernel, (fields, mask, left, right), (own, relaid), [], conv_flops // 4)
    x1 = call(
        block0_kernel,
        (x0, moved, got_a, got_b, taps, small) + params,
        padded,
        [
            ends,
            pltpu.VMEM((REACH, cols + 24, ch), F32),
            pltpu.VMEM((2, lines_in, rows + 8, ch), F32),
            pltpu.VMEM((2 * lines_in * size.pitch, ch), F32),
            pltpu.VMEM((2 * HALO, size.wide0, ch), F32),
            pltpu.VMEM((2, HALO, rows, ch), F32),
        ]
        + accs,
        conv_flops + mlp_flops,
    )
    whole = pltpu.VMEM((size.lines, ch), F32)
    return call(
        block1_kernel,
        (x1, taps, mask) + params,
        jax.ShapeDtypeStruct(fields.shape, BF),
        [pltpu.VMEM(relaid.shape, BF), ends, whole] + accs,
        conv_flops + mlp_flops,
    )


def solution(mesh):
    return jax.shard_map(
        shards,
        mesh=mesh,
        in_specs=(P("lat", "lon", None), P("lat", "lon")) + (P(),) * 9,
        out_specs=P("lat", "lon", None),
        check_vma=False,
    )
```

```python
import functools

import jax
import jax.numpy as jnp
from jax import lax
from jax.experimental import pallas as pl
from jax.experimental.pallas import tpu as pltpu
from jax.sharding import PartitionSpec as P

BF = jnp.bfloat16
F32 = jnp.float32
TAPS = 7
HALO = 3
REACH = 2 * HALO
OUTS = 8
BASE = 8
VMEM_LIMIT = 16 * 1024 * 1024
ERF_POLY = (0.7975078797359708, 0.03700565107996738, -0.0003515176683895368)


def partners(nlat, nlon, parity):
    route = []
    for lat in range(nlat):
        for lon in range(nlon):
            here = lat * nlon + lon
            if lat % 2 == parity:
                there = here + nlon if lat + 1 < nlat else lat * nlon + nlon - 1 - lon
            elif lat > 0:
                there = here - nlon
            else:
                continue
            route.append((here, there))
    return route


def edge(fields, wet_mask, r0, r1, c0, c1):
    return fields[r0:r1, c0:c1] * wet_mask[r0:r1, c0:c1].astype(BF)[:, :, None]


def exchange_columns(fields, wet_mask):
    nlon = lax.axis_size("lon")
    rows, cols = wet_mask.shape
    up = [(i, (i + 1) % nlon) for i in range(nlon)]
    down = [(j, i) for i, j in up]
    left = lax.ppermute(edge(fields, wet_mask, 0, rows, cols - REACH, cols), "lon", up)
    right = lax.ppermute(edge(fields, wet_mask, 0, rows, 0, REACH), "lon", down)
    return left, right


def exchange_rows(fields, wet_mask, left, right):
    nlat, nlon = lax.axis_size("lat"), lax.axis_size("lon")
    rows, cols = wet_mask.shape
    first = jnp.concatenate([left[:REACH], edge(fields, wet_mask, 0, REACH, 0, cols), right[:REACH]], axis=1)
    last = edge(fields, wet_mask, rows - REACH, rows, 0, cols)
    last = jnp.concatenate([left[rows - REACH :], last, right[rows - REACH :]], axis=1)
    even = lax.axis_index("lat") % 2 == 0
    got_a = lax.ppermute(jnp.where(even, last, first), ("lat", "lon"), partners(nlat, nlon, 0))
    got_b = lax.ppermute(jnp.where(even, first, last), ("lat", "lon"), partners(nlat, nlon, 1))
    return got_a, got_b


def regroup(parts, width):
    parts = list(parts)
    ch = parts[0].shape[-1]
    block = lax.broadcasted_iota(jnp.int32, parts[0].shape, parts[0].ndim - 1) // width
    step = 1
    while step < len(parts):
        low = (block & step) == 0
        for i in range(len(parts)):
            if not i & step:
                x, y = parts[i], parts[i + step]
                parts[i] = jnp.where(low, x, pltpu.roll(y, step * width, x.ndim - 1))
                parts[i + step] = jnp.where(low, pltpu.roll(x, ch - step * width, x.ndim - 1), y)
        step *= 2
    return parts


def tap_kernel(blocks, small_ref, inw_ref, w_ref, spread_ref, lines_ref, kv_ref):
    ch = small_ref.shape[1]
    lanes = w_ref.shape[3]
    width = lanes // OUTS
    groups = ch // width
    b, gr = pl.program_id(0), pl.program_id(1)

    @pl.when(gr == 0)
    def _():
        block = lax.broadcasted_iota(jnp.int32, (1, ch), 1) // width
        for n in range(3):
            vec = small_ref[pl.ds(blocks * (TAPS * TAPS + n) + b, 1), :]
            for g in range(groups):
                line = jnp.zeros((1, ch), F32)
                for j in range(groups):
                    line = jnp.where(block == j, pltpu.roll(vec, (j - g) * width % ch, 1), line)
                lines_ref[0, n * groups + g : n * groups + g + 1, :] = line
        down = [small_ref[pl.ds(b * TAPS * TAPS + s, TAPS, stride=TAPS), :] for s in range(TAPS - 1, -1, -1)]
        down.append(jnp.zeros((TAPS, ch), F32))
        halves = [regroup(down[i : i + groups], width) for i in range(0, OUTS, groups)]
        out_col = lax.broadcasted_iota(jnp.int32, (TAPS, lanes), 1) // width
        for g in range(groups):
            line = jnp.concatenate([half[g] for half in halves], axis=1)
            for p in range(2 * OUTS):
                turned = pltpu.roll(line, (p - TAPS + 1) * width % lanes, 1)
                seen = (out_col <= p) & (out_col >= p - TAPS + 1)
                kv_ref[g, p, 0:TAPS, :] = jnp.where(seen, turned, 0.0)

    lane = lax.broadcasted_iota(jnp.int32, (width, lanes), 1)
    own = (lane % width) == lax.broadcasted_iota(jnp.int32, (width, lanes), 0)
    for r in range(TAPS):
        for p in range(2 * OUTS):
            vec = kv_ref[gr, p, r : r + 1, :]
            at = (r * 2 * OUTS + p) * width
            w_ref[0, 0, at : at + width, :] = jnp.where(own, vec, 0.0).astype(BF)
    mine = inw_ref[b, pl.ds(pl.multiple_of(gr * width, width), width), :]
    for o in range(groups):
        for j in range(groups):
            spread_ref[0, o, j * width : (j + 1) * width, :] = mine if j == o else jnp.zeros_like(mine)


def tap_matrices(blocks, small, in_weight):
    ch = small.shape[1]
    hid = in_weight.shape[2]
    lanes = 2 * ch
    width = lanes // OUTS
    groups = ch // width
    depth = TAPS * 2 * OUTS * width
    return pl.pallas_call(
        functools.partial(tap_kernel, blocks),
        grid=(blocks, groups),
        in_specs=[pl.BlockSpec(memory_space=pltpu.VMEM)] * 2,
        out_specs=(
            pl.BlockSpec((1, 1, depth, lanes), lambda b, g: (b, g, 0, 0)),
            pl.BlockSpec((1, groups, ch, hid), lambda b, g: (b, 0, g, 0)),
            pl.BlockSpec((1, 3 * groups, ch), lambda b, g: (b, 0, 0)),
        ),
        out_shape=(
            jax.ShapeDtypeStruct((blocks, groups, depth, lanes), BF),
            jax.ShapeDtypeStruct((blocks, groups, groups * ch, hid), BF),
            jax.ShapeDtypeStruct((blocks, 3 * groups, ch), F32),
        ),
        scratch_shapes=[pltpu.VMEM((groups, 2 * OUTS, 8, lanes), F32)],
        compiler_params=pltpu.CompilerParams(vmem_limit_bytes=24 * 1024 * 1024),
        cost_estimate=pl.CostEstimate(
            flops=0, bytes_accessed=2 * blocks * groups * depth * lanes, transcendentals=0
        ),
        name="tap_matrices",
    )(small, in_weight)


class Sizes:
    def __init__(self, rows, cols, ch):
        self.rows, self.cols, self.ch = rows, cols, ch
        self.width = 2 * ch // OUTS
        self.groups = ch // self.width
        self.octets = cols // OUTS
        self.pitch = cols + 24
        self.lines = (rows + 2 * REACH) * self.pitch
        self.wide0 = cols + 16

    def line(self, row, above=REACH):
        return pl.multiple_of((row + above) * self.pitch, 8)


def place():
    lat = lax.axis_index("lat")
    return lat % 2 == 0, lat == lax.axis_size("lat") - 1, lat == 0


def relay(size, lines, start, relaid_ref, first=0):
    octets, groups, width, ch = size.octets, size.groups, size.width, size.ch
    step = next(d for d in (12, 6, 4, 3, 2, 1) if lines % d == 0)
    shape = (groups * ch, groups * ch)
    old = lax.broadcasted_iota(jnp.int32, shape, 0)
    new = lax.broadcasted_iota(jnp.int32, shape, 1)
    order = jnp.where(new == old % ch // width * ch + old // ch * width + old % width, 1.0, 0.0).astype(BF)

    def one(q, carry):
        cells = []
        for a in range(4):
            for i in range(step):
                src_ref, at = start(q * step + i)
                at = at + BASE - HALO + 4 * a
                parts = [src_ref[pl.ds(at + j, octets, stride=OUTS), :].astype(BF) for j in range(groups)]
                cells.append(jnp.concatenate(parts, axis=1))
        moved = jnp.dot(jnp.concatenate(cells, axis=0), order, preferred_element_type=F32).astype(BF)
        n = step * octets
        for a in range(4):
            for gr in range(groups):
                relaid_ref[gr, a, pl.ds(pl.multiple_of(first * octets + q * n, 16), n), :] = moved[
                    a * n : (a + 1) * n, gr * ch : (gr + 1) * ch
                ]
        return carry

    lax.fori_loop(0, lines // step, one, 0)


def conv(size, gr, first, count, relaid_ref, ends_ref, w_ref, acc_ref):
    octets, rows = size.octets, size.rows
    parts = []
    for r in range(TAPS):
        for a in range(4):
            low, high = first + r - HALO, first + r - HALO + count
            rows_in = [relaid_ref[gr, a, max(low, 0) * octets : min(high, rows) * octets, :]]
            if low < 0:
                rows_in.insert(0, ends_ref[gr, a, (HALO + low) * octets : HALO * octets, :])
            if high > rows:
                rows_in.append(ends_ref[gr, a, HALO * octets : (HALO + high - rows) * octets, :])
            parts.append(jnp.concatenate(rows_in, axis=0))
    acc_ref[gr] = jnp.dot(jnp.concatenate(parts, axis=1), w_ref[0, gr], preferred_element_type=F32)


def column_strip(size, side, x0_ref, edge_ref, k_ref, side_ref, strip_ref):
    rows, pitch = size.rows, size.pitch
    start = BASE + (-HALO if side == 0 else size.cols) - HALO
    north = (TAPS + HALO - 1 + HALO) * pitch
    for c in range(TAPS + HALO - 1):
        side_ref[side, c, 0:HALO, :] = edge_ref[pl.ds(HALO * pitch + start + c, HALO, stride=pitch), :]
        side_ref[side, c, HALO : HALO + rows, :] = x0_ref[pl.ds(start + c, rows, stride=pitch), :]
        side_ref[side, c, HALO + rows : 2 * HALO + rows, :] = edge_ref[pl.ds(north + start + c, HALO, stride=pitch), :]
    sums = [jnp.zeros((rows, size.ch), F32) for _ in range(HALO)]
    for r in range(TAPS):
        for c in range(TAPS + HALO - 1):
            cells = side_ref[side, c, r : r + rows, :]
            for i in range(HALO):
                if 0 <= c - i < TAPS:
                    tap = TAPS * r + c - i
                    sums[i] = sums[i] + cells * k_ref[tap : tap + 1, :]
    for i in range(HALO):
        strip_ref[side, i] = sums[i]


def row_strip(size, side, c, piece, top, edge_ref, k_ref, strip_ref):
    pitch, lead = size.pitch, BASE - REACH
    lines_in = TAPS + HALO - 1
    first = side * lines_in * pitch
    sums = [jnp.zeros((piece, size.ch), F32) for _ in range(HALO)]
    for s in range(TAPS):
        at = first + lead + s + c
        lines = [edge_ref[at + i * pitch : at + i * pitch + piece, :] for i in range(lines_in)]
        for r in range(TAPS):
            tap = TAPS * r + s
            if side == 1:
                tap = jnp.where(top, TAPS * TAPS - 1 - tap, tap)
            weight = k_ref[pl.ds(tap, 1), :]
            for i in range(HALO):
                sums[i] = sums[i] + lines[i + r] * weight
    for i in range(HALO):
        strip_ref[side * HALO + i, c : c + piece, :] = sums[i]


def lay_kernel(size, x_ref, mask_ref, left_ref, right_ref, x0_ref, relaid_ref):
    rows, cols, ch, pitch = size.rows, size.cols, size.ch, size.pitch
    lead = BASE - REACH

    def fill(i, carry):
        at = size.line(i, 0)
        x0_ref[pl.ds(at, BASE), :] = jnp.zeros((BASE, ch), F32)
        x0_ref[pl.ds(at + lead, REACH), :] = left_ref[i].astype(F32)
        x0_ref[pl.ds(at + BASE, cols), :] = (x_ref[i] * mask_ref[i]).astype(F32)
        x0_ref[pl.ds(at + BASE + cols, 16), :] = jnp.zeros((16, ch), F32)
        x0_ref[pl.ds(at + BASE + cols, REACH), :] = right_ref[i].astype(F32)
        return carry

    lax.fori_loop(0, rows, fill, 0)
    relay(size, rows, lambda i: (x0_ref, size.line(i, 0)), relaid_ref)


def gelu_twice(h):
    z = h * h
    p = jnp.full_like(z, ERF_POLY[-1])
    for coef in ERF_POLY[-2::-1]:
        p = p * z + jnp.asarray(coef, z.dtype)
    return h + h * jnp.tanh(h * p)


def norm(b, params, val):
    cbias_ref, gain_ref, nbias_ref = params[:3]
    val = val + cbias_ref[b : b + 1, :]
    cen = val - jnp.mean(val, axis=-1, keepdims=True)
    var = jnp.mean(cen * cen, axis=-1, keepdims=True)
    return (cen * lax.rsqrt(var + 1e-6) * gain_ref[b : b + 1, :] + nbias_ref[b : b + 1, :]).astype(BF)


def project(b, params, normed, weight_ref, index):
    inb_ref, outw_ref, outb_ref, scale_ref = params[4:8]
    rows = normed.shape[0]
    tile = 48 if rows % 48 == 0 else 64
    branch = None
    half_hid = outw_ref.shape[1] // 2
    for c in range(0, 2 * half_hid, half_hid):
        hid = jnp.dot(normed, weight_ref[index + (slice(None), slice(c, c + half_hid))], preferred_element_type=F32)
        bias = inb_ref[b : b + 1, c : c + half_hid]
        act = [gelu_twice((hid[i : i + tile] + bias).astype(BF)) for i in range(0, rows, tile)]
        part = jnp.dot(jnp.concatenate(act, axis=0), outw_ref[b, c : c + half_hid, :], preferred_element_type=F32)
        branch = part if branch is None else branch + part
    scale = scale_ref[b : b + 1, :]
    return branch * (0.5 * scale) + outb_ref[b : b + 1, :] * scale


def mlp(b, params, parts):
    normed = jnp.concatenate([norm(b, params, part) for part in parts], axis=0)
    branch = project(b, params, normed, params[3], (b,))
    ends = [0]
    for part in parts:
        ends.append(ends[-1] + part.shape[0])
    return [branch[low:high] for low, high in zip(ends, ends[1:])]


def block_sums(size, val):
    ch = size.ch
    row = lax.broadcasted_iota(jnp.int32, (2 * ch, ch), 0) % ch
    col = lax.broadcasted_iota(jnp.int32, (2 * ch, ch), 1)
    ones = jnp.where(row // size.width == col // size.width, 1.0, 0.0).astype(BF)
    high = val.astype(BF)
    low = (val - high.astype(F32)).astype(BF)
    return jnp.dot(jnp.concatenate([high, low], axis=1), ones, preferred_element_type=F32)


def norm_grouped(size, lines_ref, parts):
    groups = size.groups
    share = 1.0 / size.ch

    def line(n, gr):
        return lines_ref[0, n * groups + gr : n * groups + gr + 1, :]

    vals = [part + line(0, gr) for gr, part in enumerate(parts)]
    mean = block_sums(size, sum(vals[1:], vals[0])) * share
    cens = [val - mean for val in vals]
    squares = [cen * cen for cen in cens]
    inv = lax.rsqrt(block_sums(size, sum(squares[1:], squares[0])) * share + 1e-6)
    normed = [(cen * inv * line(1, gr) + line(2, gr)).astype(BF) for gr, cen in enumerate(cens)]
    return jnp.concatenate(normed, axis=1)


def rounded(val):
    return val.astype(BF).astype(F32)


def rounded(val):
    return val.astype(BF).astype(F32)


def mlp_pieces(size, b, params, first, count, acc_ref, src_ref, above, dst_ref):
    octets, groups, ch = size.octets, size.groups, size.ch
    spread_ref, lines_ref = params[8:]
    for half in range(2):
        parts = [acc_ref[gr, :, half * ch : (half + 1) * ch] for gr in range(groups)]
        normed = norm_grouped(size, lines_ref, parts)
        for j in range(groups):
            branch = project(b, params, normed, spread_ref, (0, j))
            for i in range(count):
                at = BASE + half * groups + j
                old = src_ref[pl.ds(size.line(first + i, above) + at, octets, stride=OUTS), :]
                new = rounded(old + branch[i * octets : (i + 1) * octets])
                dst_ref[pl.ds(size.line(first + i) + at, octets, stride=OUTS), :] = new
            yield


def block(size, b, params, relaid_ref, ends_ref, w_ref, accs, src_ref, above, dst_ref, beside=(), after=None):
    count = size.rows // len(accs)
    groups = size.groups
    for c in range(len(accs) + 1):
        if c:
            pieces = mlp_pieces(size, b, params, (c - 1) * count, count, accs[c - 1], src_ref, above, dst_ref)
        else:
            pieces = iter(())
        for gr in range(groups):
            if c < len(accs):
                conv(size, gr, c * count, count, relaid_ref, ends_ref, w_ref, accs[c])
            for work in beside[gr::groups] if c == 0 else ():
                work()
            next(pieces, None)
            next(pieces, None)
        for _ in pieces:
            pass
        if after is not None and c == len(accs) - 1:
            after()


def block0_kernel(size, x0_ref, relaid_ref, a_ref, b_ref, w_ref, k_ref, *refs):
    params, x1_ref, ends_ref, flip_ref, side_ref, edge_ref, row_ref, col_ref = refs[:10], *refs[10:17]
    accs = refs[17:]
    rows, cols, ch, pitch, wide0 = size.rows, size.cols, size.ch, size.pitch, size.wide0
    ext, lead = cols + 2 * REACH, BASE - REACH
    even, top, bottom = place()
    near = BASE - HALO
    lines_in = TAPS + HALO - 1

    flip_ref[...] = jnp.zeros(flip_ref.shape, F32)
    at = lax.broadcasted_iota(jnp.int32, (wide0, wide0), 0)
    to = lax.broadcasted_iota(jnp.int32, (wide0, wide0), 1)
    mirror = jnp.where(to == jnp.where(top, ext - 1 - at, at), 1.0, 0.0).astype(BF)
    edge_ref[0 : REACH * pitch, :] = jnp.zeros((REACH * pitch, ch), F32)
    north = (lines_in + HALO) * pitch
    edge_ref[north : north + REACH * pitch, :] = jnp.zeros((REACH * pitch, ch), F32)
    turned = []
    for i in range(0, REACH, 2):
        for h in range(2):
            south = (i + h) * pitch + lead
            edge_ref[south : south + ext, :] = jnp.where(even, b_ref[i + h].astype(F32), a_ref[i + h].astype(F32))
            src = jnp.where(top, REACH - 1 - i - h, i + h)
            flip_ref[i + h, 0:ext, :] = jnp.where(even, a_ref[src].astype(F32), b_ref[src].astype(F32))
        both = jnp.concatenate([flip_ref[i + h, 0:wide0, :].astype(BF) for h in range(2)], axis=1)
        turned.append(jnp.dot(mirror, both, preferred_element_type=F32))
    for i in range(REACH):
        put = north + i * pitch + lead
        edge_ref[put : put + wide0, :] = turned[i // 2][:, i % 2 * ch : (i % 2 + 1) * ch]
    for i in range(HALO):
        for slot, row in ((REACH + i, i), (lines_in + i, rows - HALO + i)):
            edge_ref[slot * pitch : (slot + 1) * pitch, :] = x0_ref[row * pitch : (row + 1) * pitch, :]

    def start(i):
        return edge_ref, pl.multiple_of(jnp.where(i < HALO, HALO + i, lines_in + i) * pitch, 8)

    relay(size, 2 * HALO, start, ends_ref)
    piece = wide0 // 3
    beside = [
        functools.partial(column_strip, size, side, x0_ref, edge_ref, k_ref, side_ref, col_ref) for side in range(2)
    ]
    for side in range(2):
        for c in range(0, wide0, piece):
            beside.append(functools.partial(row_strip, size, side, c, piece, top, edge_ref, k_ref, row_ref))

    def clear(i, carry):
        at = size.line(i)
        x1_ref[pl.ds(at, BASE), :] = jnp.zeros((BASE, ch), F32)
        x1_ref[pl.ds(at + BASE + cols, 16), :] = jnp.zeros((16, ch), F32)
        return carry

    lax.fori_loop(0, rows, clear, 0)

    def strips():
        parts = [row_ref[i] for i in range(2 * HALO)] + [col_ref[side, i] for side in range(2) for i in range(HALO)]
        branches = mlp(0, params, parts)
        for n, branch in enumerate(branches[: 2 * HALO]):
            side, i = n // HALO, n % HALO
            row = i - HALO if side == 0 else rows + i
            at = (row + REACH) * pitch + near
            here = (side * lines_in + HALO + i) * pitch + near
            new = rounded(edge_ref[here : here + wide0, :] + branch)
            if side == 0:
                new = jnp.where(bottom, 0.0, new)
            x1_ref[at : at + wide0, :] = new
        for n, branch in enumerate(branches[2 * HALO :]):
            col = n - HALO if n < HALO else cols + n - HALO
            old = x0_ref[pl.ds(BASE + col, rows, stride=pitch), :]
            x1_ref[pl.ds(REACH * pitch + BASE + col, rows, stride=pitch), :] = rounded(old + branch)

    block(size, 0, params, relaid_ref, ends_ref, w_ref, accs, x0_ref, 0, x1_ref, beside, strips)


def block1_kernel(size, x1_ref, w_ref, mask_ref, *refs):
    params, out_ref, relaid_ref, ends_ref, x2_ref = refs[:10], *refs[10:14]
    accs = refs[14:]
    relay(size, size.rows, lambda i: (x1_ref, size.line(i)), relaid_ref)

    def start(i):
        return x1_ref, size.line(jnp.where(i < HALO, i - HALO, size.rows - HALO + i))

    relay(size, 2 * HALO, start, ends_ref)
    block(size, 1, params, relaid_ref, ends_ref, w_ref, accs, x1_ref, REACH, x2_ref)

    def finish(i, carry):
        out_ref[i] = x2_ref[pl.ds(size.line(i) + BASE, size.cols), :].astype(BF) * mask_ref[i]
        return carry

    lax.fori_loop(0, size.rows, finish, 0)


def shards(
    fields,
    wet_mask,
    conv_kernel,
    conv_bias,
    norm_gain,
    norm_bias,
    in_weight,
    in_bias,
    out_weight,
    out_bias,
    layer_scale,
):
    rows, cols, ch = fields.shape
    left, right = exchange_columns(fields, wet_mask)
    mask = jnp.broadcast_to(wet_mask.astype(BF)[:, :, None], fields.shape)
    small = jnp.concatenate([conv_kernel.reshape(-1, ch), conv_bias, norm_gain, norm_bias])
    taps, spread, lines = tap_matrices(conv_kernel.shape[0], small, in_weight)
    left, right, taps, spread, lines = lax.optimization_barrier((left, right, taps, spread, lines))
    got_a, got_b = exchange_rows(fields, wet_mask, left, right)
    groups, depth, width = taps.shape[1:]
    hid = in_weight.shape[2]
    size = Sizes(rows, cols, ch)
    cells = rows * cols
    vmem = pl.BlockSpec(memory_space=pltpu.VMEM)
    relaid = jax.ShapeDtypeStruct((groups, 4, rows * size.octets, ch), BF)
    ends = pltpu.VMEM((groups, 4, 2 * HALO * size.octets, ch), BF)
    own = jax.ShapeDtypeStruct((rows * size.pitch, ch), F32)
    padded = jax.ShapeDtypeStruct((size.lines, ch), F32)
    chunks = next(d for d in (2, 1) if rows % d == 0)
    accs = [pltpu.VMEM((groups, rows // chunks * size.octets, width), F32)] * chunks

    def call(kernel, ins, out_shape, scratch, flops):
        def spec(value):
            if value is not taps and value is not spread and value is not lines:
                return vmem
            which = 0 if kernel is block0_kernel else 1
            return pl.BlockSpec((1,) + value.shape[1:], lambda i: (which,) + (0,) * (value.ndim - 1))

        several = isinstance(out_shape, tuple)
        return pl.pallas_call(
            functools.partial(kernel, size),
            grid=(1,),
            in_specs=[spec(value) for value in ins],
            out_specs=(vmem,) * len(out_shape) if several else vmem,
            out_shape=out_shape,
            scratch_shapes=scratch,
            compiler_params=pltpu.CompilerParams(vmem_limit_bytes=VMEM_LIMIT),
            cost_estimate=pl.CostEstimate(flops=flops, bytes_accessed=6 * cells * ch, transcendentals=cells * hid),
            name=kernel.__name__,
        )(*ins)

    conv_flops = 2 * cells * ch * depth // OUTS * 2
    mlp_flops = 4 * cells * ch * hid
    params = (conv_bias, norm_gain, norm_bias, in_weight, in_bias, out_weight, out_bias, layer_scale, spread, lines)
    lines_in = TAPS + HALO - 1
    x0, moved = call(lay_kernel, (fields, mask, left, right), (own, relaid), [], conv_flops // 4)
    x1 = call(
        block0_kernel,
        (x0, moved, got_a, got_b, taps, small) + params,
        padded,
        [
            ends,
            pltpu.VMEM((REACH, cols + 24, ch), F32),
            pltpu.VMEM((2, lines_in, rows + 8, ch), F32),
            pltpu.VMEM((2 * lines_in * size.pitch, ch), F32),
            pltpu.VMEM((2 * HALO, size.wide0, ch), F32),
            pltpu.VMEM((2, HALO, rows, ch), F32),
        ]
        + accs,
        conv_flops + mlp_flops,
    )
    whole = pltpu.VMEM((size.lines, ch), F32)
    return call(
        block1_kernel,
        (x1, taps, mask) + params,
        jax.ShapeDtypeStruct(fields.shape, BF),
        [pltpu.VMEM(relaid.shape, BF), ends, whole] + accs,
        conv_flops + mlp_flops,
    )


def solution(mesh):
    return jax.shard_map(
        shards,
        mesh=mesh,
        in_specs=(P("lat", "lon", None), P("lat", "lon")) + (P(),) * 9,
        out_specs=P("lat", "lon", None),
        check_vma=False,
    )
```
